128 devices in a mesh: bin: 8 (over z_hi, y), row: 4 (over x), col: 4 (over z_lo, core).
Axes of the slice: x: 4, y: 4, z: 4 (z_hi: 2, z_lo: 2; z = z_hi * 2 + z_lo), core: 2. Of those that a mesh axis runs over, the one named last changes fastest.
Arguments:
- snapshots: bfloat16 [4096, 64, 64], P('row', 'bin', 'col'), may hold values from -6 to 6
- focus_in: bfloat16 [64, 4096, 128], P('bin', 'row'), may hold values from -0.09375 to 0.09375
- focus_out: bfloat16 [64, 4096, 128], P('bin', 'row'), may hold values from -0.5 to 0.5
- start_basis: float32 [4096, 128], replicated, may hold values from -6 to 6
Outputs:
- covariance: float32 [4096, 4096], P('col', 'row')
- basis_out: float32 [4096, 128], P(('row', 'col'))
The draws below stay inside these ranges and needn't reach their ends.
All inputs are finite; a program needn't handle non-finite values.
Results may differ from the reference program's by a relative error of at most 0.0045.
Values may be sent and summed in bfloat16 or wider, within the bound.
A program may use at most 128 MiB of HBM per device.

```python
import math
import jax
import jax.numpy as jnp
from jax import lax

M = 4096
R = 128
K = 128
S = 64
ITERS = 2
NBINS = 64


def block_levels(own_key, dims, pieces, low, largest):
    def one(dim, shards_of):
        draws = jax.random.uniform(jax.random.fold_in(jax.random.fold_in(own_key, 6), dim), (shards_of,), jnp.float32, low / len(pieces), largest / len(pieces))
        return jnp.repeat(jnp.exp(draws), dims[dim] // shards_of).reshape((-1,) + (1,) * (len(dims) - dim - 1))

    gain = one(*pieces[0])
    for cut in pieces[1:]:
        gain = gain * one(*cut)
    return gain


def noise(rng, extent, deviation, reach, split=(), dtype=jnp.bfloat16):
    level = block_levels(rng, extent, split, -0.22, 0.18) if split else 1.0
    entries = jax.random.normal(rng, extent, jnp.float32) * deviation * level
    return jnp.minimum(jnp.maximum(entries, -reach), reach).astype(dtype)


def setup_inputs(seed: int = 0) -> dict:
    seeds = jax.random.split(jax.random.key(seed), 5)
    snapshots = noise(seeds[0], (M, NBINS, S), 1.0, 6.0, ((0, 4), (1, 8), (2, 4)))
    focus_in = noise(seeds[1], (NBINS, M, R), M ** -0.5, 0.09375, ((0, 8), (1, 4)))
    focus_out = noise(seeds[2], (NBINS, M, R), R ** -0.5, 0.5, ((0, 8), (1, 4)))
    start_basis = noise(seeds[3], (M, K), 1.0, 6.0, (), jnp.float32)
    return dict(snapshots=snapshots, focus_in=focus_in, focus_out=focus_out, start_basis=start_basis)


def reference(snapshots, focus_in, focus_out, start_basis):
    projected = jnp.einsum('mbs,bmr->brs', snapshots.astype(jnp.float32), focus_in.astype(jnp.float32), precision=lax.Precision.HIGHEST).astype(jnp.bfloat16)
    lifted = jnp.einsum('bmr,brs->mbs', focus_out.astype(jnp.float32), projected.astype(jnp.float32), precision=lax.Precision.HIGHEST)
    focused = (snapshots.astype(jnp.float32) + lifted).astype(jnp.bfloat16)
    flattened = focused.reshape(M, NBINS * S).astype(jnp.float32)
    covariance = jnp.dot(flattened.astype(jnp.float32), flattened.T.astype(jnp.float32), precision=lax.Precision.HIGHEST, preferred_element_type=jnp.float32) * (1.0 / (NBINS * S))
    basis_now = start_basis
    for sweep_index in range(ITERS):
        image = jnp.dot(covariance.astype(jnp.float32), basis_now.astype(jnp.float32), precision=lax.Precision.HIGHEST, preferred_element_type=jnp.float32)
        gram_matrix = jnp.dot(image.T.astype(jnp.float32), image.astype(jnp.float32), precision=lax.Precision.HIGHEST, preferred_element_type=jnp.float32)
        lower_factor = jnp.linalg.cholesky(gram_matrix)
        basis_now = jax.scipy.linalg.solve_triangular(lower_factor, image.T, lower=True).T
    return (covariance, basis_now * math.sqrt(M))
```

```python
import functools
import math

import jax
import jax.numpy as jnp
from jax import lax
from jax.experimental import pallas as pl
from jax.experimental.pallas import tpu as pltpu
from jax.sharding import PartitionSpec as P

MESH = pl.DeviceIdType.MESH
HI = lax.Precision.HIGHEST
F32 = jnp.float32
BF16 = jnp.bfloat16


def mod4(v):
    return lax.rem(v + 4, 4)


def dot(a, b, ca, cb, precision=None):
    return lax.dot_general(a, b, (((ca,), (cb,)), ((), ())), precision=precision, preferred_element_type=F32)


def invert_factor(work):
    rows = lax.broadcasted_iota(jnp.int32, (128, 128), 0)
    lanes = lax.broadcasted_iota(jnp.int32, (128, 128), 1)
    lane1 = lax.broadcasted_iota(jnp.int32, (1, 128), 1)

    def step(j, carry):
        row = work[pl.ds(j, 1), :]
        now = work[...]
        col = jnp.sum(jnp.where(lanes == j, now, 0.0), axis=1, keepdims=True)
        pivot = jnp.sum(jnp.where(lane1 == j, row, 0.0), axis=1, keepdims=True)
        mult = jnp.where(rows > j, col / pivot, 0.0)
        row = jnp.where(lane1 == j, 1.0, row)
        work[...] = jnp.where((lanes == j) & (rows > j), 0.0, now) - mult * row
        return carry

    lax.fori_loop(0, 128, step, 0)


def apply_factor(work, block):
    rows = lax.broadcasted_iota(jnp.int32, (128, 128), 0)
    lanes = lax.broadcasted_iota(jnp.int32, (128, 128), 1)
    now = work[...]
    pivots = jnp.sum(jnp.where(rows == lanes, now, 0.0), axis=0, keepdims=True)
    inverse = jnp.where(rows > lanes, now, jnp.where(rows == lanes, 1.0, 0.0))
    return dot(block, inverse, 1, 1, HI) * lax.rsqrt(pivots)


def kernel(
    snap_hbm, fi_hbm, fo_hbm, x0_hbm, cov_ref, basis_ref,
    snap, fi, fo, x0, proj, full, slab, acc, sibc, piece, img, part, sibp, scat, zall,
    gpart, gsib, gown, gscat, gram, gpart2, gscat2, gram2, in_sem,
    p_s, p_r, g_s, g_r, a_s, a_r, x_s, x_r, c_s, c_r, v_s, v_r, i_s, i_r, q_s, q_r, r_s, r_r, z_s, z_r,
    gs_s, gs_r, ga_s, ga_r, gb_s, gb_r, l_sem,
):
    b = lax.axis_index("bin")
    x = lax.axis_index("row")
    c = lax.axis_index("col")
    k = lax.rem(c, 2)
    zl = c // 2
    y = lax.rem(b, 4)
    zh = b // 4
    z = zh * 2 + zl

    def at(x_, y_, z_, k_):
        return {"bin": (z_ // 2) * 4 + y_, "row": x_, "col": lax.rem(z_, 2) * 2 + k_}

    sibling = at(x, y, z, 1 - k)

    def rdma(src, dst, s, r, device):
        return pltpu.make_async_remote_copy(
            src_ref=src, dst_ref=dst, send_sem=s, recv_sem=r, device_id=device, device_id_type=MESH
        )

    loads = [
        pltpu.make_async_copy(snap_hbm, snap, in_sem.at[0]),
        pltpu.make_async_copy(fi_hbm, fi, in_sem.at[1]),
        pltpu.make_async_copy(fo_hbm, fo, in_sem.at[2]),
        pltpu.make_async_copy(x0_hbm.at[pl.ds(pl.multiple_of(x * 1024, 1024), 1024)], x0, in_sem.at[3]),
    ]
    for load in loads:
        load.start()

    barrier = pltpu.get_barrier_semaphore()
    place = b * 4 + c

    def greet(i, carry):
        other = lax.rem(place + i, 32)
        pl.semaphore_signal(
            barrier, inc=1, device_id={"bin": other // 4, "row": x, "col": lax.rem(other, 4)}, device_id_type=MESH
        )
        return carry

    lax.fori_loop(1, 32, greet, 0)

    def greet_rows(i, carry):
        pl.semaphore_signal(
            barrier, inc=1, device_id={"bin": b, "row": lax.rem(x + 1 + i // 4, 4), "col": lax.rem(i, 4)},
            device_id_type=MESH,
        )
        return carry

    lax.fori_loop(0, 12, greet_rows, 0)

    loads[0].wait()
    loads[1].wait()
    for bb in range(8):
        proj[x, 16 * bb : 16 * bb + 16, :] = dot(snap[16 * bb : 16 * bb + 16, :], fi[bb], 1, 0)
    pl.semaphore_wait(barrier, 43)

    def row_exchange(buf, s, r):
        sends = []
        for i in (2, 1, 3):
            cp = rdma(buf.at[x], buf.at[x], s.at[i], r.at[i], at(mod4(x + i), y, z, k))
            cp.start()
            sends.append(cp)
        return sends

    def row_collect(buf, s, r):
        for i in (1, 3, 2):
            frm = mod4(x - i)
            rdma(buf.at[frm], buf.at[frm], s.at[i], r.at[i], at(frm, y, z, k)).wait_recv()
        return (buf[0] + buf[1]) + (buf[2] + buf[3])

    proj_sends = row_exchange(proj, p_s, p_r)
    loads[2].wait()
    projected = row_collect(proj, p_s, p_r).astype(BF16)
    here = z * 4 + y
    for bb in range(8):
        lifted = dot(projected[16 * bb : 16 * bb + 16, :], fo[bb], 1, 1)
        full[here, 16 * bb : 16 * bb + 16, :] = (
            snap[16 * bb : 16 * bb + 16, :].astype(F32) + lifted
        ).astype(BF16)

    is_source = zl == x // 2
    own_ci = lax.rem(x, 2)

    def slab_send(i):
        to = lax.rem(b + i, 8)
        return rdma(
            full.at[here, :, pl.ds(pl.multiple_of(to * 128, 128), 128)], slab.at[own_ci, here], a_s.at[i],
            a_r.at[here], {"bin": to, "row": x, "col": (x // 2) * 2 + k},
        )

    def start_slab(i, carry):
        slab_send(i).start()
        return carry

    lax.fori_loop(1, 8, start_slab, 0)
    slab_local = pltpu.make_async_copy(
        full.at[here, :, pl.ds(pl.multiple_of(b * 128, 128), 128)], slab.at[own_ci, here], l_sem.at[0]
    )

    @pl.when(is_source)
    def _():
        slab_local.start()

    @pl.when(jnp.logical_not(is_source))
    def _():
        slab_send(0).start()

    def block_of(half, u, v):
        return (v * 4 + u) if half == 0 else (u * 4 + v)

    def dev_of(half, u, v):
        return at(x, u, v, k) if half == 0 else at(x, v, u, k)

    def ring(half):
        return (y, z) if half == 0 else (z, y)

    def gcopy(half, event, u, v, lo, rows, tu, tv):
        blk = full.at[block_of(half, u, v), pl.ds(64 * half + lo, rows)]
        e = 20 * half + event
        return rdma(blk, blk, g_s.at[e], g_r.at[e], dev_of(half, tu, tv))

    pending = []

    def gsend(*args):
        cp = gcopy(*args)
        cp.start()
        pending.append(cp)

    def gwait(half, event, u, v, lo, rows):
        gcopy(half, event, u, v, lo, rows, mod4(ring(half)[0] + 1), v).wait_recv()

    def second_send(half, t):
        u, v = ring(half)
        w = mod4(u + (0, -1, 1, 2)[t])
        gsend(half, 4 + 4 * t, w, v, 0, 64, u, mod4(v + 1))
        gsend(half, 5 + 4 * t, w, v, 0, 64, u, mod4(v - 1))

    def second_forward(half, t):
        u, v = ring(half)
        w = mod4(u + (0, -1, 1, 2)[t])
        gwait(half, 4 + 4 * t, w, mod4(v - 1), 0, 64)
        gsend(half, 6 + 4 * t, w, mod4(v - 1), 0, 32, u, mod4(v + 1))
        gwait(half, 5 + 4 * t, w, mod4(v + 1), 0, 64)
        gsend(half, 7 + 4 * t, w, mod4(v + 1), 32, 32, u, mod4(v - 1))

    def second_last(half, t):
        u, v = ring(half)
        w = mod4(u + (0, -1, 1, 2)[t])
        gwait(half, 6 + 4 * t, w, mod4(v + 2), 0, 32)
        gwait(half, 7 + 4 * t, w, mod4(v + 2), 32, 32)

    for half in (0, 1):
        u, v = ring(half)
        gsend(half, 0, u, v, 0, 64, mod4(u + 1), v)
        gsend(half, 1, u, v, 0, 64, mod4(u - 1), v)
    for half in (0, 1):
        second_send(half, 0)
    for half in (0, 1):
        u, v = ring(half)
        gwait(half, 0, mod4(u - 1), v, 0, 64)
        gsend(half, 2, mod4(u - 1), v, 0, 32, mod4(u + 1), v)
        gwait(half, 1, mod4(u + 1), v, 0, 64)
        gsend(half, 3, mod4(u + 1), v, 32, 32, mod4(u - 1), v)
        second_send(half, 1)
        second_send(half, 2)

    def spread(ci, g, n, device):
        blk = slab.at[ci, pl.ds(4 * g, 4)]
        return rdma(blk, blk, x_s.at[ci, g, n], x_r.at[ci, g], device)

    right, left = at(mod4(x + 1), y, z, k), at(mod4(x - 1), y, z, k)

    @pl.when(is_source)
    def _():
        slab_local.wait()

        def arrived(i, carry):
            frm = lax.rem(here + i, 16)
            rdma(
                slab.at[own_ci, frm], slab.at[own_ci, frm], a_s.at[0], a_r.at[frm],
                at(x, lax.rem(frm, 4), frm // 4, k),
            ).wait_recv()
            return carry

        lax.fori_loop(1, 16, arrived, 0)
        for g in range(4):
            spread(own_ci, g, 0, right).start()
            spread(own_ci, g, 1, left).start()

    def spread_step(g):
        for ci in (0, 1):
            d = mod4(x - (2 * zl + ci))

            @pl.when(d != 0)
            def _():
                spread(ci, g, 0, right).wait_recv()

            @pl.when(d == (3 if ci == 0 else 1))
            def _():
                spread(ci, g, 0, left if ci == 0 else right).start()

    for half in (0, 1):
        second_forward(half, 0)
    for half in (0, 1):
        u, v = ring(half)
        gwait(half, 2, mod4(u + 2), v, 0, 32)
        gwait(half, 3, mod4(u + 2), v, 32, 32)
        second_send(half, 3)
    spread_step(0)
    for half in (0, 1):
        second_forward(half, 1)
        second_forward(half, 2)
    spread_step(1)
    spread_step(2)
    for half in (0, 1):
        second_forward(half, 3)
    spread_step(3)
    for half in (0, 1):
        for t in range(4):
            second_last(half, t)

    sib_sends = []
    lhs = jnp.concatenate([slab[0].reshape(2048, 128).T, slab[1].reshape(2048, 128).T], axis=0)
    for n in range(4):
        acc[n] = dot(lhs, full[:, :, 256 * n : 256 * n + 256].reshape(2048, 256), 1, 0)
        cp = rdma(
            acc.at[n, pl.ds(pl.multiple_of((1 - k) * 128, 128), 128)], sibc.at[n], c_s.at[n], c_r.at[n], sibling
        )
        cp.start()
        sib_sends.append(cp)
    scaling = 1.0 / 4096
    mine = pl.ds(pl.multiple_of(k * 128, 128), 128)
    for n in range(4):
        sib_sends[n].wait_recv()
        total = (acc[n, mine] + sibc[n]) * scaling
        piece[:, 256 * n : 256 * n + 256] = total
        cov_ref[b, :, 256 * n : 256 * n + 256] = total.astype(BF16)

    def csend(event, blk_b, lo, rows, device):
        blk = cov_ref.at[blk_b, pl.ds(lo, rows)]
        cp = rdma(blk, blk, v_s.at[event], v_r.at[event], device)
        cp.start()
        pending.append(cp)

    def cwait(event, blk_b, lo, rows):
        blk = cov_ref.at[blk_b, pl.ds(lo, rows)]
        rdma(blk, blk, v_s.at[event], v_r.at[event], sibling).wait_recv()

    yup, ydn = at(x, mod4(y + 1), z, k), at(x, mod4(y - 1), z, k)
    zfar = at(x, y, mod4(z + 2), k)
    yu, yd, yo = mod4(y + 1), mod4(y - 1), mod4(y + 2)
    far = 4 * (1 - zh)
    near = 4 * zh

    loads[3].wait()
    img[x] = dot(piece[...], x0[...], 1, 0, HI)
    img_sends = row_exchange(img, i_s, i_r)
    csend(2, b, 0, 128, zfar)
    csend(0, b, 0, 128, yup)
    csend(1, b, 0, 128, ydn)
    image = row_collect(img, i_s, i_r)

    gpart[...] = dot(image.T, image, 1, 0, HI)
    gsib_send = rdma(
        gpart.at[pl.ds(pl.multiple_of(32 * x + 16 * (1 - k), 16), 16)], gsib, gs_s.at[0], gs_r.at[0], sibling
    )
    gsib_send.start()

    part[...] = dot(piece[...].T, image, 1, 0, HI).reshape(2, 2, 256, 128)
    sibp_sends = []
    for h in (0, 1):
        cp = rdma(part.at[h, 1 - k], sibp.at[h], q_s.at[h], q_r.at[h], sibling)
        cp.start()
        sibp_sends.append(cp)

    gsib_send.wait_recv()
    gown[...] = gpart[pl.ds(pl.multiple_of(32 * x + 16 * k, 16), 16), :] + gsib[...]
    gscat[here] = gown[...]

    def plane_peer(i):
        other = lax.rem(here + i, 16)
        return at(x, lax.rem(other, 4), other // 4, k)

    def gram_send(i):
        return rdma(gown, gscat.at[here], ga_s.at[0, i], ga_r.at[0, i], plane_peer(i))

    def gram_start(i, carry):
        gram_send(i).start()
        return carry

    lax.fori_loop(1, 16, gram_start, 0)

    for h in (0, 1):
        sibp_sends[h].wait_recv()
        sibp[h] = sibp[h] + part[h, k]

    def scat_send(i):
        other = lax.rem(here + i, 16)
        oz = other // 4
        ob = (oz // 2) * 4 + lax.rem(other, 4)
        return rdma(
            sibp.at[lax.rem(oz, 2), pl.ds(pl.multiple_of(32 * ob, 32), 32)], scat.at[here], r_s.at[i], r_r.at[i],
            plane_peer(i),
        )

    def scat_start(i, carry):
        scat_send(i).start()
        return carry

    lax.fori_loop(1, 16, scat_start, 0)
    scat[here] = sibp[zl, pl.ds(pl.multiple_of(32 * b, 32), 32)]

    cwait(0, near + yd, 0, 128)
    csend(3, near + yd, 0, 64, yup)
    cwait(1, near + yu, 0, 128)
    csend(4, near + yu, 64, 64, ydn)

    def gram_arrived(i, carry):
        frm = lax.rem(here + 16 - i, 16)
        rdma(gown, gscat.at[frm], ga_s.at[0, i], ga_r.at[0, i], plane_peer(i)).wait_recv()
        return carry

    lax.fori_loop(1, 16, gram_arrived, 0)

    def add_slots(ref, n):
        total = ref[0]
        for i in range(1, n):
            total = total + ref[i]
        return total

    gslice = x * 2 + k
    gram[pl.ds(pl.multiple_of(16 * gslice, 16), 16), :] = add_slots(gscat, 16)

    def gram_share(buf, i, first):
        if first:
            own = gslice
            other = lax.rem(own + i, 8)
            device = at(other // 2, y, z, lax.rem(other, 2))
        else:
            own = b
            other = lax.rem(own + i, 8)
            device = {"bin": other, "row": x, "col": c}
        n = 0 if first else 1
        blk = buf.at[pl.ds(pl.multiple_of(16 * own, 16), 16)]
        return rdma(blk, blk, gb_s.at[n, i], gb_r.at[n, i], device)

    def share_wait(buf, i, first):
        own = gslice if first else b
        frm = lax.rem(own + 8 - i, 8)
        n = 0 if first else 1
        blk = buf.at[pl.ds(pl.multiple_of(16 * frm, 16), 16)]
        rdma(blk, blk, gb_s.at[n, i], gb_r.at[n, i], sibling).wait_recv()

    for i in range(1, 8):
        gram_share(gram, i, True).start()

    def scat_arrived(i, carry):
        frm = lax.rem(here + 16 - i, 16)
        rdma(scat.at[frm], scat.at[frm], r_s.at[i], r_r.at[i], plane_peer(i)).wait_recv()
        return carry

    lax.fori_loop(1, 16, scat_arrived, 0)
    zall[pl.ds(pl.multiple_of(32 * b, 32), 32), :] = add_slots(scat, 16)

    def bin_share(i):
        blk = zall.at[pl.ds(pl.multiple_of(32 * b, 32), 32)]
        return rdma(blk, blk, z_s.at[i], z_r.at[i], {"bin": lax.rem(b + i, 8), "row": x, "col": c})

    for i in range(1, 8):
        bin_share(i).start()

    cwait(2, far + y, 0, 128)
    csend(5, far + y, 0, 128, yup)
    csend(6, far + y, 0, 128, ydn)

    for i in range(1, 8):
        share_wait(gram, i, True)
    for i in range(1, 8):
        gram_share(gram, i, True).wait_send()
    invert_factor(gram)

    for i in range(1, 8):
        frm = lax.rem(b + 8 - i, 8)
        blk = zall.at[pl.ds(pl.multiple_of(32 * frm, 32), 32)]
        rdma(blk, blk, z_s.at[i], z_r.at[i], sibling).wait_recv()
    for i in range(1, 8):
        bin_share(i).wait_send()
    second = apply_factor(gram, zall[...])
    basis_ref[...] = second
    gpart2[...] = dot(second.T, second, 1, 0, HI)

    q = x * 4 + c
    gslice_rows = pl.ds(pl.multiple_of(16 * b, 16), 16)
    gscat2[q] = gpart2[gslice_rows, :]

    def mesh_peer(i):
        other = lax.rem(q + i, 16)
        return {"bin": b, "row": other // 4, "col": lax.rem(other, 4)}

    def gram2_send(i):
        oq = q
        return rdma(gscat2.at[oq], gscat2.at[oq], ga_s.at[1, i], ga_r.at[1, i], mesh_peer(i))

    def gram2_start(i, carry):
        gram2_send(i).start()
        return carry

    lax.fori_loop(1, 16, gram2_start, 0)

    cwait(5, far + yd, 0, 128)
    csend(7, far + yd, 0, 64, yup)
    cwait(6, far + yu, 0, 128)
    csend(8, far + yu, 64, 64, ydn)

    def gram2_arrived(i, carry):
        frm = lax.rem(q + 16 - i, 16)
        rdma(gscat2.at[frm], gscat2.at[frm], ga_s.at[1, i], ga_r.at[1, i], mesh_peer(i)).wait_recv()
        return carry

    lax.fori_loop(1, 16, gram2_arrived, 0)
    gram2[gslice_rows, :] = add_slots(gscat2, 16)
    for i in range(1, 8):
        gram_share(gram2, i, False).start()
    for i in range(1, 8):
        share_wait(gram2, i, False)
    for i in range(1, 8):
        gram_share(gram2, i, False).wait_send()
    invert_factor(gram2)
    basis_ref[...] = apply_factor(gram2, basis_ref[...]) * 64.0

    cwait(3, near + yo, 0, 64)
    cwait(4, near + yo, 64, 64)
    cwait(7, far + yo, 0, 64)
    cwait(8, far + yo, 64, 64)

    for cp in pending + proj_sends + img_sends + sib_sends + sibp_sends + [gsib_send]:
        cp.wait_send()

    def drain(i, carry):
        gram_send(i).wait_send()
        scat_send(i).wait_send()
        gram2_send(i).wait_send()
        return carry

    lax.fori_loop(1, 16, drain, 0)

    def drain_slab(i, carry):
        slab_send(i).wait_send()
        return carry

    lax.fori_loop(1, 8, drain_slab, 0)

    @pl.when(jnp.logical_not(is_source))
    def _():
        slab_send(0).wait_send()

    @pl.when(is_source)
    def _():
        for g in range(4):
            spread(own_ci, g, 0, right).wait_send()
            spread(own_ci, g, 1, left).wait_send()

    for ci in (0, 1):
        d = mod4(x - (2 * zl + ci))

        @pl.when(d == (3 if ci == 0 else 1))
        def _():
            for g in range(4):
                spread(ci, g, 0, left if ci == 0 else right).wait_send()


def shards(snapshots, focus_in, focus_out, start_basis):
    snaps = snapshots.transpose(1, 2, 0).reshape(128, 1024)
    dma = pltpu.SemaphoreType.DMA
    anywhere = pl.BlockSpec(memory_space=pl.ANY)
    in_vmem = pl.BlockSpec(memory_space=pltpu.VMEM)
    pieces, basis_out = pl.pallas_call(
        kernel,
        out_shape=(
            jax.ShapeDtypeStruct((8, 128, 1024), BF16),
            jax.ShapeDtypeStruct((256, 128), F32),
        ),
        in_specs=[anywhere] * 4,
        out_specs=(in_vmem, in_vmem),
        scratch_shapes=[
            pltpu.VMEM((128, 1024), BF16),
            pltpu.VMEM((8, 1024, 128), BF16),
            pltpu.VMEM((8, 1024, 128), BF16),
            pltpu.VMEM((1024, 128), F32),
            pltpu.VMEM((4, 128, 128), F32),
            pltpu.VMEM((16, 128, 1024), BF16),
            pltpu.VMEM((2, 16, 128, 128), BF16),
            pltpu.VMEM((4, 256, 256), F32),
            pltpu.VMEM((4, 128, 256), F32),
            pltpu.VMEM((128, 1024), F32),
            pltpu.VMEM((4, 128, 128), F32),
            pltpu.VMEM((2, 2, 256, 128), F32),
            pltpu.VMEM((2, 256, 128), F32),
            pltpu.VMEM((16, 32, 128), F32),
            pltpu.VMEM((256, 128), F32),
            pltpu.VMEM((128, 128), F32),
            pltpu.VMEM((16, 128), F32),
            pltpu.VMEM((16, 128), F32),
            pltpu.VMEM((16, 16, 128), F32),
            pltpu.VMEM((128, 128), F32),
            pltpu.VMEM((128, 128), F32),
            pltpu.VMEM((16, 16, 128), F32),
            pltpu.VMEM((128, 128), F32),
            dma((4,)),
            dma((4,)), dma((4,)),
            dma((40,)), dma((40,)),
            dma((8,)), dma((16,)),
            dma((2, 4, 2)), dma((2, 4)),
            dma((4,)), dma((4,)),
            dma((9,)), dma((9,)),
            dma((4,)), dma((4,)),
            dma((2,)), dma((2,)),
            dma((16,)), dma((16,)),
            dma((8,)), dma((8,)),
            dma((1,)), dma((1,)),
            dma((2, 16)), dma((2, 16)),
            dma((2, 8)), dma((2, 8)),
            dma((1,)),
        ],
        compiler_params=pltpu.CompilerParams(
            collective_id=0, has_side_effects=True, vmem_limit_bytes=40 * 2**20
        ),
    )(snaps, focus_in, focus_out, start_basis)
    return pieces.reshape(1024, 1024).astype(F32), basis_out


def solution(mesh):
    in_specs = (P("row", "bin", "col"), P("bin", "row", None), P("bin", "row", None), P())
    out_specs = (P("col", "row"), P(("row", "col"), None))
    return jax.shard_map(shards, mesh=mesh, in_specs=in_specs, out_specs=out_specs, check_vma=False)
```

```python
import functools
import math

import jax
import jax.numpy as jnp
from jax import lax
from jax.experimental import pallas as pl
from jax.experimental.pallas import tpu as pltpu
from jax.sharding import PartitionSpec as P

MESH = pl.DeviceIdType.MESH
HI = lax.Precision.HIGHEST
F32 = jnp.float32
BF16 = jnp.bfloat16


def mod4(v):
    return lax.rem(v + 4, 4)


def dot(a, b, ca, cb, precision=None):
    return lax.dot_general(a, b, (((ca,), (cb,)), ((), ())), precision=precision, preferred_element_type=F32)


def inverse_factor(gram):
    lane = lax.broadcasted_iota(jnp.int32, (8, 128), 1)
    sub = lax.broadcasted_iota(jnp.int32, (8, 128), 0)

    def over_lanes(tile, j):
        return jnp.broadcast_to(tile[:, j : j + 1], (8, 128))

    def over_rows(tile, i):
        return jnp.broadcast_to(tile[i : i + 1, :], (8, 128))

    tiles = list(gram)
    done = []
    for p in range(16):
        first = 8 * p
        now = tiles[p]
        cols = [over_lanes(now, first + e) for e in range(8)]
        left = [[over_rows(cols[e], i) for e in range(i + 1)] for i in range(8)]
        low = [[None] * 8 for _ in range(8)]
        inv = [None] * 8
        for e in range(8):
            inv[e] = 1.0 / left[e][e]
            for i in range(e + 1, 8):
                low[i][e] = left[i][e] * inv[e]
            for i in range(e + 1, 8):
                for f in range(e + 1, i + 1):
                    left[i][f] = left[i][f] - low[i][e] * left[f][e]
        in_panel = (lane >= first) & (lane < first + 8)
        upper = []
        for i in range(8):
            row = jnp.where(in_panel, jnp.where(lane == first + i, 1.0, 0.0), over_rows(now, i))
            for e in range(i):
                row = row - low[i][e] * upper[e]
            upper.append(row)
        tile, scale = upper[0], inv[0]
        for i in range(1, 8):
            tile = jnp.where(sub == i, upper[i], tile)
            scale = jnp.where(sub == i, inv[i], scale)
        done.append(jnp.where(lane <= sub + first, tile, 0.0) * jnp.sqrt(scale))
        scaled = [upper[e] * inv[e] for e in range(8)]
        for q in range(p + 1, 16):
            total = jnp.where(in_panel, 0.0, tiles[q])
            lower = []
            for e in range(8):
                col = over_lanes(tiles[q], first + e)
                for f in range(e):
                    col = col - lower[f] * low[e][f]
                lower.append(col)
                total = total - col * scaled[e]
            tiles[q] = total
    return jnp.concatenate(done, axis=0)


def apply_factor(gram, block):
    return dot(block, inverse_factor([gram[8 * i : 8 * i + 8, :] for i in range(16)]), 1, 1, HI)


def kernel(
    snap_hbm, fi_hbm, fo_hbm, x0_hbm, cov_ref, basis_ref,
    snap, fi, fo, x0, proj, full, slab, acc, sibc, piece, img, part, sibp, scat, zall,
    gpart, gsib, gown, gscat, gram, gpart2, gscat2, gram2, in_sem,
    p_s, p_r, g_s, g_r, a_s, a_r, x_s, x_r, c_s, c_r, v_s, v_r, i_s, i_r, q_s, q_r, r_s, r_r, z_s, z_r,
    gs_s, gs_r, ga_s, ga_r, gb_s, gb_r, l_sem,
):
    b = lax.axis_index("bin")
    x = lax.axis_index("row")
    c = lax.axis_index("col")
    k = lax.rem(c, 2)
    zl = c // 2
    y = lax.rem(b, 4)
    zh = b // 4
    z = zh * 2 + zl

    def at(x_, y_, z_, k_):
        return {"bin": (z_ // 2) * 4 + y_, "row": x_, "col": lax.rem(z_, 2) * 2 + k_}

    sibling = at(x, y, z, 1 - k)
    pending, late = [], []

    def rdma(src, dst, s, r, device):
        return pltpu.make_async_remote_copy(
            src_ref=src, dst_ref=dst, send_sem=s, recv_sem=r, device_id=device, device_id_type=MESH
        )

    loads = [
        pltpu.make_async_copy(snap_hbm, snap, in_sem.at[0]),
        pltpu.make_async_copy(fi_hbm, fi, in_sem.at[1]),
        pltpu.make_async_copy(fo_hbm, fo, in_sem.at[2]),
        pltpu.make_async_copy(x0_hbm.at[pl.ds(pl.multiple_of(x * 1024, 1024), 1024)], x0, in_sem.at[3]),
    ]
    for load in loads:
        load.start()

    barrier = pltpu.get_barrier_semaphore()
    place = b * 4 + c

    def greet(i, carry):
        other = lax.rem(place + i, 32)
        pl.semaphore_signal(
            barrier, inc=1, device_id={"bin": other // 4, "row": x, "col": lax.rem(other, 4)}, device_id_type=MESH
        )
        return carry

    lax.fori_loop(1, 32, greet, 0)

    def greet_rows(i, carry):
        pl.semaphore_signal(
            barrier, inc=1, device_id={"bin": b, "row": lax.rem(x + 1 + i // 4, 4), "col": lax.rem(i, 4)},
            device_id_type=MESH,
        )
        return carry

    lax.fori_loop(0, 12, greet_rows, 0)

    loads[0].wait()
    loads[1].wait()
    for bb in range(8):
        proj[x, 16 * bb : 16 * bb + 16, :] = dot(snap[16 * bb : 16 * bb + 16, :], fi[bb], 1, 0)
    pl.semaphore_wait(barrier, 43)

    def row_exchange(buf, s, r):
        for i in (2, 1, 3):
            cp = rdma(buf.at[x], buf.at[x], s.at[i], r.at[i], at(mod4(x + i), y, z, k))
            cp.start()
            pending.append(cp)

    def row_collect(buf, s, r):
        for i in (1, 3, 2):
            frm = mod4(x - i)
            rdma(buf.at[frm], buf.at[frm], s.at[i], r.at[i], at(frm, y, z, k)).wait_recv()
        return (buf[0] + buf[1]) + (buf[2] + buf[3])

    row_exchange(proj, p_s, p_r)
    def loop_wait(send, n):
        def one(i, carry):
            send(i).wait_send()
            return carry

        late.append(lambda: lax.fori_loop(1, n, one, 0))

    loads[2].wait()
    projected = row_collect(proj, p_s, p_r).astype(BF16)
    here = z * 4 + y
    for bb in range(8):
        lifted = dot(projected[16 * bb : 16 * bb + 16, :], fo[bb], 1, 1)
        full[here, 16 * bb : 16 * bb + 16, :] = (
            snap[16 * bb : 16 * bb + 16, :].astype(F32) + lifted
        ).astype(BF16)

    is_source = zl == x // 2
    own_ci = lax.rem(x, 2)

    def slab_send(i):
        to = lax.rem(b + i, 8)
        return rdma(
            full.at[here, :, pl.ds(pl.multiple_of(to * 128, 128), 128)], slab.at[own_ci, here], a_s.at[i],
            a_r.at[here], {"bin": to, "row": x, "col": (x // 2) * 2 + k},
        )

    def start_slab(i, carry):
        slab_send(i).start()
        return carry

    lax.fori_loop(1, 8, start_slab, 0)
    loop_wait(slab_send, 8)
    slab_local = pltpu.make_async_copy(
        full.at[here, :, pl.ds(pl.multiple_of(b * 128, 128), 128)], slab.at[own_ci, here], l_sem.at[0]
    )

    @pl.when(is_source)
    def _():
        slab_local.start()

    @pl.when(jnp.logical_not(is_source))
    def _():
        slab_send(0).start()

    def finish_slab():
        @pl.when(jnp.logical_not(is_source))
        def _():
            slab_send(0).wait_send()

    late.append(finish_slab)

    def block_of(half, u, v):
        return (v * 4 + u) if half == 0 else (u * 4 + v)

    def dev_of(half, u, v):
        return at(x, u, v, k) if half == 0 else at(x, v, u, k)

    def ring(half):
        return (y, z) if half == 0 else (z, y)

    def gcopy(half, event, u, v, lo, rows, tu, tv):
        blk = full.at[block_of(half, u, v), pl.ds(64 * half + lo, rows)]
        e = 20 * half + event
        return rdma(blk, blk, g_s.at[e], g_r.at[e], dev_of(half, tu, tv))

    def gsend(*args):
        cp = gcopy(*args)
        cp.start()
        pending.append(cp)

    def gwait(half, event, u, v, lo, rows):
        gcopy(half, event, u, v, lo, rows, mod4(ring(half)[0] + 1), v).wait_recv()

    def second_send(half, t):
        u, v = ring(half)
        w = mod4(u + (0, -1, 1, 2)[t])
        gsend(half, 4 + 4 * t, w, v, 0, 64, u, mod4(v + 1))
        gsend(half, 5 + 4 * t, w, v, 0, 64, u, mod4(v - 1))

    def second_forward(half, t):
        u, v = ring(half)
        w = mod4(u + (0, -1, 1, 2)[t])
        gwait(half, 4 + 4 * t, w, mod4(v - 1), 0, 64)
        gsend(half, 6 + 4 * t, w, mod4(v - 1), 0, 32, u, mod4(v + 1))
        gwait(half, 5 + 4 * t, w, mod4(v + 1), 0, 64)
        gsend(half, 7 + 4 * t, w, mod4(v + 1), 32, 32, u, mod4(v - 1))

    def second_last(half, t):
        u, v = ring(half)
        w = mod4(u + (0, -1, 1, 2)[t])
        gwait(half, 6 + 4 * t, w, mod4(v + 2), 0, 32)
        gwait(half, 7 + 4 * t, w, mod4(v + 2), 32, 32)

    for half in (0, 1):
        u, v = ring(half)
        gsend(half, 0, u, v, 0, 64, mod4(u + 1), v)
        gsend(half, 1, u, v, 0, 64, mod4(u - 1), v)
    for half in (0, 1):
        second_send(half, 0)
    for half in (0, 1):
        u, v = ring(half)
        gwait(half, 0, mod4(u - 1), v, 0, 64)
        gsend(half, 2, mod4(u - 1), v, 0, 32, mod4(u + 1), v)
        gwait(half, 1, mod4(u + 1), v, 0, 64)
        gsend(half, 3, mod4(u + 1), v, 32, 32, mod4(u - 1), v)
        second_send(half, 1)
        second_send(half, 2)

    def spread(ci, g, n, device):
        blk = slab.at[ci, pl.ds(4 * g, 4)]
        return rdma(blk, blk, x_s.at[ci, g, n], x_r.at[ci, g], device)

    right, left = at(mod4(x + 1), y, z, k), at(mod4(x - 1), y, z, k)

    @pl.when(is_source)
    def _():
        slab_local.wait()

        def arrived(i, carry):
            frm = lax.rem(here + i, 16)
            rdma(
                slab.at[own_ci, frm], slab.at[own_ci, frm], a_s.at[0], a_r.at[frm],
                at(x, lax.rem(frm, 4), frm // 4, k),
            ).wait_recv()
            return carry

        lax.fori_loop(1, 16, arrived, 0)
        for g in range(4):
            spread(own_ci, g, 0, right).start()
            spread(own_ci, g, 1, left).start()

    def spread_step(g):
        for ci in (0, 1):
            d = mod4(x - (2 * zl + ci))

            @pl.when(d != 0)
            def _():
                spread(ci, g, 0, right).wait_recv()

            @pl.when(d == (3 if ci == 0 else 1))
            def _():
                spread(ci, g, 0, left if ci == 0 else right).start()

    def finish_spread():
        @pl.when(is_source)
        def _():
            for g in range(4):
                spread(own_ci, g, 0, right).wait_send()
                spread(own_ci, g, 1, left).wait_send()

        for ci in (0, 1):
            d = mod4(x - (2 * zl + ci))

            @pl.when(d == (3 if ci == 0 else 1))
            def _():
                for g in range(4):
                    spread(ci, g, 0, left if ci == 0 else right).wait_send()

    late.append(finish_spread)

    for half in (0, 1):
        second_forward(half, 0)
    for half in (0, 1):
        u, v = ring(half)
        gwait(half, 2, mod4(u + 2), v, 0, 32)
        gwait(half, 3, mod4(u + 2), v, 32, 32)
        second_send(half, 3)
    spread_step(0)
    for half in (0, 1):
        second_forward(half, 1)
        second_forward(half, 2)
    spread_step(1)
    spread_step(2)
    for half in (0, 1):
        second_forward(half, 3)
    spread_step(3)
    for half in (0, 1):
        for t in range(4):
            second_last(half, t)

    sib_sends = []
    lhs = jnp.concatenate([slab[0].reshape(2048, 128).T, slab[1].reshape(2048, 128).T], axis=0)
    for n in range(4):
        acc[n] = dot(lhs, full[:, :, 256 * n : 256 * n + 256].reshape(2048, 256), 1, 0)
        cp = rdma(
            acc.at[n, pl.ds(pl.multiple_of((1 - k) * 128, 128), 128)], sibc.at[n], c_s.at[n], c_r.at[n], sibling
        )
        cp.start()
        sib_sends.append(cp)
        pending.append(cp)
    scaling = 1.0 / 4096
    mine = pl.ds(pl.multiple_of(k * 128, 128), 128)
    for n in range(4):
        sib_sends[n].wait_recv()
        total = (acc[n, mine] + sibc[n]) * scaling
        piece[:, 256 * n : 256 * n + 256] = total
        cov_ref[b, :, 256 * n : 256 * n + 256] = total.astype(BF16)

    def csend(event, blk_b, lo, rows, device):
        blk = cov_ref.at[blk_b, pl.ds(lo, rows)]
        cp = rdma(blk, blk, v_s.at[event], v_r.at[event], device)
        cp.start()
        pending.append(cp)

    def cwait(event, blk_b, lo, rows):
        blk = cov_ref.at[blk_b, pl.ds(lo, rows)]
        rdma(blk, blk, v_s.at[event], v_r.at[event], sibling).wait_recv()

    yup, ydn = at(x, mod4(y + 1), z, k), at(x, mod4(y - 1), z, k)
    zfar = at(x, y, mod4(z + 2), k)
    yu, yd, yo = mod4(y + 1), mod4(y - 1), mod4(y + 2)
    far = 4 * (1 - zh)
    near = 4 * zh

    loads[3].wait()
    img[x] = dot(piece[...], x0[...], 1, 0, HI)
    row_exchange(img, i_s, i_r)
    csend(2, b, 0, 128, zfar)
    csend(0, b, 0, 128, yup)
    csend(1, b, 0, 128, ydn)
    image = row_collect(img, i_s, i_r)

    gpart[...] = dot(image.T, image, 1, 0, HI)
    gsib_send = rdma(
        gpart.at[pl.ds(pl.multiple_of(32 * x + 16 * (1 - k), 16), 16)], gsib, gs_s.at[0], gs_r.at[0], sibling
    )
    gsib_send.start()
    pending.append(gsib_send)

    part[...] = dot(piece[...].T, image, 1, 0, HI).reshape(2, 2, 256, 128)
    sibp_sends = []
    for h in (0, 1):
        cp = rdma(part.at[h, 1 - k], sibp.at[h], q_s.at[h], q_r.at[h], sibling)
        cp.start()
        sibp_sends.append(cp)
        pending.append(cp)

    gsib_send.wait_recv()
    gown[...] = gpart[pl.ds(pl.multiple_of(32 * x + 16 * k, 16), 16), :] + gsib[...]
    gscat[here] = gown[...]

    def plane_peer(i):
        other = lax.rem(here + i, 16)
        return at(x, lax.rem(other, 4), other // 4, k)

    def gram_send(i):
        return rdma(gown, gscat.at[here], ga_s.at[0, i], ga_r.at[0, i], plane_peer(i))

    def gram_start(i, carry):
        gram_send(i).start()
        return carry

    lax.fori_loop(1, 16, gram_start, 0)
    loop_wait(gram_send, 16)

    for h in (0, 1):
        sibp_sends[h].wait_recv()
        sibp[h] = sibp[h] + part[h, k]

    def scat_send(i):
        other = lax.rem(here + i, 16)
        oz = other // 4
        ob = (oz // 2) * 4 + lax.rem(other, 4)
        return rdma(
            sibp.at[lax.rem(oz, 2), pl.ds(pl.multiple_of(32 * ob, 32), 32)], scat.at[here], r_s.at[i], r_r.at[i],
            plane_peer(i),
        )

    def scat_start(i, carry):
        scat_send(i).start()
        return carry

    lax.fori_loop(1, 16, scat_start, 0)
    loop_wait(scat_send, 16)
    scat[here] = sibp[zl, pl.ds(pl.multiple_of(32 * b, 32), 32)]

    cwait(0, near + yd, 0, 128)
    csend(3, near + yd, 0, 64, yup)
    cwait(1, near + yu, 0, 128)
    csend(4, near + yu, 64, 64, ydn)

    def gram_arrived(i, carry):
        frm = lax.rem(here + 16 - i, 16)
        rdma(gown, gscat.at[frm], ga_s.at[0, i], ga_r.at[0, i], plane_peer(i)).wait_recv()
        return carry

    lax.fori_loop(1, 16, gram_arrived, 0)

    def add_slots(ref, n):
        total = ref[0]
        for i in range(1, n):
            total = total + ref[i]
        return total

    gslice = x * 2 + k
    gram[pl.ds(pl.multiple_of(16 * gslice, 16), 16), :] = add_slots(gscat, 16)

    def gram_share(buf, i, first):
        if first:
            own = gslice
            other = lax.rem(own + i, 8)
            device = at(other // 2, y, z, lax.rem(other, 2))
        else:
            own = b
            other = lax.rem(own + i, 8)
            device = {"bin": other, "row": x, "col": c}
        n = 0 if first else 1
        blk = buf.at[pl.ds(pl.multiple_of(16 * own, 16), 16)]
        return rdma(blk, blk, gb_s.at[n, i], gb_r.at[n, i], device)

    def share_wait(buf, i, first):
        own = gslice if first else b
        frm = lax.rem(own + 8 - i, 8)
        n = 0 if first else 1
        blk = buf.at[pl.ds(pl.multiple_of(16 * frm, 16), 16)]
        rdma(blk, blk, gb_s.at[n, i], gb_r.at[n, i], sibling).wait_recv()

    for i in range(1, 8):
        gram_share(gram, i, True).start()
        pending.append(gram_share(gram, i, True))

    def scat_arrived(i, carry):
        frm = lax.rem(here + 16 - i, 16)
        rdma(scat.at[frm], scat.at[frm], r_s.at[i], r_r.at[i], plane_peer(i)).wait_recv()
        return carry

    lax.fori_loop(1, 16, scat_arrived, 0)
    zall[pl.ds(pl.multiple_of(32 * b, 32), 32), :] = add_slots(scat, 16)

    def bin_share(i):
        blk = zall.at[pl.ds(pl.multiple_of(32 * b, 32), 32)]
        return rdma(blk, blk, z_s.at[i], z_r.at[i], {"bin": lax.rem(b + i, 8), "row": x, "col": c})

    for i in range(1, 8):
        bin_share(i).start()
        pending.append(bin_share(i))

    cwait(2, far + y, 0, 128)
    csend(5, far + y, 0, 128, yup)
    csend(6, far + y, 0, 128, ydn)

    for i in range(1, 8):
        share_wait(gram, i, True)
    inverse = inverse_factor([gram[8 * i : 8 * i + 8, :] for i in range(16)])
    for i in range(1, 8):
        frm = lax.rem(b + 8 - i, 8)
        blk = zall.at[pl.ds(pl.multiple_of(32 * frm, 32), 32)]
        rdma(blk, blk, z_s.at[i], z_r.at[i], sibling).wait_recv()
    second = dot(zall[...], inverse, 1, 1, HI)
    basis_ref[...] = second
    gpart2[...] = dot(second.T, second, 1, 0, HI)

    q = x * 4 + c
    gslice_rows = pl.ds(pl.multiple_of(16 * b, 16), 16)
    gscat2[q] = gpart2[gslice_rows, :]

    def mesh_peer(i):
        other = lax.rem(q + i, 16)
        return {"bin": b, "row": other // 4, "col": lax.rem(other, 4)}

    def gram2_send(i):
        oq = q
        return rdma(gscat2.at[oq], gscat2.at[oq], ga_s.at[1, i], ga_r.at[1, i], mesh_peer(i))

    def gram2_start(i, carry):
        gram2_send(i).start()
        return carry

    lax.fori_loop(1, 16, gram2_start, 0)
    loop_wait(gram2_send, 16)

    cwait(5, far + yd, 0, 128)
    csend(7, far + yd, 0, 64, yup)
    cwait(6, far + yu, 0, 128)
    csend(8, far + yu, 64, 64, ydn)

    def gram2_arrived(i, carry):
        frm = lax.rem(q + 16 - i, 16)
        rdma(gscat2.at[frm], gscat2.at[frm], ga_s.at[1, i], ga_r.at[1, i], mesh_peer(i)).wait_recv()
        return carry

    lax.fori_loop(1, 16, gram2_arrived, 0)
    gram2[gslice_rows, :] = add_slots(gscat2, 16)
    for i in range(1, 8):
        gram_share(gram2, i, False).start()
        pending.append(gram_share(gram2, i, False))
    for i in range(1, 8):
        share_wait(gram2, i, False)
    basis_ref[...] = apply_factor(gram2, basis_ref[...]) * 64.0

    cwait(3, near + yo, 0, 64)
    cwait(4, near + yo, 64, 64)
    cwait(7, far + yo, 0, 64)
    cwait(8, far + yo, 64, 64)

    for cp in pending:
        cp.wait_send()
    for finish in late:
        finish()


def shards(snapshots, focus_in, focus_out, start_basis):
    snaps = snapshots.transpose(1, 2, 0).reshape(128, 1024)
    dma = pltpu.SemaphoreType.DMA
    anywhere = pl.BlockSpec(memory_space=pl.ANY)
    in_vmem = pl.BlockSpec(memory_space=pltpu.VMEM)
    pieces, basis_out = pl.pallas_call(
        kernel,
        out_shape=(
            jax.ShapeDtypeStruct((8, 128, 1024), BF16),
            jax.ShapeDtypeStruct((256, 128), F32),
        ),
        in_specs=[anywhere] * 4,
        out_specs=(in_vmem, in_vmem),
        scratch_shapes=[
            pltpu.VMEM((128, 1024), BF16),
            pltpu.VMEM((8, 1024, 128), BF16),
            pltpu.VMEM((8, 1024, 128), BF16),
            pltpu.VMEM((1024, 128), F32),
            pltpu.VMEM((4, 128, 128), F32),
            pltpu.VMEM((16, 128, 1024), BF16),
            pltpu.VMEM((2, 16, 128, 128), BF16),
            pltpu.VMEM((4, 256, 256), F32),
            pltpu.VMEM((4, 128, 256), F32),
            pltpu.VMEM((128, 1024), F32),
            pltpu.VMEM((4, 128, 128), F32),
            pltpu.VMEM((2, 2, 256, 128), F32),
            pltpu.VMEM((2, 256, 128), F32),
            pltpu.VMEM((16, 32, 128), F32),
            pltpu.VMEM((256, 128), F32),
            pltpu.VMEM((128, 128), F32),
            pltpu.VMEM((16, 128), F32),
            pltpu.VMEM((16, 128), F32),
            pltpu.VMEM((16, 16, 128), F32),
            pltpu.VMEM((128, 128), F32),
            pltpu.VMEM((128, 128), F32),
            pltpu.VMEM((16, 16, 128), F32),
            pltpu.VMEM((128, 128), F32),
            dma((4,)),
            dma((4,)), dma((4,)),
            dma((40,)), dma((40,)),
            dma((8,)), dma((16,)),
            dma((2, 4, 2)), dma((2, 4)),
            dma((4,)), dma((4,)),
            dma((9,)), dma((9,)),
            dma((4,)), dma((4,)),
            dma((2,)), dma((2,)),
            dma((16,)), dma((16,)),
            dma((8,)), dma((8,)),
            dma((1,)), dma((1,)),
            dma((2, 16)), dma((2, 16)),
            dma((2, 8)), dma((2, 8)),
            dma((1,)),
        ],
        compiler_params=pltpu.CompilerParams(
            collective_id=0, has_side_effects=True, vmem_limit_bytes=40 * 2**20
        ),
    )(snaps, focus_in, focus_out, start_basis)
    return pieces.reshape(1024, 1024).astype(F32), basis_out


def solution(mesh):
    in_specs = (P("row", "bin", "col"), P("bin", "row", None), P("bin", "row", None), P())
    out_specs = (P("col", "row"), P(("row", "col"), None))
    return jax.shard_map(shards, mesh=mesh, in_specs=in_specs, out_specs=out_specs, check_vma=False)
```

```python
import functools
import math

import jax
import jax.numpy as jnp
from jax import lax
from jax.experimental import pallas as pl
from jax.experimental.pallas import tpu as pltpu
from jax.sharding import PartitionSpec as P

MESH = pl.DeviceIdType.MESH
HI = lax.Precision.HIGHEST
F32 = jnp.float32
BF16 = jnp.bfloat16


def mod4(v):
    return lax.rem(v + 4, 4)


def dot(a, b, ca, cb, precision=None):
    return lax.dot_general(a, b, (((ca,), (cb,)), ((), ())), precision=precision, preferred_element_type=F32)


def inverse_factor(gram):
    lane = lax.broadcasted_iota(jnp.int32, (8, 128), 1)
    sub = lax.broadcasted_iota(jnp.int32, (8, 128), 0)

    def over_lanes(tile, j):
        return jnp.broadcast_to(tile[:, j : j + 1], (8, 128))

    def over_rows(tile, i):
        return jnp.broadcast_to(tile[i : i + 1, :], (8, 128))

    tiles = list(gram)
    done = []
    for p in range(16):
        first = 8 * p
        now = tiles[p]
        cols = [over_lanes(now, first + e) for e in range(8)]
        left = [[over_rows(cols[e], i) for e in range(i + 1)] for i in range(8)]
        low = [[None] * 8 for _ in range(8)]
        inv = [None] * 8
        for e in range(8):
            inv[e] = 1.0 / left[e][e]
            for i in range(e + 1, 8):
                low[i][e] = left[i][e] * inv[e]
            for i in range(e + 1, 8):
                for f in range(e + 1, i + 1):
                    left[i][f] = left[i][f] - low[i][e] * left[f][e]
        in_panel = (lane >= first) & (lane < first + 8)
        upper = []
        for i in range(8):
            row = jnp.where(in_panel, jnp.where(lane == first + i, 1.0, 0.0), over_rows(now, i))
            for e in range(i):
                row = row - low[i][e] * upper[e]
            upper.append(row)
        tile, scale = upper[0], inv[0]
        for i in range(1, 8):
            tile = jnp.where(sub == i, upper[i], tile)
            scale = jnp.where(sub == i, inv[i], scale)
        done.append(jnp.where(lane <= sub + first, tile, 0.0) * jnp.sqrt(scale))
        scaled = [upper[e] * inv[e] for e in range(8)]
        for q in range(p + 1, 16):
            total = jnp.where(in_panel, 0.0, tiles[q])
            lower = []
            for e in range(8):
                col = over_lanes(tiles[q], first + e)
                for f in range(e):
                    col = col - lower[f] * low[e][f]
                lower.append(col)
                total = total - col * scaled[e]
            tiles[q] = total
    return jnp.concatenate(done, axis=0)


def apply_factor(gram, block):
    return dot(block, inverse_factor([gram[8 * i : 8 * i + 8, :] for i in range(16)]), 1, 1, HI)


def kernel(
    snap_hbm, fi_hbm, fo_hbm, x0_hbm, cov_ref, basis_ref,
    snap, fi, fo, x0, proj, full, slab, acc, sibc, piece, img, part, sibp, scat, zall,
    gpart, gsib, gown, gscat, gram, gpart2, gscat2, gram2, in_sem,
    p_s, p_r, g_s, g_r, a_s, a_r, x_s, x_r, c_s, c_r, v_s, v_r, i_s, i_r, q_s, q_r, r_s, r_r, z_s, z_r,
    gs_s, gs_r, ga_s, ga_r, gb_s, gb_r, l_sem,
):
    b = lax.axis_index("bin")
    x = lax.axis_index("row")
    c = lax.axis_index("col")
    k = lax.rem(c, 2)
    zl = c // 2
    y = lax.rem(b, 4)
    zh = b // 4
    z = zh * 2 + zl

    def at(x_, y_, z_, k_):
        return {"bin": (z_ // 2) * 4 + y_, "row": x_, "col": lax.rem(z_, 2) * 2 + k_}

    sibling = at(x, y, z, 1 - k)
    pending, late = [], []

    def rdma(src, dst, s, r, device):
        return pltpu.make_async_remote_copy(
            src_ref=src, dst_ref=dst, send_sem=s, recv_sem=r, device_id=device, device_id_type=MESH
        )

    loads = [
        pltpu.make_async_copy(snap_hbm, snap, in_sem.at[0]),
        pltpu.make_async_copy(fi_hbm, fi, in_sem.at[1]),
        pltpu.make_async_copy(fo_hbm, fo, in_sem.at[2]),
        pltpu.make_async_copy(x0_hbm.at[pl.ds(pl.multiple_of(x * 1024, 1024), 1024)], x0, in_sem.at[3]),
    ]
    for load in loads:
        load.start()

    barrier = pltpu.get_barrier_semaphore()
    place = b * 4 + c

    def greet(i, carry):
        other = lax.rem(place + i, 32)
        pl.semaphore_signal(
            barrier, inc=1, device_id={"bin": other // 4, "row": x, "col": lax.rem(other, 4)}, device_id_type=MESH
        )
        return carry

    lax.fori_loop(1, 32, greet, 0)

    def greet_rows(i, carry):
        pl.semaphore_signal(
            barrier, inc=1, device_id={"bin": b, "row": lax.rem(x + 1 + i // 4, 4), "col": lax.rem(i, 4)},
            device_id_type=MESH,
        )
        return carry

    lax.fori_loop(0, 12, greet_rows, 0)

    loads[0].wait()
    loads[1].wait()
    for bb in range(8):
        proj[x, 16 * bb : 16 * bb + 16, :] = dot(snap[16 * bb : 16 * bb + 16, :], fi[bb], 1, 0)
    pl.semaphore_wait(barrier, 43)

    def row_exchange(buf, s, r):
        for i in (2, 1, 3):
            cp = rdma(buf.at[x], buf.at[x], s.at[i], r.at[i], at(mod4(x + i), y, z, k))
            cp.start()
            pending.append(cp)

    def row_collect(buf, s, r):
        for i in (1, 3, 2):
            frm = mod4(x - i)
            rdma(buf.at[frm], buf.at[frm], s.at[i], r.at[i], at(frm, y, z, k)).wait_recv()
        return (buf[0] + buf[1]) + (buf[2] + buf[3])

    row_exchange(proj, p_s, p_r)
    def loop_wait(send, n):
        def one(i, carry):
            send(i).wait_send()
            return carry

        late.append(lambda: lax.fori_loop(1, n, one, 0))

    loads[2].wait()
    projected = row_collect(proj, p_s, p_r).astype(BF16)
    here = z * 4 + y
    for bb in range(8):
        lifted = dot(projected[16 * bb : 16 * bb + 16, :], fo[bb], 1, 1)
        full[here, 16 * bb : 16 * bb + 16, :] = (
            snap[16 * bb : 16 * bb + 16, :].astype(F32) + lifted
        ).astype(BF16)

    is_source = zl == x // 2
    own_ci = lax.rem(x, 2)

    def slab_send(i):
        to = lax.rem(b + i, 8)
        return rdma(
            full.at[here, :, pl.ds(pl.multiple_of(to * 128, 128), 128)], slab.at[own_ci, here], a_s.at[i],
            a_r.at[here], {"bin": to, "row": x, "col": (x // 2) * 2 + k},
        )

    def start_slab(i, carry):
        slab_send(i).start()
        return carry

    lax.fori_loop(1, 8, start_slab, 0)
    loop_wait(slab_send, 8)
    slab_local = pltpu.make_async_copy(
        full.at[here, :, pl.ds(pl.multiple_of(b * 128, 128), 128)], slab.at[own_ci, here], l_sem.at[0]
    )

    @pl.when(is_source)
    def _():
        slab_local.start()

    @pl.when(jnp.logical_not(is_source))
    def _():
        slab_send(0).start()

    def finish_slab():
        @pl.when(jnp.logical_not(is_source))
        def _():
            slab_send(0).wait_send()

    late.append(finish_slab)

    def block_of(half, u, v):
        return (v * 4 + u) if half == 0 else (u * 4 + v)

    def dev_of(half, u, v):
        return at(x, u, v, k) if half == 0 else at(x, v, u, k)

    def ring(half):
        return (y, z) if half == 0 else (z, y)

    def gcopy(half, event, u, v, lo, rows, tu, tv):
        blk = full.at[block_of(half, u, v), pl.ds(64 * half + lo, rows)]
        e = 20 * half + event
        return rdma(blk, blk, g_s.at[e], g_r.at[e], dev_of(half, tu, tv))

    def gsend(*args):
        cp = gcopy(*args)
        cp.start()
        pending.append(cp)

    def gwait(half, event, u, v, lo, rows):
        gcopy(half, event, u, v, lo, rows, mod4(ring(half)[0] + 1), v).wait_recv()

    def second_send(half, t):
        u, v = ring(half)
        w = mod4(u + (0, -1, 1, 2)[t])
        gsend(half, 4 + 4 * t, w, v, 0, 64, u, mod4(v + 1))
        gsend(half, 5 + 4 * t, w, v, 0, 64, u, mod4(v - 1))

    def second_forward(half, t):
        u, v = ring(half)
        w = mod4(u + (0, -1, 1, 2)[t])
        gwait(half, 4 + 4 * t, w, mod4(v - 1), 0, 64)
        gsend(half, 6 + 4 * t, w, mod4(v - 1), 0, 32, u, mod4(v + 1))
        gwait(half, 5 + 4 * t, w, mod4(v + 1), 0, 64)
        gsend(half, 7 + 4 * t, w, mod4(v + 1), 32, 32, u, mod4(v - 1))

    def second_last(half, t):
        u, v = ring(half)
        w = mod4(u + (0, -1, 1, 2)[t])
        gwait(half, 6 + 4 * t, w, mod4(v + 2), 0, 32)
        gwait(half, 7 + 4 * t, w, mod4(v + 2), 32, 32)

    for half in (0, 1):
        u, v = ring(half)
        gsend(half, 0, u, v, 0, 64, mod4(u + 1), v)
        gsend(half, 1, u, v, 0, 64, mod4(u - 1), v)
    for half in (0, 1):
        second_send(half, 0)
    for half in (0, 1):
        u, v = ring(half)
        gwait(half, 0, mod4(u - 1), v, 0, 64)
        gsend(half, 2, mod4(u - 1), v, 0, 32, mod4(u + 1), v)
        gwait(half, 1, mod4(u + 1), v, 0, 64)
        gsend(half, 3, mod4(u + 1), v, 32, 32, mod4(u - 1), v)
        second_send(half, 1)
        second_send(half, 2)

    def spread(ci, g, n, device):
        blk = slab.at[ci, pl.ds(4 * g, 4)]
        return rdma(blk, blk, x_s.at[ci, g, n], x_r.at[ci, g], device)

    right, left = at(mod4(x + 1), y, z, k), at(mod4(x - 1), y, z, k)

    @pl.when(is_source)
    def _():
        slab_local.wait()

        def arrived(i, carry):
            frm = lax.rem(here + i, 16)
            rdma(
                slab.at[own_ci, frm], slab.at[own_ci, frm], a_s.at[0], a_r.at[frm],
                at(x, lax.rem(frm, 4), frm // 4, k),
            ).wait_recv()
            return carry

        lax.fori_loop(1, 16, arrived, 0)
        for g in range(4):
            spread(own_ci, g, 0, right).start()
            spread(own_ci, g, 1, left).start()

    def spread_roles(forward):
        for ci in (0, 1):
            d = mod4(x - (2 * zl + ci))
            passes_on = d == (3 if ci == 0 else 1)
            yield ci, (passes_on if forward else (d != 0) & jnp.logical_not(passes_on))

    def spread_step(g):
        for ci, passes_on in spread_roles(True):

            @pl.when(passes_on)
            def _():
                spread(ci, g, 0, right).wait_recv()
                spread(ci, g, 0, left if ci == 0 else right).start()

    def spread_last():
        for ci, receives in spread_roles(False):

            @pl.when(receives)
            def _():
                for g in range(4):
                    spread(ci, g, 0, right).wait_recv()

    def finish_spread():
        @pl.when(is_source)
        def _():
            for g in range(4):
                spread(own_ci, g, 0, right).wait_send()
                spread(own_ci, g, 1, left).wait_send()

        for ci, passes_on in spread_roles(True):

            @pl.when(passes_on)
            def _():
                for g in range(4):
                    spread(ci, g, 0, left if ci == 0 else right).wait_send()

    late.append(finish_spread)

    for half in (0, 1):
        second_forward(half, 0)
    for half in (0, 1):
        u, v = ring(half)
        gwait(half, 2, mod4(u + 2), v, 0, 32)
        gwait(half, 3, mod4(u + 2), v, 32, 32)
        second_send(half, 3)
    spread_step(0)
    for half in (0, 1):
        second_forward(half, 1)
        second_forward(half, 2)
    spread_step(1)
    spread_step(2)
    for half in (0, 1):
        second_forward(half, 3)
    spread_step(3)
    for half in (0, 1):
        for t in range(4):
            second_last(half, t)

    spread_last()

    sib_sends = []
    lhs = jnp.concatenate([slab[0].reshape(2048, 128).T, slab[1].reshape(2048, 128).T], axis=0)
    for n in range(4):
        acc[n] = dot(lhs, full[:, :, 256 * n : 256 * n + 256].reshape(2048, 256), 1, 0)
        cp = rdma(
            acc.at[n, pl.ds(pl.multiple_of((1 - k) * 128, 128), 128)], sibc.at[n], c_s.at[n], c_r.at[n], sibling
        )
        cp.start()
        sib_sends.append(cp)
        pending.append(cp)
    scaling = 1.0 / 4096
    mine = pl.ds(pl.multiple_of(k * 128, 128), 128)
    for n in range(4):
        sib_sends[n].wait_recv()
        total = (acc[n, mine] + sibc[n]) * scaling
        piece[:, 256 * n : 256 * n + 256] = total
        cov_ref[b, :, 256 * n : 256 * n + 256] = total.astype(BF16)

    def csend(event, blk_b, lo, rows, device):
        blk = cov_ref.at[blk_b, pl.ds(lo, rows)]
        cp = rdma(blk, blk, v_s.at[event], v_r.at[event], device)
        cp.start()
        pending.append(cp)

    def cwait(event, blk_b, lo, rows):
        blk = cov_ref.at[blk_b, pl.ds(lo, rows)]
        rdma(blk, blk, v_s.at[event], v_r.at[event], sibling).wait_recv()

    yup, ydn = at(x, mod4(y + 1), z, k), at(x, mod4(y - 1), z, k)
    zfar = at(x, y, mod4(z + 2), k)
    yu, yd, yo = mod4(y + 1), mod4(y - 1), mod4(y + 2)
    far = 4 * (1 - zh)
    near = 4 * zh

    loads[3].wait()
    img[x] = dot(piece[...], x0[...], 1, 0, HI)
    row_exchange(img, i_s, i_r)
    csend(2, b, 0, 128, zfar)
    csend(0, b, 0, 128, yup)
    csend(1, b, 0, 128, ydn)
    image = row_collect(img, i_s, i_r)

    gpart[...] = dot(image.T, image, 1, 0, HI)
    gsib_send = rdma(
        gpart.at[pl.ds(pl.multiple_of(32 * x + 16 * (1 - k), 16), 16)], gsib, gs_s.at[0], gs_r.at[0], sibling
    )
    gsib_send.start()
    pending.append(gsib_send)

    part[...] = dot(piece[...].T, image, 1, 0, HI).reshape(2, 2, 256, 128)
    sibp_sends = []
    for h in (0, 1):
        cp = rdma(part.at[h, 1 - k], sibp.at[h], q_s.at[h], q_r.at[h], sibling)
        cp.start()
        sibp_sends.append(cp)
        pending.append(cp)

    gsib_send.wait_recv()
    gown[...] = gpart[pl.ds(pl.multiple_of(32 * x + 16 * k, 16), 16), :] + gsib[...]
    gscat[here] = gown[...]

    def plane_peer(i):
        other = lax.rem(here + i, 16)
        return at(x, lax.rem(other, 4), other // 4, k)

    def gram_send(i):
        return rdma(gown, gscat.at[here], ga_s.at[0, i], ga_r.at[0, i], plane_peer(i))

    def gram_start(i, carry):
        gram_send(i).start()
        return carry

    lax.fori_loop(1, 16, gram_start, 0)
    loop_wait(gram_send, 16)

    for h in (0, 1):
        sibp_sends[h].wait_recv()
        sibp[h] = sibp[h] + part[h, k]

    def scat_send(i):
        other = lax.rem(here + i, 16)
        oz = other // 4
        ob = (oz // 2) * 4 + lax.rem(other, 4)
        return rdma(
            sibp.at[lax.rem(oz, 2), pl.ds(pl.multiple_of(32 * ob, 32), 32)], scat.at[here], r_s.at[i], r_r.at[i],
            plane_peer(i),
        )

    def scat_start(i, carry):
        scat_send(i).start()
        return carry

    lax.fori_loop(1, 16, scat_start, 0)
    loop_wait(scat_send, 16)
    scat[here] = sibp[zl, pl.ds(pl.multiple_of(32 * b, 32), 32)]

    cwait(0, near + yd, 0, 128)
    csend(3, near + yd, 0, 64, yup)
    cwait(1, near + yu, 0, 128)
    csend(4, near + yu, 64, 64, ydn)

    def gram_arrived(i, carry):
        frm = lax.rem(here + 16 - i, 16)
        rdma(gown, gscat.at[frm], ga_s.at[0, i], ga_r.at[0, i], plane_peer(i)).wait_recv()
        return carry

    lax.fori_loop(1, 16, gram_arrived, 0)

    def add_slots(ref, n):
        total = ref[0]
        for i in range(1, n):
            total = total + ref[i]
        return total

    gslice = x * 2 + k
    gram[pl.ds(pl.multiple_of(16 * gslice, 16), 16), :] = add_slots(gscat, 16)

    def gram_share(buf, i, first):
        if first:
            own = gslice
            other = lax.rem(own + i, 8)
            device = at(other // 2, y, z, lax.rem(other, 2))
        else:
            own = b
            other = lax.rem(own + i, 8)
            device = {"bin": other, "row": x, "col": c}
        n = 0 if first else 1
        blk = buf.at[pl.ds(pl.multiple_of(16 * own, 16), 16)]
        return rdma(blk, blk, gb_s.at[n, i], gb_r.at[n, i], device)

    def share_wait(buf, i, first):
        own = gslice if first else b
        frm = lax.rem(own + 8 - i, 8)
        n = 0 if first else 1
        blk = buf.at[pl.ds(pl.multiple_of(16 * frm, 16), 16)]
        rdma(blk, blk, gb_s.at[n, i], gb_r.at[n, i], sibling).wait_recv()

    for i in range(1, 8):
        gram_share(gram, i, True).start()
        pending.append(gram_share(gram, i, True))

    def scat_arrived(i, carry):
        frm = lax.rem(here + 16 - i, 16)
        rdma(scat.at[frm], scat.at[frm], r_s.at[i], r_r.at[i], plane_peer(i)).wait_recv()
        return carry

    lax.fori_loop(1, 16, scat_arrived, 0)
    zall[pl.ds(pl.multiple_of(32 * b, 32), 32), :] = add_slots(scat, 16)

    def bin_share(i):
        blk = zall.at[pl.ds(pl.multiple_of(32 * b, 32), 32)]
        return rdma(blk, blk, z_s.at[i], z_r.at[i], {"bin": lax.rem(b + i, 8), "row": x, "col": c})

    for i in range(1, 8):
        bin_share(i).start()
        pending.append(bin_share(i))

    cwait(2, far + y, 0, 128)
    csend(5, far + y, 0, 128, yup)
    csend(6, far + y, 0, 128, ydn)

    for i in range(1, 8):
        share_wait(gram, i, True)
    inverse = inverse_factor([gram[8 * i : 8 * i + 8, :] for i in range(16)])
    for i in range(1, 8):
        frm = lax.rem(b + 8 - i, 8)
        blk = zall.at[pl.ds(pl.multiple_of(32 * frm, 32), 32)]
        rdma(blk, blk, z_s.at[i], z_r.at[i], sibling).wait_recv()
    second = dot(zall[...], inverse, 1, 1, HI)
    basis_ref[...] = second
    gpart2[...] = dot(second.T, second, 1, 0, HI)

    q = x * 4 + c
    gslice_rows = pl.ds(pl.multiple_of(16 * b, 16), 16)
    gscat2[q] = gpart2[gslice_rows, :]

    def mesh_peer(i):
        other = lax.rem(q + i, 16)
        return {"bin": b, "row": other // 4, "col": lax.rem(other, 4)}

    def gram2_send(i):
        oq = q
        return rdma(gscat2.at[oq], gscat2.at[oq], ga_s.at[1, i], ga_r.at[1, i], mesh_peer(i))

    def gram2_start(i, carry):
        gram2_send(i).start()
        return carry

    lax.fori_loop(1, 16, gram2_start, 0)
    loop_wait(gram2_send, 16)

    cwait(5, far + yd, 0, 128)
    csend(7, far + yd, 0, 64, yup)
    cwait(6, far + yu, 0, 128)
    csend(8, far + yu, 64, 64, ydn)

    def gram2_arrived(i, carry):
        frm = lax.rem(q + 16 - i, 16)
        rdma(gscat2.at[frm], gscat2.at[frm], ga_s.at[1, i], ga_r.at[1, i], mesh_peer(i)).wait_recv()
        return carry

    lax.fori_loop(1, 16, gram2_arrived, 0)
    gram2[gslice_rows, :] = add_slots(gscat2, 16)
    for i in range(1, 8):
        gram_share(gram2, i, False).start()
        pending.append(gram_share(gram2, i, False))
    for i in range(1, 8):
        share_wait(gram2, i, False)
    basis_ref[...] = apply_factor(gram2, basis_ref[...]) * 64.0

    cwait(3, near + yo, 0, 64)
    cwait(4, near + yo, 64, 64)
    cwait(7, far + yo, 0, 64)
    cwait(8, far + yo, 64, 64)

    for cp in pending:
        cp.wait_send()
    for finish in late:
        finish()


def shards(snapshots, focus_in, focus_out, start_basis):
    snaps = snapshots.transpose(1, 2, 0).reshape(128, 1024)
    dma = pltpu.SemaphoreType.DMA
    anywhere = pl.BlockSpec(memory_space=pl.ANY)
    in_vmem = pl.BlockSpec(memory_space=pltpu.VMEM)
    pieces, basis_out = pl.pallas_call(
        kernel,
        out_shape=(
            jax.ShapeDtypeStruct((8, 128, 1024), BF16),
            jax.ShapeDtypeStruct((256, 128), F32),
        ),
        in_specs=[pl.BlockSpec(memory_space=pltpu.HBM)] * 4,
        out_specs=(in_vmem, in_vmem),
        scratch_shapes=[
            pltpu.VMEM((128, 1024), BF16),
            pltpu.VMEM((8, 1024, 128), BF16),
            pltpu.VMEM((8, 1024, 128), BF16),
            pltpu.VMEM((1024, 128), F32),
            pltpu.VMEM((4, 128, 128), F32),
            pltpu.VMEM((16, 128, 1024), BF16),
            pltpu.VMEM((2, 16, 128, 128), BF16),
            pltpu.VMEM((4, 256, 256), F32),
            pltpu.VMEM((4, 128, 256), F32),
            pltpu.VMEM((128, 1024), F32),
            pltpu.VMEM((4, 128, 128), F32),
            pltpu.VMEM((2, 2, 256, 128), F32),
            pltpu.VMEM((2, 256, 128), F32),
            pltpu.VMEM((16, 32, 128), F32),
            pltpu.VMEM((256, 128), F32),
            pltpu.VMEM((128, 128), F32),
            pltpu.VMEM((16, 128), F32),
            pltpu.VMEM((16, 128), F32),
            pltpu.VMEM((16, 16, 128), F32),
            pltpu.VMEM((128, 128), F32),
            pltpu.VMEM((128, 128), F32),
            pltpu.VMEM((16, 16, 128), F32),
            pltpu.VMEM((128, 128), F32),
            dma((4,)),
            dma((4,)), dma((4,)),
            dma((40,)), dma((40,)),
            dma((8,)), dma((16,)),
            dma((2, 4, 2)), dma((2, 4)),
            dma((4,)), dma((4,)),
            dma((9,)), dma((9,)),
            dma((4,)), dma((4,)),
            dma((2,)), dma((2,)),
            dma((16,)), dma((16,)),
            dma((8,)), dma((8,)),
            dma((1,)), dma((1,)),
            dma((2, 16)), dma((2, 16)),
            dma((2, 8)), dma((2, 8)),
            dma((1,)),
        ],
        compiler_params=pltpu.CompilerParams(
            collective_id=0, has_side_effects=True, vmem_limit_bytes=60 * 2**20
        ),
    )(snaps, focus_in, focus_out, start_basis)
    return pieces.reshape(1024, 1024).astype(F32), basis_out


def solution(mesh):
    in_specs = (P("row", "bin", "col"), P("bin", "row", None), P("bin", "row", None), P())
    out_specs = (P("col", "row"), P(("row", "col"), None))
    return jax.shard_map(shards, mesh=mesh, in_specs=in_specs, out_specs=out_specs, check_vma=False)
```

```python
import functools
import math

import jax
import jax.numpy as jnp
from jax import lax
from jax.experimental import pallas as pl
from jax.experimental.pallas import tpu as pltpu
from jax.sharding import PartitionSpec as P

MESH = pl.DeviceIdType.MESH
HI = lax.Precision.HIGHEST
F32 = jnp.float32
BF16 = jnp.bfloat16


def mod4(v):
    return lax.rem(v + 4, 4)


def dot(a, b, ca, cb, precision=None):
    return lax.dot_general(a, b, (((ca,), (cb,)), ((), ())), precision=precision, preferred_element_type=F32)


def dot_split(a, b, ca, cb):
    high = b.astype(BF16)
    low = (b - high.astype(F32)).astype(BF16)
    return dot(a, high, ca, cb) + dot(a, low, ca, cb)


def inverse_factor(gram):
    lane = lax.broadcasted_iota(jnp.int32, (8, 128), 1)
    sub = lax.broadcasted_iota(jnp.int32, (8, 128), 0)

    def over_lanes(tile, j):
        return jnp.broadcast_to(tile[:, j : j + 1], (8, 128))

    def over_rows(tile, i):
        return jnp.broadcast_to(tile[i : i + 1, :], (8, 128))

    tiles = list(gram)
    done = []
    for p in range(16):
        first = 8 * p
        now = tiles[p]
        cols = [over_lanes(now, first + e) for e in range(8)]
        left = [[over_rows(cols[e], i) for e in range(i + 1)] for i in range(8)]
        low = [[None] * 8 for _ in range(8)]
        inv = [None] * 8
        for e in range(8):
            inv[e] = 1.0 / left[e][e]
            for i in range(e + 1, 8):
                low[i][e] = left[i][e] * inv[e]
            for i in range(e + 1, 8):
                for f in range(e + 1, i + 1):
                    left[i][f] = left[i][f] - low[i][e] * left[f][e]
        in_panel = (lane >= first) & (lane < first + 8)
        upper = []
        for i in range(8):
            row = jnp.where(in_panel, jnp.where(lane == first + i, 1.0, 0.0), over_rows(now, i))
            for e in range(i):
                row = row - low[i][e] * upper[e]
            upper.append(row)
        tile, scale = upper[0], inv[0]
        for i in range(1, 8):
            tile = jnp.where(sub == i, upper[i], tile)
            scale = jnp.where(sub == i, inv[i], scale)
        done.append(jnp.where(lane <= sub + first, tile, 0.0) * jnp.sqrt(scale))
        scaled = [upper[e] * inv[e] for e in range(8)]
        for q in range(p + 1, 16):
            total = jnp.where(in_panel, 0.0, tiles[q])
            lower = []
            for e in range(8):
                col = over_lanes(tiles[q], first + e)
                for f in range(e):
                    col = col - lower[f] * low[e][f]
                lower.append(col)
                total = total - col * scaled[e]
            tiles[q] = total
    return jnp.concatenate(done, axis=0)


def apply_factor(gram, block):
    return dot(block, inverse_factor([gram[8 * i : 8 * i + 8, :] for i in range(16)]), 1, 1, HI)


def kernel(
    snap_hbm, fi_hbm, fo_hbm, x0_hbm, cov_ref, basis_ref,
    snap, fi, fo, x0, proj, full, slab, acc, sibc, piece, img, part, sibp, scat, zall, xr, img2, image2, last,
    gpart, gsib, gown, gscat, gram, gpart2, gscat2, gram2, in_sem,
    p_s, p_r, g_s, g_r, a_s, a_r, x_s, x_r, c_s, c_r, v_s, v_r, i_s, i_r, q_s, q_r, r_s, r_r, z_s, z_r,
    y_s, y_r, j_s, j_r, o_s, o_r, gs_s, gs_r, ga_s, ga_r, gb_s, gb_r, l_sem,
):
    b = lax.axis_index("bin")
    x = lax.axis_index("row")
    c = lax.axis_index("col")
    k = lax.rem(c, 2)
    zl = c // 2
    y = lax.rem(b, 4)
    zh = b // 4
    z = zh * 2 + zl

    def at(x_, y_, z_, k_):
        return {"bin": (z_ // 2) * 4 + y_, "row": x_, "col": lax.rem(z_, 2) * 2 + k_}

    sibling = at(x, y, z, 1 - k)
    pending, late = [], []

    def rdma(src, dst, s, r, device):
        return pltpu.make_async_remote_copy(
            src_ref=src, dst_ref=dst, send_sem=s, recv_sem=r, device_id=device, device_id_type=MESH
        )

    loads = [
        pltpu.make_async_copy(snap_hbm, snap, in_sem.at[0]),
        pltpu.make_async_copy(fi_hbm, fi, in_sem.at[1]),
        pltpu.make_async_copy(fo_hbm, fo, in_sem.at[2]),
        pltpu.make_async_copy(x0_hbm.at[pl.ds(pl.multiple_of(x * 1024, 1024), 1024)], x0, in_sem.at[3]),
    ]
    for load in loads:
        load.start()

    barrier = pltpu.get_barrier_semaphore()
    place = b * 4 + c

    def greet(i, carry):
        other = lax.rem(place + i, 32)
        pl.semaphore_signal(
            barrier, inc=1, device_id={"bin": other // 4, "row": x, "col": lax.rem(other, 4)}, device_id_type=MESH
        )
        return carry

    lax.fori_loop(1, 32, greet, 0)

    def greet_rows(i, carry):
        pl.semaphore_signal(
            barrier, inc=1, device_id={"bin": b, "row": lax.rem(x + 1 + i // 4, 4), "col": lax.rem(i, 4)},
            device_id_type=MESH,
        )
        return carry

    lax.fori_loop(0, 12, greet_rows, 0)

    loads[0].wait()
    loads[1].wait()
    for bb in range(8):
        proj[x, 16 * bb : 16 * bb + 16, :] = dot(snap[16 * bb : 16 * bb + 16, :], fi[bb], 1, 0)
    pl.semaphore_wait(barrier, 43)

    def row_exchange(buf, s, r):
        for i in (2, 1, 3):
            cp = rdma(buf.at[x], buf.at[x], s.at[i], r.at[i], at(mod4(x + i), y, z, k))
            cp.start()
            pending.append(cp)

    def row_collect(buf, s, r):
        for i in (1, 3, 2):
            frm = mod4(x - i)
            rdma(buf.at[frm], buf.at[frm], s.at[i], r.at[i], at(frm, y, z, k)).wait_recv()
        return (buf[0] + buf[1]) + (buf[2] + buf[3])

    row_exchange(proj, p_s, p_r)
    def loop_wait(send, n):
        def one(i, carry):
            send(i).wait_send()
            return carry

        late.append(lambda: lax.fori_loop(1, n, one, 0))

    loads[2].wait()
    projected = row_collect(proj, p_s, p_r).astype(BF16)
    here = z * 4 + y
    for bb in range(8):
        lifted = dot(projected[16 * bb : 16 * bb + 16, :], fo[bb], 1, 1)
        full[here, 16 * bb : 16 * bb + 16, :] = (
            snap[16 * bb : 16 * bb + 16, :].astype(F32) + lifted
        ).astype(BF16)

    is_source = zl == x // 2
    own_ci = lax.rem(x, 2)

    def slab_send(i):
        to = lax.rem(b + i, 8)
        return rdma(
            full.at[here, :, pl.ds(pl.multiple_of(to * 128, 128), 128)], slab.at[own_ci, here], a_s.at[i],
            a_r.at[here], {"bin": to, "row": x, "col": (x // 2) * 2 + k},
        )

    def start_slab(i, carry):
        slab_send(i).start()
        return carry

    lax.fori_loop(1, 8, start_slab, 0)
    loop_wait(slab_send, 8)
    slab_local = pltpu.make_async_copy(
        full.at[here, :, pl.ds(pl.multiple_of(b * 128, 128), 128)], slab.at[own_ci, here], l_sem.at[0]
    )

    @pl.when(is_source)
    def _():
        slab_local.start()

    @pl.when(jnp.logical_not(is_source))
    def _():
        slab_send(0).start()

    def finish_slab():
        @pl.when(jnp.logical_not(is_source))
        def _():
            slab_send(0).wait_send()

    late.append(finish_slab)

    def block_of(half, u, v):
        return (v * 4 + u) if half == 0 else (u * 4 + v)

    def dev_of(half, u, v):
        return at(x, u, v, k) if half == 0 else at(x, v, u, k)

    def ring(half):
        return (y, z) if half == 0 else (z, y)

    def gcopy(half, event, u, v, lo, rows, tu, tv):
        blk = full.at[block_of(half, u, v), pl.ds(64 * half + lo, rows)]
        e = 20 * half + event
        return rdma(blk, blk, g_s.at[e], g_r.at[e], dev_of(half, tu, tv))

    def gsend(*args):
        cp = gcopy(*args)
        cp.start()
        pending.append(cp)

    def gwait(half, event, u, v, lo, rows):
        gcopy(half, event, u, v, lo, rows, mod4(ring(half)[0] + 1), v).wait_recv()

    def second_send(half, t):
        u, v = ring(half)
        w = mod4(u + (0, -1, 1, 2)[t])
        gsend(half, 4 + 4 * t, w, v, 0, 64, u, mod4(v + 1))
        gsend(half, 5 + 4 * t, w, v, 0, 64, u, mod4(v - 1))

    def second_forward(half, t):
        u, v = ring(half)
        w = mod4(u + (0, -1, 1, 2)[t])
        gwait(half, 4 + 4 * t, w, mod4(v - 1), 0, 64)
        gsend(half, 6 + 4 * t, w, mod4(v - 1), 0, 32, u, mod4(v + 1))
        gwait(half, 5 + 4 * t, w, mod4(v + 1), 0, 64)
        gsend(half, 7 + 4 * t, w, mod4(v + 1), 32, 32, u, mod4(v - 1))

    def second_last(half, t):
        u, v = ring(half)
        w = mod4(u + (0, -1, 1, 2)[t])
        gwait(half, 6 + 4 * t, w, mod4(v + 2), 0, 32)
        gwait(half, 7 + 4 * t, w, mod4(v + 2), 32, 32)

    for half in (0, 1):
        u, v = ring(half)
        gsend(half, 0, u, v, 0, 64, mod4(u + 1), v)
        gsend(half, 1, u, v, 0, 64, mod4(u - 1), v)
    for half in (0, 1):
        second_send(half, 0)

    loads[3].wait()
    img[x] = dot_split(full[here], x0[...], 1, 0)
    row_exchange(img, i_s, i_r)

    for half in (0, 1):
        u, v = ring(half)
        gwait(half, 0, mod4(u - 1), v, 0, 64)
        gsend(half, 2, mod4(u - 1), v, 0, 32, mod4(u + 1), v)
        gwait(half, 1, mod4(u + 1), v, 0, 64)
        gsend(half, 3, mod4(u + 1), v, 32, 32, mod4(u - 1), v)
        second_send(half, 1)
        second_send(half, 2)

    weights = row_collect(img, i_s, i_r)
    part[...] = (dot_split(full[here].T, weights, 1, 0) * (1.0 / 4096)).reshape(2, 2, 256, 128)
    sibp_sends = []
    for h in (0, 1):
        cp = rdma(part.at[h, 1 - k], sibp.at[h], q_s.at[h], q_r.at[h], sibling)
        cp.start()
        sibp_sends.append(cp)
        pending.append(cp)

    def spread(ci, g, n, device):
        blk = slab.at[ci, pl.ds(4 * g, 4)]
        return rdma(blk, blk, x_s.at[ci, g, n], x_r.at[ci, g], device)

    right, left = at(mod4(x + 1), y, z, k), at(mod4(x - 1), y, z, k)

    @pl.when(is_source)
    def _():
        slab_local.wait()

        def arrived(i, carry):
            frm = lax.rem(here + i, 16)
            rdma(
                slab.at[own_ci, frm], slab.at[own_ci, frm], a_s.at[0], a_r.at[frm],
                at(x, lax.rem(frm, 4), frm // 4, k),
            ).wait_recv()
            return carry

        lax.fori_loop(1, 16, arrived, 0)
        for g in range(4):
            spread(own_ci, g, 0, right).start()
            spread(own_ci, g, 1, left).start()

    def spread_roles(forward):
        for ci in (0, 1):
            d = mod4(x - (2 * zl + ci))
            passes_on = d == (3 if ci == 0 else 1)
            yield ci, (passes_on if forward else (d != 0) & jnp.logical_not(passes_on))

    def spread_step(g):
        for ci, passes_on in spread_roles(True):

            @pl.when(passes_on)
            def _():
                spread(ci, g, 0, right).wait_recv()
                spread(ci, g, 0, left if ci == 0 else right).start()

    def spread_last():
        for ci, receives in spread_roles(False):

            @pl.when(receives)
            def _():
                for g in range(4):
                    spread(ci, g, 0, right).wait_recv()

    def finish_spread():
        @pl.when(is_source)
        def _():
            for g in range(4):
                spread(own_ci, g, 0, right).wait_send()
                spread(own_ci, g, 1, left).wait_send()

        for ci, passes_on in spread_roles(True):

            @pl.when(passes_on)
            def _():
                for g in range(4):
                    spread(ci, g, 0, left if ci == 0 else right).wait_send()

    late.append(finish_spread)

    for half in (0, 1):
        second_forward(half, 0)

    def plane_peer(i):
        other = lax.rem(here + i, 16)
        return at(x, lax.rem(other, 4), other // 4, k)

    def add_slots(ref, n):
        total = ref[0]
        for i in range(1, n):
            total = total + ref[i]
        return total

    for h in (0, 1):
        sibp_sends[h].wait_recv()
        sibp[h] = sibp[h] + part[h, k]

    def scat_send(i):
        other = lax.rem(here + i, 16)
        oz = other // 4
        ob = (oz // 2) * 4 + lax.rem(other, 4)
        return rdma(
            sibp.at[lax.rem(oz, 2), pl.ds(pl.multiple_of(32 * ob, 32), 32)], scat.at[here], r_s.at[i], r_r.at[i],
            plane_peer(i),
        )

    def scat_start(i, carry):
        scat_send(i).start()
        return carry

    lax.fori_loop(1, 16, scat_start, 0)
    loop_wait(scat_send, 16)
    scat[here] = sibp[zl, pl.ds(pl.multiple_of(32 * b, 32), 32)]

    for half in (0, 1):
        u, v = ring(half)
        gwait(half, 2, mod4(u + 2), v, 0, 32)
        gwait(half, 3, mod4(u + 2), v, 32, 32)
        second_send(half, 3)
    spread_step(0)
    for half in (0, 1):
        second_forward(half, 1)

    def scat_arrived(i, carry):
        frm = lax.rem(here + 16 - i, 16)
        rdma(scat.at[frm], scat.at[frm], r_s.at[i], r_r.at[i], plane_peer(i)).wait_recv()
        return carry

    lax.fori_loop(1, 16, scat_arrived, 0)
    zall[pl.ds(pl.multiple_of(32 * b, 32), 32), :] = add_slots(scat, 16)

    def bin_share(i):
        blk = zall.at[pl.ds(pl.multiple_of(32 * b, 32), 32)]
        return rdma(blk, blk, z_s.at[i], z_r.at[i], {"bin": lax.rem(b + i, 8), "row": x, "col": c})

    for i in range(1, 8):
        bin_share(i).start()
        pending.append(bin_share(i))

    for half in (0, 1):
        second_forward(half, 2)
    spread_step(1)
    spread_step(2)

    for i in range(1, 8):
        frm = lax.rem(b + 8 - i, 8)
        blk = zall.at[pl.ds(pl.multiple_of(32 * frm, 32), 32)]
        rdma(blk, blk, z_s.at[i], z_r.at[i], sibling).wait_recv()

    def col_share(i):
        return rdma(zall, xr.at[c], y_s.at[i], y_r.at[i], {"bin": b, "row": x, "col": mod4(c + i)})

    for i in (2, 1, 3):
        col_share(i).start()
        pending.append(col_share(i))
    first = zall[...]
    xr[c] = first
    gpart[...] = dot(first.T, first, 1, 0, HI)
    q = x * 4 + c
    bin_slice = pl.ds(pl.multiple_of(16 * b, 16), 16)
    gscat2[q] = gpart[bin_slice, :]

    def mesh_peer(i):
        other = lax.rem(q + i, 16)
        return {"bin": b, "row": other // 4, "col": lax.rem(other, 4)}

    def gram_send(i):
        return rdma(gscat2.at[q], gscat2.at[q], ga_s.at[0, i], ga_r.at[0, i], mesh_peer(i))

    def gram_start(i, carry):
        gram_send(i).start()
        return carry

    lax.fori_loop(1, 16, gram_start, 0)
    loop_wait(gram_send, 16)

    for half in (0, 1):
        second_forward(half, 3)
    spread_step(3)

    def gram_share(buf, i, n):
        if n == 0:
            own = b
            other = lax.rem(own + i, 8)
            device = {"bin": other, "row": x, "col": c}
        else:
            own = x * 2 + k
            other = lax.rem(own + i, 8)
            device = at(other // 2, y, z, lax.rem(other, 2))
        blk = buf.at[pl.ds(pl.multiple_of(16 * own, 16), 16)]
        return rdma(blk, blk, gb_s.at[n, i], gb_r.at[n, i], device)

    def share_start(buf, n):
        for i in range(1, 8):
            gram_share(buf, i, n).start()
            pending.append(gram_share(buf, i, n))

    def share_wait(buf, n):
        own = b if n == 0 else x * 2 + k
        for i in range(1, 8):
            frm = lax.rem(own + 8 - i, 8)
            blk = buf.at[pl.ds(pl.multiple_of(16 * frm, 16), 16)]
            rdma(blk, blk, gb_s.at[n, i], gb_r.at[n, i], sibling).wait_recv()

    def gram_arrived(i, carry):
        frm = lax.rem(q + 16 - i, 16)
        rdma(gscat2.at[frm], gscat2.at[frm], ga_s.at[0, i], ga_r.at[0, i], mesh_peer(i)).wait_recv()
        return carry

    lax.fori_loop(1, 16, gram_arrived, 0)
    gram[bin_slice, :] = add_slots(gscat2, 16)
    share_start(gram, 0)
    spread_last()

    def stack(places):
        lhs = [
            jnp.concatenate([slab[ci, j, 64 * half : 64 * half + 64, :] for half, j in places], axis=0).T
            for ci in (0, 1)
        ]
        return jnp.concatenate(lhs, axis=0)

    def multiply(places, lhs, n):
        rhs = jnp.concatenate(
            [full[j, 64 * half : 64 * half + 64, 256 * n : 256 * n + 256] for half, j in places], axis=0
        )
        return dot(lhs, rhs, 1, 0)

    early, late_blocks = [], []
    for half in (0, 1):
        u, v = ring(half)
        for i in (0, 1, 3, 2):
            for w in range(4):
                (late_blocks if i == 2 else early).append((half, block_of(half, w, mod4(v + i))))
    lhs = stack(early)
    for n in range(4):
        acc[n] = multiply(early, lhs, n)
    for half in (0, 1):
        for t in range(4):
            second_last(half, t)
    sib_sends = []
    lhs = stack(late_blocks)
    for n in range(4):
        acc[n] = acc[n] + multiply(late_blocks, lhs, n)
        cp = rdma(
            acc.at[n, pl.ds(pl.multiple_of((1 - k) * 128, 128), 128)], sibc.at[n], c_s.at[n], c_r.at[n], sibling
        )
        cp.start()
        sib_sends.append(cp)
        pending.append(cp)
    for i in (1, 2, 3):
        frm = mod4(c - i)
        rdma(zall, xr.at[frm], y_s.at[i], y_r.at[i], sibling).wait_recv()
    scaling = 1.0 / 4096
    mine = pl.ds(pl.multiple_of(k * 128, 128), 128)
    for n in range(4):
        sib_sends[n].wait_recv()
        total = (acc[n, mine] + sibc[n]) * scaling
        piece[:, 256 * n : 256 * n + 256] = total
        cov_ref[b, :, 256 * n : 256 * n + 256] = total.astype(BF16)

    img2[x] = dot(piece[...], xr[...].reshape(1024, 128), 1, 0, HI)
    row_exchange(img2, j_s, j_r)

    def csend(event, blk_b, lo, rows, device):
        blk = cov_ref.at[blk_b, pl.ds(lo, rows)]
        cp = rdma(blk, blk, v_s.at[event], v_r.at[event], device)
        cp.start()
        pending.append(cp)

    def cwait(event, blk_b, lo, rows):
        blk = cov_ref.at[blk_b, pl.ds(lo, rows)]
        rdma(blk, blk, v_s.at[event], v_r.at[event], sibling).wait_recv()

    yup, ydn = at(x, mod4(y + 1), z, k), at(x, mod4(y - 1), z, k)
    zfar = at(x, y, mod4(z + 2), k)
    yu, yd, yo = mod4(y + 1), mod4(y - 1), mod4(y + 2)
    far = 4 * (1 - zh)
    near = 4 * zh
    csend(2, b, 0, 128, zfar)
    csend(0, b, 0, 128, yup)
    csend(1, b, 0, 128, ydn)

    share_wait(gram, 0)
    inverse = inverse_factor([gram[8 * i : 8 * i + 8, :] for i in range(16)])
    second = dot(row_collect(img2, j_s, j_r), inverse, 1, 1, HI)

    gpart2[...] = dot(second.T, second, 1, 0, HI)
    gsib_send = rdma(
        gpart2.at[pl.ds(pl.multiple_of(32 * x + 16 * (1 - k), 16), 16)], gsib, gs_s.at[0], gs_r.at[0], sibling
    )
    gsib_send.start()
    pending.append(gsib_send)

    image2[...] = second
    holder = c == x

    def out_send(i):
        return rdma(
            image2, last.at[lax.rem(b, 2)], o_s.at[i], o_r.at[lax.rem(b, 2)],
            {"bin": lax.rem(b + i, 8), "row": x, "col": b // 2},
        )

    @pl.when(holder)
    def _():
        for i in range(1, 8):
            out_send(i).start()

        @pl.when(b // 2 == c)
        def _():
            last[lax.rem(b, 2)] = second

        @pl.when(b // 2 != c)
        def _():
            out_send(0).start()

    def finish_out():
        @pl.when(holder)
        def _():
            for i in range(1, 8):
                out_send(i).wait_send()

            @pl.when(b // 2 != c)
            def _():
                out_send(0).wait_send()

    late.append(finish_out)

    gsib_send.wait_recv()
    gown[...] = gpart2[pl.ds(pl.multiple_of(32 * x + 16 * k, 16), 16), :] + gsib[...]
    gscat[here] = gown[...]

    def gram2_send(i):
        return rdma(gown, gscat.at[here], ga_s.at[1, i], ga_r.at[1, i], plane_peer(i))

    def gram2_start(i, carry):
        gram2_send(i).start()
        return carry

    lax.fori_loop(1, 16, gram2_start, 0)
    loop_wait(gram2_send, 16)

    cwait(0, near + yd, 0, 128)
    csend(3, near + yd, 0, 64, yup)
    cwait(1, near + yu, 0, 128)
    csend(4, near + yu, 64, 64, ydn)

    def gram2_arrived(i, carry):
        frm = lax.rem(here + 16 - i, 16)
        rdma(gown, gscat.at[frm], ga_s.at[1, i], ga_r.at[1, i], plane_peer(i)).wait_recv()
        return carry

    lax.fori_loop(1, 16, gram2_arrived, 0)
    gram2[pl.ds(pl.multiple_of(32 * x + 16 * k, 16), 16), :] = add_slots(gscat, 16)
    share_start(gram2, 1)

    cwait(2, far + y, 0, 128)
    csend(5, far + y, 0, 128, yup)
    csend(6, far + y, 0, 128, ydn)

    share_wait(gram2, 1)
    inverse = inverse_factor([gram2[8 * i : 8 * i + 8, :] for i in range(16)])

    cwait(5, far + yd, 0, 128)
    csend(7, far + yd, 0, 64, yup)
    cwait(6, far + yu, 0, 128)
    csend(8, far + yu, 64, 64, ydn)

    for h in (0, 1):
        @pl.when(jnp.logical_not((c == x) & (b == 2 * c + h)))
        def _():
            rdma(image2, last.at[h], o_s.at[0], o_r.at[h], sibling).wait_recv()

    basis_ref[...] = dot(last[...].reshape(256, 128), inverse, 1, 1, HI) * 64.0

    cwait(3, near + yo, 0, 64)
    cwait(4, near + yo, 64, 64)
    cwait(7, far + yo, 0, 64)
    cwait(8, far + yo, 64, 64)

    for cp in pending:
        cp.wait_send()
    for finish in late:
        finish()


def shards(snapshots, focus_in, focus_out, start_basis):
    snaps = snapshots.transpose(1, 2, 0).reshape(128, 1024)
    dma = pltpu.SemaphoreType.DMA
    anywhere = pl.BlockSpec(memory_space=pl.ANY)
    in_vmem = pl.BlockSpec(memory_space=pltpu.VMEM)
    pieces, basis_out = pl.pallas_call(
        kernel,
        out_shape=(
            jax.ShapeDtypeStruct((8, 128, 1024), BF16),
            jax.ShapeDtypeStruct((256, 128), F32),
        ),
        in_specs=[pl.BlockSpec(memory_space=pltpu.HBM)] * 4,
        out_specs=(in_vmem, in_vmem),
        scratch_shapes=[
            pltpu.VMEM((128, 1024), BF16),
            pltpu.VMEM((8, 1024, 128), BF16),
            pltpu.VMEM((8, 1024, 128), BF16),
            pltpu.VMEM((1024, 128), F32),
            pltpu.VMEM((4, 128, 128), F32),
            pltpu.VMEM((16, 128, 1024), BF16),
            pltpu.VMEM((2, 16, 128, 128), BF16),
            pltpu.VMEM((4, 256, 256), F32),
            pltpu.VMEM((4, 128, 256), F32),
            pltpu.VMEM((128, 1024), F32),
            pltpu.VMEM((4, 128, 128), F32),
            pltpu.VMEM((2, 2, 256, 128), F32),
            pltpu.VMEM((2, 256, 128), F32),
            pltpu.VMEM((16, 32, 128), F32),
            pltpu.VMEM((256, 128), F32),
            pltpu.VMEM((4, 256, 128), F32),
            pltpu.VMEM((4, 128, 128), F32),
            pltpu.VMEM((128, 128), F32),
            pltpu.VMEM((2, 128, 128), F32),
            pltpu.VMEM((128, 128), F32),
            pltpu.VMEM((16, 128), F32),
            pltpu.VMEM((16, 128), F32),
            pltpu.VMEM((16, 16, 128), F32),
            pltpu.VMEM((128, 128), F32),
            pltpu.VMEM((128, 128), F32),
            pltpu.VMEM((16, 16, 128), F32),
            pltpu.VMEM((128, 128), F32),
            dma((4,)),
            dma((4,)), dma((4,)),
            dma((40,)), dma((40,)),
            dma((8,)), dma((16,)),
            dma((2, 4, 2)), dma((2, 4)),
            dma((4,)), dma((4,)),
            dma((9,)), dma((9,)),
            dma((4,)), dma((4,)),
            dma((2,)), dma((2,)),
            dma((16,)), dma((16,)),
            dma((8,)), dma((8,)),
            dma((4,)), dma((4,)),
            dma((4,)), dma((4,)),
            dma((8,)), dma((2,)),
            dma((1,)), dma((1,)),
            dma((2, 16)), dma((2, 16)),
            dma((2, 8)), dma((2, 8)),
            dma((1,)),
        ],
        compiler_params=pltpu.CompilerParams(
            collective_id=0, has_side_effects=True, vmem_limit_bytes=60 * 2**20
        ),
    )(snaps, focus_in, focus_out, start_basis)
    return pieces.reshape(1024, 1024).astype(F32), basis_out


def solution(mesh):
    in_specs = (P("row", "bin", "col"), P("bin", "row", None), P("bin", "row", None), P())
    out_specs = (P("col", "row"), P(("row", "col"), None))
    return jax.shard_map(shards, mesh=mesh, in_specs=in_specs, out_specs=out_specs, check_vma=False)
```

```python
import functools
import math

import jax
import jax.numpy as jnp
from jax import lax
from jax.experimental import pallas as pl
from jax.experimental.pallas import tpu as pltpu
from jax.sharding import PartitionSpec as P

MESH = pl.DeviceIdType.MESH
HI = lax.Precision.HIGHEST
F32 = jnp.float32
BF16 = jnp.bfloat16


def mod4(v):
    return lax.rem(v + 4, 4)


def dot(a, b, ca, cb, precision=None):
    return lax.dot_general(a, b, (((ca,), (cb,)), ((), ())), precision=precision, preferred_element_type=F32)


def dot_split(a, b, ca, cb):
    high = b.astype(BF16)
    low = (b - high.astype(F32)).astype(BF16)
    return dot(a, high, ca, cb) + dot(a, low, ca, cb)


def inverse_factor(gram):
    lane = lax.broadcasted_iota(jnp.int32, (8, 128), 1)
    sub = lax.broadcasted_iota(jnp.int32, (8, 128), 0)

    def over_lanes(tile, j):
        return jnp.broadcast_to(tile[:, j : j + 1], (8, 128))

    def over_rows(tile, i):
        return jnp.broadcast_to(tile[i : i + 1, :], (8, 128))

    tiles = list(gram)
    done = []
    for p in range(16):
        first = 8 * p
        now = tiles[p]
        cols = [over_lanes(now, first + e) for e in range(8)]
        left = [[over_rows(cols[e], i) for e in range(i + 1)] for i in range(8)]
        low = [[None] * 8 for _ in range(8)]
        inv = [None] * 8
        for e in range(8):
            inv[e] = 1.0 / left[e][e]
            for i in range(e + 1, 8):
                low[i][e] = left[i][e] * inv[e]
            for i in range(e + 1, 8):
                for f in range(e + 1, i + 1):
                    left[i][f] = left[i][f] - low[i][e] * left[f][e]
        in_panel = (lane >= first) & (lane < first + 8)
        upper = []
        for i in range(8):
            row = jnp.where(in_panel, jnp.where(lane == first + i, 1.0, 0.0), over_rows(now, i))
            for e in range(i):
                row = row - low[i][e] * upper[e]
            upper.append(row)
        tile, scale = upper[0], inv[0]
        for i in range(1, 8):
            tile = jnp.where(sub == i, upper[i], tile)
            scale = jnp.where(sub == i, inv[i], scale)
        done.append(jnp.where(lane <= sub + first, tile, 0.0) * jnp.sqrt(scale))
        scaled = [upper[e] * inv[e] for e in range(8)]
        for q in range(p + 1, 16):
            total = jnp.where(in_panel, 0.0, tiles[q])
            lower = []
            for e in range(8):
                col = over_lanes(tiles[q], first + e)
                for f in range(e):
                    col = col - lower[f] * low[e][f]
                lower.append(col)
                total = total - col * scaled[e]
            tiles[q] = total
    return jnp.concatenate(done, axis=0)


def apply_factor(gram, block):
    return dot(block, inverse_factor([gram[8 * i : 8 * i + 8, :] for i in range(16)]), 1, 1, HI)


def kernel(
    snap_hbm, fi_hbm, fo_hbm, x0_hbm, cov_ref, basis_ref,
    snap, fi, fo, x0, proj, full, slab, acc, sibc, piece, img, part, sibp, scat, zall, xr, img2, image2, last,
    gpart, gsib, gown, gscat, gram, gpart2, gscat2, gram2, in_sem,
    p_s, p_r, g_s, g_r, a_s, a_r, x_s, x_r, c_s, c_r, v_s, v_r, i_s, i_r, q_s, q_r, r_s, r_r, z_s, z_r,
    y_s, y_r, j_s, j_r, o_s, o_r, gs_s, gs_r, ga_s, ga_r, gb_s, gb_r, l_sem,
):
    b = lax.axis_index("bin")
    x = lax.axis_index("row")
    c = lax.axis_index("col")
    k = lax.rem(c, 2)
    zl = c // 2
    y = lax.rem(b, 4)
    zh = b // 4
    z = zh * 2 + zl

    def at(x_, y_, z_, k_):
        return {"bin": (z_ // 2) * 4 + y_, "row": x_, "col": lax.rem(z_, 2) * 2 + k_}

    sibling = at(x, y, z, 1 - k)
    pending, late = [], []

    def rdma(src, dst, s, r, device):
        return pltpu.make_async_remote_copy(
            src_ref=src, dst_ref=dst, send_sem=s, recv_sem=r, device_id=device, device_id_type=MESH
        )

    loads = [
        pltpu.make_async_copy(snap_hbm, snap, in_sem.at[0]),
        pltpu.make_async_copy(fi_hbm, fi, in_sem.at[1]),
        pltpu.make_async_copy(fo_hbm, fo, in_sem.at[2]),
        pltpu.make_async_copy(x0_hbm.at[pl.ds(pl.multiple_of(x * 1024, 1024), 1024)], x0, in_sem.at[3]),
    ]
    for load in loads:
        load.start()

    barrier = pltpu.get_barrier_semaphore()
    place = b * 4 + c

    def greet(i, carry):
        other = lax.rem(place + i, 32)
        pl.semaphore_signal(
            barrier, inc=1, device_id={"bin": other // 4, "row": x, "col": lax.rem(other, 4)}, device_id_type=MESH
        )
        return carry

    lax.fori_loop(1, 32, greet, 0)

    def greet_rows(i, carry):
        pl.semaphore_signal(
            barrier, inc=1, device_id={"bin": b, "row": lax.rem(x + 1 + i // 4, 4), "col": lax.rem(i, 4)},
            device_id_type=MESH,
        )
        return carry

    lax.fori_loop(0, 12, greet_rows, 0)

    loads[0].wait()
    loads[1].wait()
    for bb in range(8):
        proj[x, 16 * bb : 16 * bb + 16, :] = dot(snap[16 * bb : 16 * bb + 16, :], fi[bb], 1, 0)
    pl.semaphore_wait(barrier, 43)

    def row_exchange(buf, s, r):
        for i in (2, 1, 3):
            cp = rdma(buf.at[x], buf.at[x], s.at[i], r.at[i], at(mod4(x + i), y, z, k))
            cp.start()
            pending.append(cp)

    def row_collect(buf, s, r):
        for i in (1, 3, 2):
            frm = mod4(x - i)
            rdma(buf.at[frm], buf.at[frm], s.at[i], r.at[i], at(frm, y, z, k)).wait_recv()
        return (buf[0] + buf[1]) + (buf[2] + buf[3])

    row_exchange(proj, p_s, p_r)
    def loop_wait(send, n):
        def one(i, carry):
            send(i).wait_send()
            return carry

        late.append(lambda: lax.fori_loop(1, n, one, 0))

    loads[2].wait()
    projected = row_collect(proj, p_s, p_r).astype(BF16)
    here = z * 4 + y
    for bb in range(8):
        lifted = dot(projected[16 * bb : 16 * bb + 16, :], fo[bb], 1, 1)
        full[here, 16 * bb : 16 * bb + 16, :] = (
            snap[16 * bb : 16 * bb + 16, :].astype(F32) + lifted
        ).astype(BF16)

    is_source = zl == x // 2
    own_ci = lax.rem(x, 2)

    def slab_send(i):
        to = lax.rem(b + i, 8)
        return rdma(
            full.at[here, :, pl.ds(pl.multiple_of(to * 128, 128), 128)], slab.at[own_ci, here], a_s.at[i],
            a_r.at[here], {"bin": to, "row": x, "col": (x // 2) * 2 + k},
        )

    def start_slab(i, carry):
        slab_send(i).start()
        return carry

    lax.fori_loop(1, 8, start_slab, 0)
    loop_wait(slab_send, 8)
    slab_local = pltpu.make_async_copy(
        full.at[here, :, pl.ds(pl.multiple_of(b * 128, 128), 128)], slab.at[own_ci, here], l_sem.at[0]
    )

    @pl.when(is_source)
    def _():
        slab_local.start()

    @pl.when(jnp.logical_not(is_source))
    def _():
        slab_send(0).start()

    def finish_slab():
        @pl.when(jnp.logical_not(is_source))
        def _():
            slab_send(0).wait_send()

    late.append(finish_slab)

    def block_of(half, u, v):
        return (v * 4 + u) if half == 0 else (u * 4 + v)

    def dev_of(half, u, v):
        return at(x, u, v, k) if half == 0 else at(x, v, u, k)

    def ring(half):
        return (y, z) if half == 0 else (z, y)

    def gcopy(half, event, u, v, lo, rows, tu, tv):
        blk = full.at[block_of(half, u, v), pl.ds(64 * half + lo, rows)]
        e = 20 * half + event
        return rdma(blk, blk, g_s.at[e], g_r.at[e], dev_of(half, tu, tv))

    def gsend(*args):
        cp = gcopy(*args)
        cp.start()
        pending.append(cp)

    def gwait(half, event, u, v, lo, rows):
        gcopy(half, event, u, v, lo, rows, mod4(ring(half)[0] + 1), v).wait_recv()

    def second_send(half, t):
        u, v = ring(half)
        w = mod4(u + (0, -1, 1, 2)[t])
        gsend(half, 4 + 4 * t, w, v, 0, 64, u, mod4(v + 1))
        gsend(half, 5 + 4 * t, w, v, 0, 64, u, mod4(v - 1))

    def second_forward(half, t):
        u, v = ring(half)
        w = mod4(u + (0, -1, 1, 2)[t])
        gwait(half, 4 + 4 * t, w, mod4(v - 1), 0, 64)
        gsend(half, 6 + 4 * t, w, mod4(v - 1), 0, 32, u, mod4(v + 1))
        gwait(half, 5 + 4 * t, w, mod4(v + 1), 0, 64)
        gsend(half, 7 + 4 * t, w, mod4(v + 1), 32, 32, u, mod4(v - 1))

    def second_last(half, t):
        u, v = ring(half)
        w = mod4(u + (0, -1, 1, 2)[t])
        gwait(half, 6 + 4 * t, w, mod4(v + 2), 0, 32)
        gwait(half, 7 + 4 * t, w, mod4(v + 2), 32, 32)

    for half in (0, 1):
        u, v = ring(half)
        gsend(half, 0, u, v, 0, 64, mod4(u + 1), v)
        gsend(half, 1, u, v, 0, 64, mod4(u - 1), v)
    for half in (0, 1):
        second_send(half, 0)

    loads[3].wait()
    img[x] = dot_split(full[here], x0[...], 1, 0)
    row_exchange(img, i_s, i_r)

    for half in (0, 1):
        u, v = ring(half)
        gwait(half, 0, mod4(u - 1), v, 0, 64)
        gsend(half, 2, mod4(u - 1), v, 0, 32, mod4(u + 1), v)
        gwait(half, 1, mod4(u + 1), v, 0, 64)
        gsend(half, 3, mod4(u + 1), v, 32, 32, mod4(u - 1), v)
        second_send(half, 1)
        second_send(half, 2)

    def spread(ci, g, n, device):
        blk = slab.at[ci, pl.ds(4 * g, 4)]
        return rdma(blk, blk, x_s.at[ci, g, n], x_r.at[ci, g], device)

    right, left = at(mod4(x + 1), y, z, k), at(mod4(x - 1), y, z, k)

    @pl.when(is_source)
    def _():
        slab_local.wait()

        def arrived(i, carry):
            frm = lax.rem(here + i, 16)
            rdma(
                slab.at[own_ci, frm], slab.at[own_ci, frm], a_s.at[0], a_r.at[frm],
                at(x, lax.rem(frm, 4), frm // 4, k),
            ).wait_recv()
            return carry

        lax.fori_loop(1, 16, arrived, 0)
        for g in range(4):
            spread(own_ci, g, 0, right).start()
            spread(own_ci, g, 1, left).start()

    weights = row_collect(img, i_s, i_r)
    part[...] = (dot_split(full[here].T, weights, 1, 0) * (1.0 / 4096)).reshape(2, 2, 256, 128)
    sibp_sends = []
    for h in (0, 1):
        cp = rdma(part.at[h, 1 - k], sibp.at[h], q_s.at[h], q_r.at[h], sibling)
        cp.start()
        sibp_sends.append(cp)
        pending.append(cp)

    def spread_roles(forward):
        for ci in (0, 1):
            d = mod4(x - (2 * zl + ci))
            passes_on = d == (3 if ci == 0 else 1)
            yield ci, (passes_on if forward else (d != 0) & jnp.logical_not(passes_on))

    def spread_step(g):
        for ci, passes_on in spread_roles(True):

            @pl.when(passes_on)
            def _():
                spread(ci, g, 0, right).wait_recv()
                spread(ci, g, 0, left if ci == 0 else right).start()

    def spread_last():
        for ci, receives in spread_roles(False):

            @pl.when(receives)
            def _():
                for g in range(4):
                    spread(ci, g, 0, right).wait_recv()

    def finish_spread():
        @pl.when(is_source)
        def _():
            for g in range(4):
                spread(own_ci, g, 0, right).wait_send()
                spread(own_ci, g, 1, left).wait_send()

        for ci, passes_on in spread_roles(True):

            @pl.when(passes_on)
            def _():
                for g in range(4):
                    spread(ci, g, 0, left if ci == 0 else right).wait_send()

    late.append(finish_spread)

    for half in (0, 1):
        second_forward(half, 0)

    def plane_peer(i):
        other = lax.rem(here + i, 16)
        return at(x, lax.rem(other, 4), other // 4, k)

    def add_slots(ref, n):
        total = ref[0]
        for i in range(1, n):
            total = total + ref[i]
        return total

    for h in (0, 1):
        sibp_sends[h].wait_recv()
        sibp[h] = sibp[h] + part[h, k]

    def scat_send(i):
        other = lax.rem(here + i, 16)
        oz = other // 4
        ob = (oz // 2) * 4 + lax.rem(other, 4)
        return rdma(
            sibp.at[lax.rem(oz, 2), pl.ds(pl.multiple_of(32 * ob, 32), 32)], scat.at[here], r_s.at[i], r_r.at[i],
            plane_peer(i),
        )

    def scat_start(i, carry):
        scat_send(i).start()
        return carry

    lax.fori_loop(1, 16, scat_start, 0)
    loop_wait(scat_send, 16)
    scat[here] = sibp[zl, pl.ds(pl.multiple_of(32 * b, 32), 32)]

    for half in (0, 1):
        u, v = ring(half)
        gwait(half, 2, mod4(u + 2), v, 0, 32)
        gwait(half, 3, mod4(u + 2), v, 32, 32)
        second_send(half, 3)
    spread_step(0)
    for half in (0, 1):
        second_forward(half, 1)

    def scat_arrived(i, carry):
        frm = lax.rem(here + 16 - i, 16)
        rdma(scat.at[frm], scat.at[frm], r_s.at[i], r_r.at[i], plane_peer(i)).wait_recv()
        return carry

    lax.fori_loop(1, 16, scat_arrived, 0)
    zall[pl.ds(pl.multiple_of(32 * b, 32), 32), :] = add_slots(scat, 16)

    def bin_share(i):
        blk = zall.at[pl.ds(pl.multiple_of(32 * b, 32), 32)]
        return rdma(blk, blk, z_s.at[i], z_r.at[i], {"bin": lax.rem(b + i, 8), "row": x, "col": c})

    for i in range(1, 8):
        bin_share(i).start()
        pending.append(bin_share(i))

    for half in (0, 1):
        second_forward(half, 2)
    spread_step(1)
    spread_step(2)

    for half in (0, 1):
        second_forward(half, 3)
    spread_step(3)

    for i in range(1, 8):
        frm = lax.rem(b + 8 - i, 8)
        blk = zall.at[pl.ds(pl.multiple_of(32 * frm, 32), 32)]
        rdma(blk, blk, z_s.at[i], z_r.at[i], sibling).wait_recv()

    def col_share(i):
        return rdma(zall, xr.at[c], y_s.at[i], y_r.at[i], {"bin": b, "row": x, "col": mod4(c + i)})

    for i in (2, 1, 3):
        col_share(i).start()
        pending.append(col_share(i))
    first = zall[...]
    xr[c] = first
    gpart[...] = dot(first.T, first, 1, 0, HI)
    q = x * 4 + c
    bin_slice = pl.ds(pl.multiple_of(16 * b, 16), 16)
    gscat2[q] = gpart[bin_slice, :]

    def mesh_peer(i):
        other = lax.rem(q + i, 16)
        return {"bin": b, "row": other // 4, "col": lax.rem(other, 4)}

    def gram_send(i):
        return rdma(gscat2.at[q], gscat2.at[q], ga_s.at[0, i], ga_r.at[0, i], mesh_peer(i))

    def gram_start(i, carry):
        gram_send(i).start()
        return carry

    lax.fori_loop(1, 16, gram_start, 0)
    loop_wait(gram_send, 16)

    def gram_share(buf, i, n):
        if n == 0:
            own = b
            other = lax.rem(own + i, 8)
            device = {"bin": other, "row": x, "col": c}
        else:
            own = x * 2 + k
            other = lax.rem(own + i, 8)
            device = at(other // 2, y, z, lax.rem(other, 2))
        blk = buf.at[pl.ds(pl.multiple_of(16 * own, 16), 16)]
        return rdma(blk, blk, gb_s.at[n, i], gb_r.at[n, i], device)

    def share_start(buf, n):
        for i in range(1, 8):
            gram_share(buf, i, n).start()
            pending.append(gram_share(buf, i, n))

    def share_wait(buf, n):
        own = b if n == 0 else x * 2 + k
        for i in range(1, 8):
            frm = lax.rem(own + 8 - i, 8)
            blk = buf.at[pl.ds(pl.multiple_of(16 * frm, 16), 16)]
            rdma(blk, blk, gb_s.at[n, i], gb_r.at[n, i], sibling).wait_recv()

    spread_last()

    def stack(places):
        lhs = [
            jnp.concatenate([slab[ci, j, 64 * half : 64 * half + 64, :] for half, j in places], axis=0).T
            for ci in (0, 1)
        ]
        return jnp.concatenate(lhs, axis=0)

    def multiply(places, lhs, n):
        rhs = jnp.concatenate(
            [full[j, 64 * half : 64 * half + 64, 256 * n : 256 * n + 256] for half, j in places], axis=0
        )
        return dot(lhs, rhs, 1, 0)

    early, late_blocks = [], []
    for half in (0, 1):
        u, v = ring(half)
        for i in (0, 1, 3, 2):
            for w in range(4):
                (late_blocks if i == 2 else early).append((half, block_of(half, w, mod4(v + i))))
    lhs = stack(early)
    for n in range(4):
        acc[n] = multiply(early, lhs, n)
    for half in (0, 1):
        for t in range(4):
            second_last(half, t)
    sib_sends = []
    lhs = stack(late_blocks)
    for n in range(4):
        acc[n] = acc[n] + multiply(late_blocks, lhs, n)
        cp = rdma(
            acc.at[n, pl.ds(pl.multiple_of((1 - k) * 128, 128), 128)], sibc.at[n], c_s.at[n], c_r.at[n], sibling
        )
        cp.start()
        sib_sends.append(cp)
        pending.append(cp)
    def gram_arrived(i, carry):
        frm = lax.rem(q + 16 - i, 16)
        rdma(gscat2.at[frm], gscat2.at[frm], ga_s.at[0, i], ga_r.at[0, i], mesh_peer(i)).wait_recv()
        return carry

    lax.fori_loop(1, 16, gram_arrived, 0)
    gram[bin_slice, :] = add_slots(gscat2, 16)
    share_start(gram, 0)
    for i in (1, 2, 3):
        frm = mod4(c - i)
        rdma(zall, xr.at[frm], y_s.at[i], y_r.at[i], sibling).wait_recv()
    scaling = 1.0 / 4096
    mine = pl.ds(pl.multiple_of(k * 128, 128), 128)
    for n in range(4):
        sib_sends[n].wait_recv()
        total = (acc[n, mine] + sibc[n]) * scaling
        piece[:, 256 * n : 256 * n + 256] = total
        cov_ref[b, :, 256 * n : 256 * n + 256] = total.astype(BF16)

    img2[x] = dot(piece[...], xr[...].reshape(1024, 128), 1, 0, HI)
    row_exchange(img2, j_s, j_r)

    def csend(event, blk_b, lo, rows, device):
        blk = cov_ref.at[blk_b, pl.ds(lo, rows)]
        cp = rdma(blk, blk, v_s.at[event], v_r.at[event], device)
        cp.start()
        pending.append(cp)

    def cwait(event, blk_b, lo, rows):
        blk = cov_ref.at[blk_b, pl.ds(lo, rows)]
        rdma(blk, blk, v_s.at[event], v_r.at[event], sibling).wait_recv()

    yup, ydn = at(x, mod4(y + 1), z, k), at(x, mod4(y - 1), z, k)
    zfar = at(x, y, mod4(z + 2), k)
    yu, yd, yo = mod4(y + 1), mod4(y - 1), mod4(y + 2)
    far = 4 * (1 - zh)
    near = 4 * zh
    for event, lo, device in ((0, 0, yup), (1, 0, ydn), (8, 64, zfar), (2, 0, zfar), (9, 64, yup), (10, 64, ydn)):
        csend(event, b, lo, 64, device)

    share_wait(gram, 0)
    inverse = inverse_factor([gram[8 * i : 8 * i + 8, :] for i in range(16)])
    second = dot(row_collect(img2, j_s, j_r), inverse, 1, 1, HI)

    gpart2[...] = dot(second.T, second, 1, 0, HI)
    gsib_send = rdma(
        gpart2.at[pl.ds(pl.multiple_of(32 * x + 16 * (1 - k), 16), 16)], gsib, gs_s.at[0], gs_r.at[0], sibling
    )
    gsib_send.start()
    pending.append(gsib_send)

    image2[...] = second
    holder = c == x

    def out_send(i):
        return rdma(
            image2, last.at[lax.rem(b, 2)], o_s.at[i], o_r.at[lax.rem(b, 2)],
            {"bin": lax.rem(b + i, 8), "row": x, "col": b // 2},
        )

    @pl.when(holder)
    def _():
        for i in range(1, 8):
            out_send(i).start()

        @pl.when(b // 2 == c)
        def _():
            last[lax.rem(b, 2)] = second

        @pl.when(b // 2 != c)
        def _():
            out_send(0).start()

    def finish_out():
        @pl.when(holder)
        def _():
            for i in range(1, 8):
                out_send(i).wait_send()

            @pl.when(b // 2 != c)
            def _():
                out_send(0).wait_send()

    late.append(finish_out)

    cwait(0, near + yd, 0, 64)
    csend(3, near + yd, 0, 32, yup)
    csend(5, near + yd, 0, 64, zfar)
    cwait(1, near + yu, 0, 64)
    csend(4, near + yu, 32, 32, ydn)
    csend(6, near + yu, 0, 64, zfar)
    cwait(8, far + y, 64, 64)
    csend(11, far + y, 64, 64, yup)
    csend(12, far + y, 64, 64, ydn)
    cwait(9, near + yd, 64, 64)
    csend(13, near + yd, 64, 32, yup)
    cwait(10, near + yu, 64, 64)
    csend(14, near + yu, 96, 32, ydn)

    gsib_send.wait_recv()
    gown[...] = gpart2[pl.ds(pl.multiple_of(32 * x + 16 * k, 16), 16), :] + gsib[...]
    gscat[here] = gown[...]

    def gram2_send(i):
        return rdma(gown, gscat.at[here], ga_s.at[1, i], ga_r.at[1, i], plane_peer(i))

    def gram2_start(i, carry):
        gram2_send(i).start()
        return carry

    lax.fori_loop(1, 16, gram2_start, 0)
    loop_wait(gram2_send, 16)

    cwait(3, near + yo, 0, 32)
    cwait(4, near + yo, 32, 32)
    csend(7, near + yo, 0, 64, zfar)
    cwait(11, far + yd, 64, 64)
    csend(15, far + yd, 64, 32, yup)
    cwait(12, far + yu, 64, 64)
    csend(16, far + yu, 96, 32, ydn)

    def gram2_arrived(i, carry):
        frm = lax.rem(here + 16 - i, 16)
        rdma(gown, gscat.at[frm], ga_s.at[1, i], ga_r.at[1, i], plane_peer(i)).wait_recv()
        return carry

    lax.fori_loop(1, 16, gram2_arrived, 0)
    gram2[pl.ds(pl.multiple_of(32 * x + 16 * k, 16), 16), :] = add_slots(gscat, 16)
    share_start(gram2, 1)

    share_wait(gram2, 1)
    inverse = inverse_factor([gram2[8 * i : 8 * i + 8, :] for i in range(16)])

    for h in (0, 1):
        @pl.when(jnp.logical_not((c == x) & (b == 2 * c + h)))
        def _():
            rdma(image2, last.at[h], o_s.at[0], o_r.at[h], sibling).wait_recv()

    basis_ref[...] = dot(last[...].reshape(256, 128), inverse, 1, 1, HI) * 64.0

    cwait(2, far + y, 0, 64)
    cwait(5, far + yd, 0, 64)
    cwait(6, far + yu, 0, 64)
    cwait(7, far + yo, 0, 64)
    cwait(13, near + yo, 64, 32)
    cwait(14, near + yo, 96, 32)
    cwait(15, far + yo, 64, 32)
    cwait(16, far + yo, 96, 32)

    for cp in pending:
        cp.wait_send()
    for finish in late:
        finish()


def shards(snapshots, focus_in, focus_out, start_basis):
    snaps = snapshots.transpose(1, 2, 0).reshape(128, 1024)
    dma = pltpu.SemaphoreType.DMA
    anywhere = pl.BlockSpec(memory_space=pl.ANY)
    in_vmem = pl.BlockSpec(memory_space=pltpu.VMEM)
    pieces, basis_out = pl.pallas_call(
        kernel,
        out_shape=(
            jax.ShapeDtypeStruct((8, 128, 1024), BF16),
            jax.ShapeDtypeStruct((256, 128), F32),
        ),
        in_specs=[pl.BlockSpec(memory_space=pltpu.HBM)] * 4,
        out_specs=(in_vmem, in_vmem),
        scratch_shapes=[
            pltpu.VMEM((128, 1024), BF16),
            pltpu.VMEM((8, 1024, 128), BF16),
            pltpu.VMEM((8, 1024, 128), BF16),
            pltpu.VMEM((1024, 128), F32),
            pltpu.VMEM((4, 128, 128), F32),
            pltpu.VMEM((16, 128, 1024), BF16),
            pltpu.VMEM((2, 16, 128, 128), BF16),
            pltpu.VMEM((4, 256, 256), F32),
            pltpu.VMEM((4, 128, 256), F32),
            pltpu.VMEM((128, 1024), F32),
            pltpu.VMEM((4, 128, 128), F32),
            pltpu.VMEM((2, 2, 256, 128), F32),
            pltpu.VMEM((2, 256, 128), F32),
            pltpu.VMEM((16, 32, 128), F32),
            pltpu.VMEM((256, 128), F32),
            pltpu.VMEM((4, 256, 128), F32),
            pltpu.VMEM((4, 128, 128), F32),
            pltpu.VMEM((128, 128), F32),
            pltpu.VMEM((2, 128, 128), F32),
            pltpu.VMEM((128, 128), F32),
            pltpu.VMEM((16, 128), F32),
            pltpu.VMEM((16, 128), F32),
            pltpu.VMEM((16, 16, 128), F32),
            pltpu.VMEM((128, 128), F32),
            pltpu.VMEM((128, 128), F32),
            pltpu.VMEM((16, 16, 128), F32),
            pltpu.VMEM((128, 128), F32),
            dma((4,)),
            dma((4,)), dma((4,)),
            dma((40,)), dma((40,)),
            dma((8,)), dma((16,)),
            dma((2, 4, 2)), dma((2, 4)),
            dma((4,)), dma((4,)),
            dma((17,)), dma((17,)),
            dma((4,)), dma((4,)),
            dma((2,)), dma((2,)),
            dma((16,)), dma((16,)),
            dma((8,)), dma((8,)),
            dma((4,)), dma((4,)),
            dma((4,)), dma((4,)),
            dma((8,)), dma((2,)),
            dma((1,)), dma((1,)),
            dma((2, 16)), dma((2, 16)),
            dma((2, 8)), dma((2, 8)),
            dma((1,)),
        ],
        compiler_params=pltpu.CompilerParams(
            collective_id=0, has_side_effects=True, vmem_limit_bytes=60 * 2**20
        ),
    )(snaps, focus_in, focus_out, start_basis)
    return pieces.reshape(1024, 1024).astype(F32), basis_out


def solution(mesh):
    in_specs = (P("row", "bin", "col"), P("bin", "row", None), P("bin", "row", None), P())
    out_specs = (P("col", "row"), P(("row", "col"), None))
    return jax.shard_map(shards, mesh=mesh, in_specs=in_specs, out_specs=out_specs, check_vma=False)
```

```python
import functools
import math

import jax
import jax.numpy as jnp
from jax import lax
from jax.experimental import pallas as pl
from jax.experimental.pallas import tpu as pltpu
from jax.sharding import PartitionSpec as P

MESH = pl.DeviceIdType.MESH
HI = lax.Precision.HIGHEST
F32 = jnp.float32
BF16 = jnp.bfloat16


def mod4(v):
    return lax.rem(v + 4, 4)


def dot(a, b, ca, cb, precision=None):
    return lax.dot_general(a, b, (((ca,), (cb,)), ((), ())), precision=precision, preferred_element_type=F32)


def dot_split(a, b, ca, cb):
    high = b.astype(BF16)
    low = (b - high.astype(F32)).astype(BF16)
    return dot(a, high, ca, cb) + dot(a, low, ca, cb)


def inverse_factor(gram):
    lane = lax.broadcasted_iota(jnp.int32, (8, 128), 1)
    sub = lax.broadcasted_iota(jnp.int32, (8, 128), 0)

    def over_lanes(tile, j):
        return jnp.broadcast_to(tile[:, j : j + 1], (8, 128))

    def over_rows(tile, i):
        return jnp.broadcast_to(tile[i : i + 1, :], (8, 128))

    tiles = list(gram)
    done = []
    for p in range(16):
        first = 8 * p
        now = tiles[p]
        cols = [over_lanes(now, first + e) for e in range(8)]
        left = [[over_rows(cols[e], i) for e in range(i + 1)] for i in range(8)]
        low = [[None] * 8 for _ in range(8)]
        inv = [None] * 8
        for e in range(8):
            inv[e] = 1.0 / left[e][e]
            for i in range(e + 1, 8):
                low[i][e] = left[i][e] * inv[e]
            for i in range(e + 1, 8):
                for f in range(e + 1, i + 1):
                    left[i][f] = left[i][f] - low[i][e] * left[f][e]
        in_panel = (lane >= first) & (lane < first + 8)
        upper = []
        for i in range(8):
            row = jnp.where(in_panel, jnp.where(lane == first + i, 1.0, 0.0), over_rows(now, i))
            for e in range(i):
                row = row - low[i][e] * upper[e]
            upper.append(row)
        tile, scale = upper[0], inv[0]
        for i in range(1, 8):
            tile = jnp.where(sub == i, upper[i], tile)
            scale = jnp.where(sub == i, inv[i], scale)
        done.append(jnp.where(lane <= sub + first, tile, 0.0) * jnp.sqrt(scale))
        scaled = [upper[e] * inv[e] for e in range(8)]
        for q in range(p + 1, 16):
            total = jnp.where(in_panel, 0.0, tiles[q])
            lower = []
            for e in range(8):
                col = over_lanes(tiles[q], first + e)
                for f in range(e):
                    col = col - lower[f] * low[e][f]
                lower.append(col)
                total = total - col * scaled[e]
            tiles[q] = total
    return jnp.concatenate(done, axis=0)


def apply_factor(gram, block):
    return dot(block, inverse_factor([gram[8 * i : 8 * i + 8, :] for i in range(16)]), 1, 1, HI)


def kernel(
    snap_hbm, fi_hbm, fo_hbm, x0_hbm, cov_ref, basis_ref,
    snap, fi, fo, x0, proj, full, slab, acc, sibc, piece, img, part, sibp, scat, zall, xr, img2, image2, last,
    gpart, gsib, gown, gscat, gram, gpart2, gscat2, gram2, in_sem,
    p_s, p_r, g_s, g_r, a_s, a_r, x_s, x_r, c_s, c_r, v_s, v_r, i_s, i_r, q_s, q_r, r_s, r_r, z_s, z_r,
    y_s, y_r, j_s, j_r, o_s, o_r, gs_s, gs_r, ga_s, ga_r, gb_s, gb_r, l_sem,
):
    b = lax.axis_index("bin")
    x = lax.axis_index("row")
    c = lax.axis_index("col")
    k = lax.rem(c, 2)
    zl = c // 2
    y = lax.rem(b, 4)
    zh = b // 4
    z = zh * 2 + zl

    def at(x_, y_, z_, k_):
        return {"bin": (z_ // 2) * 4 + y_, "row": x_, "col": lax.rem(z_, 2) * 2 + k_}

    xs, ys, zs = ([v] + [mod4(v + i) for i in (1, 2, 3)] for v in (x, y, z))
    zhs = [zh] + [v // 2 for v in zs[1:]]
    zls = [zl] + [v - 2 * h for v, h in zip(zs[1:], zhs[1:])]
    zh2, zl2, ks = (zh, 1 - zh), (zl, 1 - zl), (k, 1 - k)

    def plane_peer(i, dk=0):
        return {"bin": zhs[i // 4] * 4 + ys[i % 4], "row": x, "col": zls[i // 4] * 2 + ks[dk]}

    def plane_from(i):
        return zs[-(i // 4)] * 4 + ys[-(i % 4)]

    def mesh_peer(i):
        return {"bin": b, "row": xs[i // 4], "col": zl2[i // 2 % 2] * 2 + ks[i % 2]}

    def mesh_from(i):
        return xs[-(i // 4)] * 4 + zl2[i // 2 % 2] * 2 + ks[i % 2]

    def bin_peer(i):
        return zh2[i // 4] * 4 + ys[i % 4]

    def bin_from(i):
        return zh2[i // 4] * 4 + ys[-(i % 4)]

    sibling = {"bin": b, "row": x, "col": zl * 2 + (1 - k)}
    pending, late = [], []

    def rdma(src, dst, s, r, device):
        return pltpu.make_async_remote_copy(
            src_ref=src, dst_ref=dst, send_sem=s, recv_sem=r, device_id=device, device_id_type=MESH
        )

    loads = [
        pltpu.make_async_copy(snap_hbm, snap, in_sem.at[0]),
        pltpu.make_async_copy(fi_hbm, fi, in_sem.at[1]),
        pltpu.make_async_copy(fo_hbm, fo, in_sem.at[2]),
        pltpu.make_async_copy(x0_hbm.at[pl.ds(pl.multiple_of(x * 1024, 1024), 1024)], x0, in_sem.at[3]),
    ]
    for load in loads:
        load.start()

    barrier = pltpu.get_barrier_semaphore()
    for i in range(1, 32):
        pl.semaphore_signal(barrier, inc=1, device_id=plane_peer(i // 2, i % 2), device_id_type=MESH)
    for i in range(4, 16):
        pl.semaphore_signal(barrier, inc=1, device_id=mesh_peer(i), device_id_type=MESH)

    loads[0].wait()
    loads[1].wait()
    for bb in range(8):
        proj[x, 16 * bb : 16 * bb + 16, :] = dot(snap[16 * bb : 16 * bb + 16, :], fi[bb], 1, 0)
    pl.semaphore_wait(barrier, 43)

    def row_exchange(buf, s, r):
        for i in (2, 1, 3):
            cp = rdma(buf.at[x], buf.at[x], s.at[i], r.at[i], {"bin": b, "row": xs[i], "col": c})
            cp.start()
            pending.append(cp)

    def row_collect(buf, s, r):
        for i in (1, 3, 2):
            frm = xs[-i]
            rdma(buf.at[frm], buf.at[frm], s.at[i], r.at[i], sibling).wait_recv()
        return (buf[0] + buf[1]) + (buf[2] + buf[3])

    row_exchange(proj, p_s, p_r)
    def start_all(send, n):
        for i in range(1, n):
            cp = send(i)
            cp.start()
            pending.append(cp)

    loads[2].wait()
    projected = row_collect(proj, p_s, p_r).astype(BF16)
    here = z * 4 + y
    for bb in range(8):
        lifted = dot(projected[16 * bb : 16 * bb + 16, :], fo[bb], 1, 1)
        full[here, 16 * bb : 16 * bb + 16, :] = (
            snap[16 * bb : 16 * bb + 16, :].astype(F32) + lifted
        ).astype(BF16)

    is_source = zl == x // 2
    own_ci = lax.rem(x, 2)

    def slab_send(i):
        to = bin_peer(i)
        return rdma(
            full.at[here, :, pl.ds(pl.multiple_of(to * 128, 128), 128)], slab.at[own_ci, here], a_s.at[i],
            a_r.at[here], {"bin": to, "row": x, "col": (x // 2) * 2 + k},
        )

    start_all(slab_send, 8)
    slab_local = pltpu.make_async_copy(
        full.at[here, :, pl.ds(pl.multiple_of(b * 128, 128), 128)], slab.at[own_ci, here], l_sem.at[0]
    )

    @pl.when(is_source)
    def _():
        slab_local.start()

    @pl.when(jnp.logical_not(is_source))
    def _():
        slab_send(0).start()

    def finish_slab():
        @pl.when(jnp.logical_not(is_source))
        def _():
            slab_send(0).wait_send()

    late.append(finish_slab)

    def block_of(half, u, v):
        return (v * 4 + u) if half == 0 else (u * 4 + v)

    def dev_of(half, u, v):
        return at(x, u, v, k) if half == 0 else at(x, v, u, k)

    def ring(half):
        return (y, z) if half == 0 else (z, y)

    def gcopy(half, event, u, v, lo, rows, tu, tv):
        blk = full.at[block_of(half, u, v), pl.ds(64 * half + lo, rows)]
        e = 20 * half + event
        return rdma(blk, blk, g_s.at[e], g_r.at[e], dev_of(half, tu, tv))

    def gsend(*args):
        cp = gcopy(*args)
        cp.start()
        pending.append(cp)

    def gwait(half, event, u, v, lo, rows):
        gcopy(half, event, u, v, lo, rows, mod4(ring(half)[0] + 1), v).wait_recv()

    def second_send(half, t):
        u, v = ring(half)
        w = mod4(u + (0, -1, 1, 2)[t])
        gsend(half, 4 + 4 * t, w, v, 0, 64, u, mod4(v + 1))
        gsend(half, 5 + 4 * t, w, v, 0, 64, u, mod4(v - 1))

    def second_forward(half, t):
        u, v = ring(half)
        w = mod4(u + (0, -1, 1, 2)[t])
        gwait(half, 4 + 4 * t, w, mod4(v - 1), 0, 64)
        gsend(half, 6 + 4 * t, w, mod4(v - 1), 0, 32, u, mod4(v + 1))
        gwait(half, 5 + 4 * t, w, mod4(v + 1), 0, 64)
        gsend(half, 7 + 4 * t, w, mod4(v + 1), 32, 32, u, mod4(v - 1))

    def second_last(half, t):
        u, v = ring(half)
        w = mod4(u + (0, -1, 1, 2)[t])
        gwait(half, 6 + 4 * t, w, mod4(v + 2), 0, 32)
        gwait(half, 7 + 4 * t, w, mod4(v + 2), 32, 32)

    for half in (0, 1):
        u, v = ring(half)
        gsend(half, 0, u, v, 0, 64, mod4(u + 1), v)
        gsend(half, 1, u, v, 0, 64, mod4(u - 1), v)
    for half in (0, 1):
        second_send(half, 0)

    loads[3].wait()
    img[x] = dot_split(full[here], x0[...], 1, 0)
    row_exchange(img, i_s, i_r)

    for half in (0, 1):
        u, v = ring(half)
        gwait(half, 0, mod4(u - 1), v, 0, 64)
        gsend(half, 2, mod4(u - 1), v, 0, 32, mod4(u + 1), v)
        gwait(half, 1, mod4(u + 1), v, 0, 64)
        gsend(half, 3, mod4(u + 1), v, 32, 32, mod4(u - 1), v)
        second_send(half, 1)
        second_send(half, 2)

    def spread(ci, g, n, device):
        blk = slab.at[ci, pl.ds(4 * g, 4)]
        return rdma(blk, blk, x_s.at[ci, g, n], x_r.at[ci, g], device)

    right, left = at(mod4(x + 1), y, z, k), at(mod4(x - 1), y, z, k)

    @pl.when(is_source)
    def _():
        slab_local.wait()

        for i in range(1, 16):
            frm = plane_from(i)
            rdma(slab.at[own_ci, frm], slab.at[own_ci, frm], a_s.at[0], a_r.at[frm], sibling).wait_recv()
        for g in range(4):
            spread(own_ci, g, 0, right).start()
            spread(own_ci, g, 1, left).start()

    weights = row_collect(img, i_s, i_r)
    part[...] = (dot_split(full[here].T, weights, 1, 0) * (1.0 / 4096)).reshape(2, 2, 256, 128)
    sibp_sends = []
    for h in (0, 1):
        cp = rdma(part.at[h, 1 - k], sibp.at[h], q_s.at[h], q_r.at[h], sibling)
        cp.start()
        sibp_sends.append(cp)
        pending.append(cp)

    def spread_roles(forward):
        for ci in (0, 1):
            d = mod4(x - (2 * zl + ci))
            passes_on = d == (3 if ci == 0 else 1)
            yield ci, (passes_on if forward else (d != 0) & jnp.logical_not(passes_on))

    def spread_step(g):
        for ci, passes_on in spread_roles(True):

            @pl.when(passes_on)
            def _():
                spread(ci, g, 0, right).wait_recv()
                spread(ci, g, 0, left if ci == 0 else right).start()

    def spread_last():
        for ci, receives in spread_roles(False):

            @pl.when(receives)
            def _():
                for g in range(4):
                    spread(ci, g, 0, right).wait_recv()

    def finish_spread():
        @pl.when(is_source)
        def _():
            for g in range(4):
                spread(own_ci, g, 0, right).wait_send()
                spread(own_ci, g, 1, left).wait_send()

        for ci, passes_on in spread_roles(True):

            @pl.when(passes_on)
            def _():
                for g in range(4):
                    spread(ci, g, 0, left if ci == 0 else right).wait_send()

    late.append(finish_spread)

    for half in (0, 1):
        second_forward(half, 0)

    def add_slots(ref, n):
        total = ref[0]
        for i in range(1, n):
            total = total + ref[i]
        return total

    for h in (0, 1):
        sibp_sends[h].wait_recv()
        sibp[h] = sibp[h] + part[h, k]

    def scat_send(i):
        ob = zhs[i // 4] * 4 + ys[i % 4]
        return rdma(
            sibp.at[zls[i // 4], pl.ds(pl.multiple_of(32 * ob, 32), 32)], scat.at[here], r_s.at[i], r_r.at[i],
            plane_peer(i),
        )

    start_all(scat_send, 16)
    scat[here] = sibp[zl, pl.ds(pl.multiple_of(32 * b, 32), 32)]

    for half in (0, 1):
        u, v = ring(half)
        gwait(half, 2, mod4(u + 2), v, 0, 32)
        gwait(half, 3, mod4(u + 2), v, 32, 32)
        second_send(half, 3)
    spread_step(0)
    for half in (0, 1):
        second_forward(half, 1)

    for i in range(1, 16):
        frm = plane_from(i)
        rdma(scat.at[frm], scat.at[frm], r_s.at[i], r_r.at[i], sibling).wait_recv()
    zall[pl.ds(pl.multiple_of(32 * b, 32), 32), :] = add_slots(scat, 16)

    def bin_share(i):
        blk = zall.at[pl.ds(pl.multiple_of(32 * b, 32), 32)]
        return rdma(blk, blk, z_s.at[i], z_r.at[i], {"bin": bin_peer(i), "row": x, "col": c})

    start_all(bin_share, 8)

    for half in (0, 1):
        second_forward(half, 2)
    spread_step(1)
    spread_step(2)

    for half in (0, 1):
        second_forward(half, 3)
    spread_step(3)

    for i in range(1, 8):
        frm = bin_from(i)
        blk = zall.at[pl.ds(pl.multiple_of(32 * frm, 32), 32)]
        rdma(blk, blk, z_s.at[i], z_r.at[i], sibling).wait_recv()

    def col_share(i):
        return rdma(zall, xr.at[c], y_s.at[i], y_r.at[i], {"bin": b, "row": x, "col": mod4(c + i)})

    for i in (2, 1, 3):
        col_share(i).start()
        pending.append(col_share(i))
    first = zall[...]
    xr[c] = first
    gpart[...] = dot(first.T, first, 1, 0, HI)
    q = x * 4 + c
    bin_slice = pl.ds(pl.multiple_of(16 * b, 16), 16)
    gscat2[q] = gpart[bin_slice, :]

    def gram_send(i):
        return rdma(gscat2.at[q], gscat2.at[q], ga_s.at[0, i], ga_r.at[0, i], mesh_peer(i))

    start_all(gram_send, 16)

    def gram_share(buf, i, n):
        if n == 0:
            own = b
            device = {"bin": bin_peer(i), "row": x, "col": c}
        else:
            own = x * 2 + k
            device = {"bin": b, "row": xs[i // 2], "col": zl * 2 + ks[i % 2]}
        blk = buf.at[pl.ds(pl.multiple_of(16 * own, 16), 16)]
        return rdma(blk, blk, gb_s.at[n, i], gb_r.at[n, i], device)

    def share_wait(buf, n):
        for i in range(1, 8):
            frm = bin_from(i) if n == 0 else xs[-(i // 2)] * 2 + ks[i % 2]
            blk = buf.at[pl.ds(pl.multiple_of(16 * frm, 16), 16)]
            rdma(blk, blk, gb_s.at[n, i], gb_r.at[n, i], sibling).wait_recv()

    spread_last()

    def stack(places):
        lhs = [
            jnp.concatenate([slab[ci, j, 64 * half : 64 * half + 64, :] for half, j in places], axis=0).T
            for ci in (0, 1)
        ]
        return jnp.concatenate(lhs, axis=0)

    def multiply(places, lhs, n):
        rhs = jnp.concatenate(
            [full[j, 64 * half : 64 * half + 64, 256 * n : 256 * n + 256] for half, j in places], axis=0
        )
        return dot(lhs, rhs, 1, 0)

    early, late_blocks = [], []
    for half in (0, 1):
        u, v = ring(half)
        for i in (0, 1, 3, 2):
            for w in range(4):
                (late_blocks if i == 2 else early).append((half, block_of(half, w, mod4(v + i))))
    lhs = stack(early)
    for n in range(4):
        acc[n] = multiply(early, lhs, n)
    for half in (0, 1):
        for t in range(4):
            second_last(half, t)
    sib_sends = []
    lhs = stack(late_blocks)
    for n in range(4):
        acc[n] = acc[n] + multiply(late_blocks, lhs, n)
        cp = rdma(
            acc.at[n, pl.ds(pl.multiple_of((1 - k) * 128, 128), 128)], sibc.at[n], c_s.at[n], c_r.at[n], sibling
        )
        cp.start()
        sib_sends.append(cp)
        pending.append(cp)
    for i in range(1, 16):
        frm = mesh_from(i)
        rdma(gscat2.at[frm], gscat2.at[frm], ga_s.at[0, i], ga_r.at[0, i], sibling).wait_recv()
    gram[bin_slice, :] = add_slots(gscat2, 16)
    start_all(lambda i: gram_share(gram, i, 0), 8)
    for i in (1, 2, 3):
        frm = mod4(c - i)
        rdma(zall, xr.at[frm], y_s.at[i], y_r.at[i], sibling).wait_recv()
    scaling = 1.0 / 4096
    mine = pl.ds(pl.multiple_of(k * 128, 128), 128)
    for n in range(4):
        sib_sends[n].wait_recv()
        total = (acc[n, mine] + sibc[n]) * scaling
        piece[:, 256 * n : 256 * n + 256] = total
        cov_ref[b, :, 256 * n : 256 * n + 256] = total.astype(BF16)

    img2[x] = dot(piece[...], xr[...].reshape(1024, 128), 1, 0, HI)
    row_exchange(img2, j_s, j_r)

    def csend(event, blk_b, lo, rows, device):
        blk = cov_ref.at[blk_b, pl.ds(lo, rows)]
        cp = rdma(blk, blk, v_s.at[event], v_r.at[event], device)
        cp.start()
        pending.append(cp)

    def cwait(event, blk_b, lo, rows):
        blk = cov_ref.at[blk_b, pl.ds(lo, rows)]
        rdma(blk, blk, v_s.at[event], v_r.at[event], sibling).wait_recv()

    yup, ydn = at(x, mod4(y + 1), z, k), at(x, mod4(y - 1), z, k)
    zfar = at(x, y, mod4(z + 2), k)
    yu, yd, yo = mod4(y + 1), mod4(y - 1), mod4(y + 2)
    far = 4 * (1 - zh)
    near = 4 * zh
    for event, lo, device in ((0, 0, yup), (1, 0, ydn), (8, 64, zfar), (2, 0, zfar), (9, 64, yup), (10, 64, ydn)):
        csend(event, b, lo, 64, device)

    share_wait(gram, 0)
    inverse = inverse_factor([gram[8 * i : 8 * i + 8, :] for i in range(16)])
    second = dot(row_collect(img2, j_s, j_r), inverse, 1, 1, HI)

    gpart2[...] = dot(second.T, second, 1, 0, HI)
    gsib_send = rdma(
        gpart2.at[pl.ds(pl.multiple_of(32 * x + 16 * (1 - k), 16), 16)], gsib, gs_s.at[0], gs_r.at[0], sibling
    )
    gsib_send.start()
    pending.append(gsib_send)

    image2[...] = second
    holder = c == x
    half_bin = b // 2
    odd = b - 2 * half_bin

    def out_send(i):
        return rdma(
            image2, last.at[odd], o_s.at[i], o_r.at[odd],
            {"bin": bin_peer(i), "row": x, "col": half_bin},
        )

    @pl.when(holder)
    def _():
        for i in range(1, 8):
            out_send(i).start()

        @pl.when(half_bin == c)
        def _():
            last[odd] = second

        @pl.when(half_bin != c)
        def _():
            out_send(0).start()

    def finish_out():
        @pl.when(holder)
        def _():
            for i in range(1, 8):
                out_send(i).wait_send()

            @pl.when(half_bin != c)
            def _():
                out_send(0).wait_send()

    late.append(finish_out)

    gsib_send.wait_recv()
    gown[...] = gpart2[pl.ds(pl.multiple_of(32 * x + 16 * k, 16), 16), :] + gsib[...]
    gscat[here] = gown[...]

    def gram2_send(i):
        return rdma(gown, gscat.at[here], ga_s.at[1, i], ga_r.at[1, i], plane_peer(i))

    start_all(gram2_send, 16)

    cwait(0, near + yd, 0, 64)
    csend(3, near + yd, 0, 32, yup)
    csend(5, near + yd, 0, 64, zfar)
    cwait(1, near + yu, 0, 64)
    csend(4, near + yu, 32, 32, ydn)
    csend(6, near + yu, 0, 64, zfar)
    cwait(8, far + y, 64, 64)
    csend(11, far + y, 64, 64, yup)
    csend(12, far + y, 64, 64, ydn)
    cwait(9, near + yd, 64, 64)
    csend(13, near + yd, 64, 32, yup)
    cwait(10, near + yu, 64, 64)
    csend(14, near + yu, 96, 32, ydn)

    for i in range(1, 16):
        frm = plane_from(i)
        rdma(gown, gscat.at[frm], ga_s.at[1, i], ga_r.at[1, i], sibling).wait_recv()
    gram2[pl.ds(pl.multiple_of(32 * x + 16 * k, 16), 16), :] = add_slots(gscat, 16)
    start_all(lambda i: gram_share(gram2, i, 1), 8)

    cwait(3, near + yo, 0, 32)
    cwait(4, near + yo, 32, 32)
    csend(7, near + yo, 0, 64, zfar)
    cwait(11, far + yd, 64, 64)
    csend(15, far + yd, 64, 32, yup)
    cwait(12, far + yu, 64, 64)
    csend(16, far + yu, 96, 32, ydn)

    share_wait(gram2, 1)
    inverse = inverse_factor([gram2[8 * i : 8 * i + 8, :] for i in range(16)])

    for h in (0, 1):
        @pl.when(jnp.logical_not((c == x) & (b == 2 * c + h)))
        def _():
            rdma(image2, last.at[h], o_s.at[0], o_r.at[h], sibling).wait_recv()

    basis_ref[...] = dot(last[...].reshape(256, 128), inverse, 1, 1, HI) * 64.0

    cwait(2, far + y, 0, 64)
    cwait(5, far + yd, 0, 64)
    cwait(6, far + yu, 0, 64)
    cwait(7, far + yo, 0, 64)
    cwait(13, near + yo, 64, 32)
    cwait(14, near + yo, 96, 32)
    cwait(15, far + yo, 64, 32)
    cwait(16, far + yo, 96, 32)

    for cp in pending:
        cp.wait_send()
    for finish in late:
        finish()


def shards(snapshots, focus_in, focus_out, start_basis):
    snaps = snapshots.transpose(1, 2, 0).reshape(128, 1024)
    dma = pltpu.SemaphoreType.DMA
    anywhere = pl.BlockSpec(memory_space=pl.ANY)
    in_vmem = pl.BlockSpec(memory_space=pltpu.VMEM)
    pieces, basis_out = pl.pallas_call(
        kernel,
        out_shape=(
            jax.ShapeDtypeStruct((8, 128, 1024), BF16),
            jax.ShapeDtypeStruct((256, 128), F32),
        ),
        in_specs=[pl.BlockSpec(memory_space=pltpu.HBM)] * 4,
        out_specs=(in_vmem, in_vmem),
        scratch_shapes=[
            pltpu.VMEM((128, 1024), BF16),
            pltpu.VMEM((8, 1024, 128), BF16),
            pltpu.VMEM((8, 1024, 128), BF16),
            pltpu.VMEM((1024, 128), F32),
            pltpu.VMEM((4, 128, 128), F32),
            pltpu.VMEM((16, 128, 1024), BF16),
            pltpu.VMEM((2, 16, 128, 128), BF16),
            pltpu.VMEM((4, 256, 256), F32),
            pltpu.VMEM((4, 128, 256), F32),
            pltpu.VMEM((128, 1024), F32),
            pltpu.VMEM((4, 128, 128), F32),
            pltpu.VMEM((2, 2, 256, 128), F32),
            pltpu.VMEM((2, 256, 128), F32),
            pltpu.VMEM((16, 32, 128), F32),
            pltpu.VMEM((256, 128), F32),
            pltpu.VMEM((4, 256, 128), F32),
            pltpu.VMEM((4, 128, 128), F32),
            pltpu.VMEM((128, 128), F32),
            pltpu.VMEM((2, 128, 128), F32),
            pltpu.VMEM((128, 128), F32),
            pltpu.VMEM((16, 128), F32),
            pltpu.VMEM((16, 128), F32),
            pltpu.VMEM((16, 16, 128), F32),
            pltpu.VMEM((128, 128), F32),
            pltpu.VMEM((128, 128), F32),
            pltpu.VMEM((16, 16, 128), F32),
            pltpu.VMEM((128, 128), F32),
            dma((4,)),
            dma((4,)), dma((4,)),
            dma((40,)), dma((40,)),
            dma((8,)), dma((16,)),
            dma((2, 4, 2)), dma((2, 4)),
            dma((4,)), dma((4,)),
            dma((17,)), dma((17,)),
            dma((4,)), dma((4,)),
            dma((2,)), dma((2,)),
            dma((16,)), dma((16,)),
            dma((8,)), dma((8,)),
            dma((4,)), dma((4,)),
            dma((4,)), dma((4,)),
            dma((8,)), dma((2,)),
            dma((1,)), dma((1,)),
            dma((2, 16)), dma((2, 16)),
            dma((2, 8)), dma((2, 8)),
            dma((1,)),
        ],
        compiler_params=pltpu.CompilerParams(
            collective_id=0, has_side_effects=True, vmem_limit_bytes=60 * 2**20
        ),
    )(snaps, focus_in, focus_out, start_basis)
    return pieces.reshape(1024, 1024).astype(F32), basis_out


def solution(mesh):
    in_specs = (P("row", "bin", "col"), P("bin", "row", None), P("bin", "row", None), P())
    out_specs = (P("col", "row"), P(("row", "col"), None))
    return jax.shard_map(shards, mesh=mesh, in_specs=in_specs, out_specs=out_specs, check_vma=False)
```

```python
import functools
import math

import jax
import jax.numpy as jnp
from jax import lax
from jax.experimental import pallas as pl
from jax.experimental.pallas import tpu as pltpu
from jax.sharding import PartitionSpec as P

MESH = pl.DeviceIdType.MESH
HI = lax.Precision.HIGHEST
F32 = jnp.float32
BF16 = jnp.bfloat16


def mod4(v):
    return lax.rem(v + 4, 4)


def dot(a, b, ca, cb, precision=None):
    return lax.dot_general(a, b, (((ca,), (cb,)), ((), ())), precision=precision, preferred_element_type=F32)


def dot_split(a, b, ca, cb):
    high = b.astype(BF16)
    low = (b - high.astype(F32)).astype(BF16)
    return dot(a, high, ca, cb) + dot(a, low, ca, cb)


def inverse_factor(gram):
    lane = lax.broadcasted_iota(jnp.int32, (8, 128), 1)
    sub = lax.broadcasted_iota(jnp.int32, (8, 128), 0)

    def over_lanes(tile, j):
        return jnp.broadcast_to(tile[:, j : j + 1], (8, 128))

    def over_rows(tile, i):
        return jnp.broadcast_to(tile[i : i + 1, :], (8, 128))

    tiles = list(gram)
    done = []
    for p in range(16):
        first = 8 * p
        now = tiles[p]
        cols = [over_lanes(now, first + e) for e in range(8)]
        left = [[over_rows(cols[e], i) for e in range(i + 1)] for i in range(8)]
        low = [[None] * 8 for _ in range(8)]
        inv = [None] * 8
        for e in range(8):
            inv[e] = 1.0 / left[e][e]
            for i in range(e + 1, 8):
                low[i][e] = left[i][e] * inv[e]
            for i in range(e + 1, 8):
                for f in range(e + 1, i + 1):
                    left[i][f] = left[i][f] - low[i][e] * left[f][e]
        in_panel = (lane >= first) & (lane < first + 8)
        upper = []
        for i in range(8):
            row = jnp.where(in_panel, jnp.where(lane == first + i, 1.0, 0.0), over_rows(now, i))
            for e in range(i):
                row = row - low[i][e] * upper[e]
            upper.append(row)
        tile, scale = upper[0], inv[0]
        for i in range(1, 8):
            tile = jnp.where(sub == i, upper[i], tile)
            scale = jnp.where(sub == i, inv[i], scale)
        done.append(jnp.where(lane <= sub + first, tile, 0.0) * jnp.sqrt(scale))
        scaled = [upper[e] * inv[e] for e in range(8)]
        for q in range(p + 1, 16):
            total = jnp.where(in_panel, 0.0, tiles[q])
            lower = []
            for e in range(8):
                col = over_lanes(tiles[q], first + e)
                for f in range(e):
                    col = col - lower[f] * low[e][f]
                lower.append(col)
                total = total - col * scaled[e]
            tiles[q] = total
    return jnp.concatenate(done, axis=0)


def apply_factor(gram, block):
    return dot(block, inverse_factor([gram[8 * i : 8 * i + 8, :] for i in range(16)]), 1, 1, HI)


def kernel(
    snap_hbm, fi_hbm, fo_hbm, x0_hbm, cov_ref, basis_ref,
    snap, fi, fo, x0, proj, full, slab, acc, sibc, piece, img, part, sibp, scat, zall, xr, img2, image2, last,
    gx, gsib, gown, gscat, gpart2, gram2, in_sem,
    p_s, p_r, g_s, g_r, a_s, a_r, x_s, x_r, c_s, c_r, v_s, v_r, i_s, i_r, q_s, q_r, r_s, r_r, z_s, z_r,
    y_s, y_r, j_s, j_r, o_s, o_r, gs_s, gs_r, ga_s, ga_r, gb_s, gb_r, h_s, h_r, l_sem,
):
    b = lax.axis_index("bin")
    x = lax.axis_index("row")
    c = lax.axis_index("col")
    k = lax.rem(c, 2)
    zl = c // 2
    y = lax.rem(b, 4)
    zh = b // 4
    z = zh * 2 + zl

    def at(x_, y_, z_, k_):
        return {"bin": (z_ // 2) * 4 + y_, "row": x_, "col": lax.rem(z_, 2) * 2 + k_}

    xs, ys, zs = ([v] + [mod4(v + i) for i in (1, 2, 3)] for v in (x, y, z))
    zhs = [zh] + [v // 2 for v in zs[1:]]
    zls = [zl] + [v - 2 * h for v, h in zip(zs[1:], zhs[1:])]
    zh2, zl2, ks = (zh, 1 - zh), (zl, 1 - zl), (k, 1 - k)

    def plane_peer(i, dk=0):
        return {"bin": zhs[i // 4] * 4 + ys[i % 4], "row": x, "col": zls[i // 4] * 2 + ks[dk]}

    def plane_from(i):
        return zs[-(i // 4)] * 4 + ys[-(i % 4)]

    def mesh_peer(i):
        return {"bin": b, "row": xs[i // 4], "col": zl2[i // 2 % 2] * 2 + ks[i % 2]}

    def mesh_from(i):
        return xs[-(i // 4)] * 4 + zl2[i // 2 % 2] * 2 + ks[i % 2]

    def bin_peer(i):
        return zh2[i // 4] * 4 + ys[i % 4]

    def bin_from(i):
        return zh2[i // 4] * 4 + ys[-(i % 4)]

    sibling = {"bin": b, "row": x, "col": zl * 2 + (1 - k)}
    pending, late = [], []

    def rdma(src, dst, s, r, device):
        return pltpu.make_async_remote_copy(
            src_ref=src, dst_ref=dst, send_sem=s, recv_sem=r, device_id=device, device_id_type=MESH
        )

    loads = [
        pltpu.make_async_copy(snap_hbm, snap, in_sem.at[0]),
        pltpu.make_async_copy(fi_hbm, fi, in_sem.at[1]),
        pltpu.make_async_copy(fo_hbm, fo, in_sem.at[2]),
        pltpu.make_async_copy(x0_hbm.at[pl.ds(pl.multiple_of(x * 1024, 1024), 1024)], x0, in_sem.at[3]),
    ]
    for load in loads:
        load.start()

    barrier = pltpu.get_barrier_semaphore()
    for i in range(1, 32):
        pl.semaphore_signal(barrier, inc=1, device_id=plane_peer(i // 2, i % 2), device_id_type=MESH)
    for i in range(4, 16):
        pl.semaphore_signal(barrier, inc=1, device_id=mesh_peer(i), device_id_type=MESH)

    loads[0].wait()
    loads[1].wait()
    for bb in range(8):
        proj[x, 16 * bb : 16 * bb + 16, :] = dot(snap[16 * bb : 16 * bb + 16, :], fi[bb], 1, 0)
    pl.semaphore_wait(barrier, 43)

    def row_exchange(buf, s, r):
        for i in (2, 1, 3):
            cp = rdma(buf.at[x], buf.at[x], s.at[i], r.at[i], {"bin": b, "row": xs[i], "col": c})
            cp.start()
            pending.append(cp)

    def row_collect(buf, s, r):
        for i in (1, 3, 2):
            frm = xs[-i]
            rdma(buf.at[frm], buf.at[frm], s.at[i], r.at[i], sibling).wait_recv()
        return (buf[0] + buf[1]) + (buf[2] + buf[3])

    row_exchange(proj, p_s, p_r)
    def start_all(send, n):
        for i in range(1, n):
            cp = send(i)
            cp.start()
            pending.append(cp)

    loads[2].wait()
    projected = row_collect(proj, p_s, p_r).astype(BF16)
    here = z * 4 + y
    for bb in range(8):
        lifted = dot(projected[16 * bb : 16 * bb + 16, :], fo[bb], 1, 1)
        full[here, 16 * bb : 16 * bb + 16, :] = (
            snap[16 * bb : 16 * bb + 16, :].astype(F32) + lifted
        ).astype(BF16)

    is_source = zl == x // 2
    own_ci = lax.rem(x, 2)

    def slab_send(i):
        to = bin_peer(i)
        return rdma(
            full.at[here, :, pl.ds(pl.multiple_of(to * 128, 128), 128)], slab.at[own_ci, here], a_s.at[i],
            a_r.at[here], {"bin": to, "row": x, "col": (x // 2) * 2 + k},
        )

    start_all(slab_send, 8)
    slab_local = pltpu.make_async_copy(
        full.at[here, :, pl.ds(pl.multiple_of(b * 128, 128), 128)], slab.at[own_ci, here], l_sem.at[0]
    )

    @pl.when(is_source)
    def _():
        slab_local.start()

    @pl.when(jnp.logical_not(is_source))
    def _():
        slab_send(0).start()

    def finish_slab():
        @pl.when(jnp.logical_not(is_source))
        def _():
            slab_send(0).wait_send()

    late.append(finish_slab)

    def block_of(half, u, v):
        return (v * 4 + u) if half == 0 else (u * 4 + v)

    def dev_of(half, u, v):
        return at(x, u, v, k) if half == 0 else at(x, v, u, k)

    def ring(half):
        return (y, z) if half == 0 else (z, y)

    def gcopy(half, event, u, v, lo, rows, tu, tv):
        blk = full.at[block_of(half, u, v), pl.ds(64 * half + lo, rows)]
        e = 20 * half + event
        return rdma(blk, blk, g_s.at[e], g_r.at[e], dev_of(half, tu, tv))

    def gsend(*args):
        cp = gcopy(*args)
        cp.start()
        pending.append(cp)

    def gwait(half, event, u, v, lo, rows):
        gcopy(half, event, u, v, lo, rows, mod4(ring(half)[0] + 1), v).wait_recv()

    def second_send(half, t):
        u, v = ring(half)
        w = mod4(u + (0, -1, 1, 2)[t])
        gsend(half, 4 + 4 * t, w, v, 0, 64, u, mod4(v + 1))
        gsend(half, 5 + 4 * t, w, v, 0, 64, u, mod4(v - 1))

    def second_forward(half, t):
        u, v = ring(half)
        w = mod4(u + (0, -1, 1, 2)[t])
        gwait(half, 4 + 4 * t, w, mod4(v - 1), 0, 64)
        gsend(half, 6 + 4 * t, w, mod4(v - 1), 0, 32, u, mod4(v + 1))
        gwait(half, 5 + 4 * t, w, mod4(v + 1), 0, 64)
        gsend(half, 7 + 4 * t, w, mod4(v + 1), 32, 32, u, mod4(v - 1))

    def second_last(half, t):
        u, v = ring(half)
        w = mod4(u + (0, -1, 1, 2)[t])
        gwait(half, 6 + 4 * t, w, mod4(v + 2), 0, 32)
        gwait(half, 7 + 4 * t, w, mod4(v + 2), 32, 32)

    for half in (0, 1):
        u, v = ring(half)
        gsend(half, 0, u, v, 0, 64, mod4(u + 1), v)
        gsend(half, 1, u, v, 0, 64, mod4(u - 1), v)
    for half in (0, 1):
        second_send(half, 0)

    loads[3].wait()
    img[x] = dot_split(full[here], x0[...], 1, 0)
    row_exchange(img, i_s, i_r)

    for half in (0, 1):
        u, v = ring(half)
        gwait(half, 0, mod4(u - 1), v, 0, 64)
        gsend(half, 2, mod4(u - 1), v, 0, 32, mod4(u + 1), v)
        gwait(half, 1, mod4(u + 1), v, 0, 64)
        gsend(half, 3, mod4(u + 1), v, 32, 32, mod4(u - 1), v)
        second_send(half, 1)
        second_send(half, 2)

    def spread(ci, g, n, device):
        blk = slab.at[ci, pl.ds(4 * g, 4)]
        return rdma(blk, blk, x_s.at[ci, g, n], x_r.at[ci, g], device)

    right, left = at(mod4(x + 1), y, z, k), at(mod4(x - 1), y, z, k)

    @pl.when(is_source)
    def _():
        slab_local.wait()

        for i in range(1, 16):
            frm = plane_from(i)
            rdma(slab.at[own_ci, frm], slab.at[own_ci, frm], a_s.at[0], a_r.at[frm], sibling).wait_recv()
        for g in range(4):
            spread(own_ci, g, 0, right).start()
            spread(own_ci, g, 1, left).start()

    weights = row_collect(img, i_s, i_r)
    part[...] = (dot_split(full[here].T, weights, 1, 0) * (1.0 / 4096)).reshape(2, 2, 256, 128)
    sibp_sends = []
    for h in (0, 1):
        cp = rdma(part.at[h, 1 - k], sibp.at[h], q_s.at[h], q_r.at[h], sibling)
        cp.start()
        sibp_sends.append(cp)
        pending.append(cp)

    def spread_roles(forward):
        for ci in (0, 1):
            d = mod4(x - (2 * zl + ci))
            passes_on = d == (3 if ci == 0 else 1)
            yield ci, (passes_on if forward else (d != 0) & jnp.logical_not(passes_on))

    def spread_step(g):
        for ci, passes_on in spread_roles(True):

            @pl.when(passes_on)
            def _():
                spread(ci, g, 0, right).wait_recv()
                spread(ci, g, 0, left if ci == 0 else right).start()

    def spread_last():
        for ci, receives in spread_roles(False):

            @pl.when(receives)
            def _():
                for g in range(4):
                    spread(ci, g, 0, right).wait_recv()

    def finish_spread():
        @pl.when(is_source)
        def _():
            for g in range(4):
                spread(own_ci, g, 0, right).wait_send()
                spread(own_ci, g, 1, left).wait_send()

        for ci, passes_on in spread_roles(True):

            @pl.when(passes_on)
            def _():
                for g in range(4):
                    spread(ci, g, 0, left if ci == 0 else right).wait_send()

    late.append(finish_spread)

    for half in (0, 1):
        second_forward(half, 0)

    def add_slots(ref, n):
        total = ref[0]
        for i in range(1, n):
            total = total + ref[i]
        return total

    for h in (0, 1):
        sibp_sends[h].wait_recv()
        sibp[h] = sibp[h] + part[h, k]

    def scat_send(i):
        ob = zhs[i // 4] * 4 + ys[i % 4]
        return rdma(
            sibp.at[zls[i // 4], pl.ds(pl.multiple_of(32 * ob, 32), 32)], scat.at[here], r_s.at[i], r_r.at[i],
            plane_peer(i),
        )

    start_all(scat_send, 16)
    scat[here] = sibp[zl, pl.ds(pl.multiple_of(32 * b, 32), 32)]

    for half in (0, 1):
        u, v = ring(half)
        gwait(half, 2, mod4(u + 2), v, 0, 32)
        gwait(half, 3, mod4(u + 2), v, 32, 32)
        second_send(half, 3)
    spread_step(0)
    for half in (0, 1):
        second_forward(half, 1)

    for i in range(1, 16):
        frm = plane_from(i)
        rdma(scat.at[frm], scat.at[frm], r_s.at[i], r_r.at[i], sibling).wait_recv()
    zall[pl.ds(pl.multiple_of(32 * b, 32), 32), :] = add_slots(scat, 16)

    def bin_share(i):
        blk = zall.at[pl.ds(pl.multiple_of(32 * b, 32), 32)]
        return rdma(blk, blk, z_s.at[i], z_r.at[i], {"bin": bin_peer(i), "row": x, "col": c})

    start_all(bin_share, 8)

    for half in (0, 1):
        second_forward(half, 2)
    spread_step(1)
    spread_step(2)

    for half in (0, 1):
        second_forward(half, 3)
    spread_step(3)

    for i in range(1, 8):
        frm = bin_from(i)
        blk = zall.at[pl.ds(pl.multiple_of(32 * frm, 32), 32)]
        rdma(blk, blk, z_s.at[i], z_r.at[i], sibling).wait_recv()

    def col_share(i):
        return rdma(zall, xr.at[c], y_s.at[i], y_r.at[i], {"bin": b, "row": x, "col": mod4(c + i)})

    for i in (2, 1, 3):
        col_share(i).start()
        pending.append(col_share(i))
    xr[c] = zall[...]

    def gram_share(i):
        blk = gram2.at[pl.ds(pl.multiple_of(16 * (x * 2 + k), 16), 16)]
        return rdma(blk, blk, gb_s.at[i], gb_r.at[i], {"bin": b, "row": xs[i // 2], "col": zl * 2 + ks[i % 2]})

    def share_wait():
        for i in range(1, 8):
            frm = xs[-(i // 2)] * 2 + ks[i % 2]
            blk = gram2.at[pl.ds(pl.multiple_of(16 * frm, 16), 16)]
            rdma(blk, blk, gb_s.at[i], gb_r.at[i], sibling).wait_recv()

    spread_last()

    def stack(places):
        lhs = [
            jnp.concatenate([slab[ci, j, 64 * half : 64 * half + 64, :] for half, j in places], axis=0).T
            for ci in (0, 1)
        ]
        return jnp.concatenate(lhs, axis=0)

    def multiply(places, lhs, n):
        rhs = jnp.concatenate(
            [full[j, 64 * half : 64 * half + 64, 256 * n : 256 * n + 256] for half, j in places], axis=0
        )
        return dot(lhs, rhs, 1, 0)

    early, late_blocks = [], []
    for half in (0, 1):
        u, v = ring(half)
        for i in (0, 1, 3, 2):
            for w in range(4):
                (late_blocks if i == 2 else early).append((half, block_of(half, w, mod4(v + i))))
    lhs = stack(early)
    for n in range(4):
        acc[n] = multiply(early, lhs, n)

    for i in (1, 2, 3):
        frm = mod4(c - i)
        rdma(zall, xr.at[frm], y_s.at[i], y_r.at[i], sibling).wait_recv()
    rows_image = xr[...].reshape(1024, 128)
    gx[x] = dot(rows_image.T, rows_image, 1, 0, HI)
    row_exchange(gx, h_s, h_r)

    for half in (0, 1):
        for t in range(4):
            second_last(half, t)
    sib_sends = []
    lhs = stack(late_blocks)
    for n in range(4):
        acc[n] = acc[n] + multiply(late_blocks, lhs, n)
        cp = rdma(
            acc.at[n, pl.ds(pl.multiple_of((1 - k) * 128, 128), 128)], sibc.at[n], c_s.at[n], c_r.at[n], sibling
        )
        cp.start()
        sib_sends.append(cp)
        pending.append(cp)
    scaling = 1.0 / 4096
    mine = pl.ds(pl.multiple_of(k * 128, 128), 128)
    for n in range(4):
        sib_sends[n].wait_recv()
        total = (acc[n, mine] + sibc[n]) * scaling
        piece[:, 256 * n : 256 * n + 256] = total
        cov_ref[b, :, 256 * n : 256 * n + 256] = total.astype(BF16)

    img2[x] = dot(piece[...], xr[...].reshape(1024, 128), 1, 0, HI)
    row_exchange(img2, j_s, j_r)

    def csend(event, blk_b, lo, rows, device):
        blk = cov_ref.at[blk_b, pl.ds(lo, rows)]
        cp = rdma(blk, blk, v_s.at[event], v_r.at[event], device)
        cp.start()
        pending.append(cp)

    def cwait(event, blk_b, lo, rows):
        blk = cov_ref.at[blk_b, pl.ds(lo, rows)]
        rdma(blk, blk, v_s.at[event], v_r.at[event], sibling).wait_recv()

    yup, ydn = at(x, mod4(y + 1), z, k), at(x, mod4(y - 1), z, k)
    zfar = at(x, y, mod4(z + 2), k)
    yu, yd, yo = mod4(y + 1), mod4(y - 1), mod4(y + 2)
    far = 4 * (1 - zh)
    near = 4 * zh
    for event, lo, device in ((0, 0, yup), (1, 0, ydn), (8, 64, zfar), (2, 0, zfar), (9, 64, yup), (10, 64, ydn)):
        csend(event, b, lo, 64, device)

    gram = row_collect(gx, h_s, h_r)
    inverse = inverse_factor([gram[8 * i : 8 * i + 8, :] for i in range(16)])
    second = dot(row_collect(img2, j_s, j_r), inverse, 1, 1, HI)

    gpart2[...] = dot(second.T, second, 1, 0, HI)
    gsib_send = rdma(
        gpart2.at[pl.ds(pl.multiple_of(32 * x + 16 * (1 - k), 16), 16)], gsib, gs_s.at[0], gs_r.at[0], sibling
    )
    gsib_send.start()
    pending.append(gsib_send)

    gsib_send.wait_recv()
    gown[...] = gpart2[pl.ds(pl.multiple_of(32 * x + 16 * k, 16), 16), :] + gsib[...]
    gscat[here] = gown[...]

    def gram2_send(i):
        return rdma(gown, gscat.at[here], ga_s.at[i], ga_r.at[i], plane_peer(i))

    start_all(gram2_send, 16)

    image2[...] = second
    holder = c == x
    half_bin = b // 2
    odd = b - 2 * half_bin

    def out_send(i):
        return rdma(
            image2, last.at[odd], o_s.at[i], o_r.at[odd],
            {"bin": bin_peer(i), "row": x, "col": half_bin},
        )

    @pl.when(holder)
    def _():
        for i in range(1, 8):
            out_send(i).start()

        @pl.when(half_bin == c)
        def _():
            last[odd] = second

        @pl.when(half_bin != c)
        def _():
            out_send(0).start()

    def finish_out():
        @pl.when(holder)
        def _():
            for i in range(1, 8):
                out_send(i).wait_send()

            @pl.when(half_bin != c)
            def _():
                out_send(0).wait_send()

    late.append(finish_out)

    cwait(0, near + yd, 0, 64)
    csend(3, near + yd, 0, 32, yup)
    csend(5, near + yd, 0, 64, zfar)
    cwait(1, near + yu, 0, 64)
    csend(4, near + yu, 32, 32, ydn)
    csend(6, near + yu, 0, 64, zfar)
    cwait(8, far + y, 64, 64)
    csend(11, far + y, 64, 64, yup)
    csend(12, far + y, 64, 64, ydn)
    cwait(9, near + yd, 64, 64)
    csend(13, near + yd, 64, 32, yup)
    cwait(10, near + yu, 64, 64)
    csend(14, near + yu, 96, 32, ydn)

    for i in range(1, 16):
        frm = plane_from(i)
        rdma(gown, gscat.at[frm], ga_s.at[i], ga_r.at[i], sibling).wait_recv()
    gram2[pl.ds(pl.multiple_of(32 * x + 16 * k, 16), 16), :] = add_slots(gscat, 16)
    start_all(gram_share, 8)

    cwait(3, near + yo, 0, 32)
    cwait(4, near + yo, 32, 32)
    csend(7, near + yo, 0, 64, zfar)
    cwait(11, far + yd, 64, 64)
    csend(15, far + yd, 64, 32, yup)
    cwait(12, far + yu, 64, 64)
    csend(16, far + yu, 96, 32, ydn)

    share_wait()
    inverse = inverse_factor([gram2[8 * i : 8 * i + 8, :] for i in range(16)])

    for h in (0, 1):
        @pl.when(jnp.logical_not((c == x) & (b == 2 * c + h)))
        def _():
            rdma(image2, last.at[h], o_s.at[0], o_r.at[h], sibling).wait_recv()

    basis_ref[...] = dot(last[...].reshape(256, 128), inverse, 1, 1, HI) * 64.0

    cwait(2, far + y, 0, 64)
    cwait(5, far + yd, 0, 64)
    cwait(6, far + yu, 0, 64)
    cwait(7, far + yo, 0, 64)
    cwait(13, near + yo, 64, 32)
    cwait(14, near + yo, 96, 32)
    cwait(15, far + yo, 64, 32)
    cwait(16, far + yo, 96, 32)

    for cp in pending:
        cp.wait_send()
    for finish in late:
        finish()


def shards(snapshots, focus_in, focus_out, start_basis):
    snaps = snapshots.transpose(1, 2, 0).reshape(128, 1024)
    dma = pltpu.SemaphoreType.DMA
    anywhere = pl.BlockSpec(memory_space=pl.ANY)
    in_vmem = pl.BlockSpec(memory_space=pltpu.VMEM)
    pieces, basis_out = pl.pallas_call(
        kernel,
        out_shape=(
            jax.ShapeDtypeStruct((8, 128, 1024), BF16),
            jax.ShapeDtypeStruct((256, 128), F32),
        ),
        in_specs=[pl.BlockSpec(memory_space=pltpu.HBM)] * 4,
        out_specs=(in_vmem, in_vmem),
        scratch_shapes=[
            pltpu.VMEM((128, 1024), BF16),
            pltpu.VMEM((8, 1024, 128), BF16),
            pltpu.VMEM((8, 1024, 128), BF16),
            pltpu.VMEM((1024, 128), F32),
            pltpu.VMEM((4, 128, 128), F32),
            pltpu.VMEM((16, 128, 1024), BF16),
            pltpu.VMEM((2, 16, 128, 128), BF16),
            pltpu.VMEM((4, 256, 256), F32),
            pltpu.VMEM((4, 128, 256), F32),
            pltpu.VMEM((128, 1024), F32),
            pltpu.VMEM((4, 128, 128), F32),
            pltpu.VMEM((2, 2, 256, 128), F32),
            pltpu.VMEM((2, 256, 128), F32),
            pltpu.VMEM((16, 32, 128), F32),
            pltpu.VMEM((256, 128), F32),
            pltpu.VMEM((4, 256, 128), F32),
            pltpu.VMEM((4, 128, 128), F32),
            pltpu.VMEM((128, 128), F32),
            pltpu.VMEM((2, 128, 128), F32),
            pltpu.VMEM((4, 128, 128), F32),
            pltpu.VMEM((16, 128), F32),
            pltpu.VMEM((16, 128), F32),
            pltpu.VMEM((16, 16, 128), F32),
            pltpu.VMEM((128, 128), F32),
            pltpu.VMEM((128, 128), F32),
            dma((4,)),
            dma((4,)), dma((4,)),
            dma((40,)), dma((40,)),
            dma((8,)), dma((16,)),
            dma((2, 4, 2)), dma((2, 4)),
            dma((4,)), dma((4,)),
            dma((17,)), dma((17,)),
            dma((4,)), dma((4,)),
            dma((2,)), dma((2,)),
            dma((16,)), dma((16,)),
            dma((8,)), dma((8,)),
            dma((4,)), dma((4,)),
            dma((4,)), dma((4,)),
            dma((8,)), dma((2,)),
            dma((1,)), dma((1,)),
            dma((16,)), dma((16,)),
            dma((8,)), dma((8,)),
            dma((4,)), dma((4,)),
            dma((1,)),
        ],
        compiler_params=pltpu.CompilerParams(
            collective_id=0, has_side_effects=True, vmem_limit_bytes=60 * 2**20
        ),
    )(snaps, focus_in, focus_out, start_basis)
    return pieces.reshape(1024, 1024).astype(F32), basis_out


def solution(mesh):
    in_specs = (P("row", "bin", "col"), P("bin", "row", None), P("bin", "row", None), P())
    out_specs = (P("col", "row"), P(("row", "col"), None))
    return jax.shard_map(shards, mesh=mesh, in_specs=in_specs, out_specs=out_specs, check_vma=False)
```

```python
import functools
import math

import jax
import jax.numpy as jnp
from jax import lax
from jax.experimental import pallas as pl
from jax.experimental.pallas import tpu as pltpu
from jax.sharding import PartitionSpec as P

MESH = pl.DeviceIdType.MESH
HI = lax.Precision.HIGHEST
F32 = jnp.float32
BF16 = jnp.bfloat16


def mod4(v):
    return lax.rem(v + 4, 4)


def dot(a, b, ca, cb, precision=None):
    return lax.dot_general(a, b, (((ca,), (cb,)), ((), ())), precision=precision, preferred_element_type=F32)


def dot_split(a, b, ca, cb):
    high = b.astype(BF16)
    low = (b - high.astype(F32)).astype(BF16)
    return dot(a, high, ca, cb) + dot(a, low, ca, cb)


def inverse_factor(gram):
    lane = lax.broadcasted_iota(jnp.int32, (8, 128), 1)
    sub = lax.broadcasted_iota(jnp.int32, (8, 128), 0)

    def over_lanes(tile, j):
        return jnp.broadcast_to(tile[:, j : j + 1], (8, 128))

    def over_rows(tile, i):
        return jnp.broadcast_to(tile[i : i + 1, :], (8, 128))

    tiles = list(gram)
    done = []
    for p in range(16):
        first = 8 * p
        now = tiles[p]
        cols = [over_lanes(now, first + e) for e in range(8)]
        left = [[over_rows(cols[e], i) for e in range(i + 1)] for i in range(8)]
        low = [[None] * 8 for _ in range(8)]
        inv = [None] * 8
        for e in range(8):
            inv[e] = 1.0 / left[e][e]
            for i in range(e + 1, 8):
                low[i][e] = left[i][e] * inv[e]
            for i in range(e + 1, 8):
                for f in range(e + 1, i + 1):
                    left[i][f] = left[i][f] - low[i][e] * left[f][e]
        in_panel = (lane >= first) & (lane < first + 8)
        upper = []
        for i in range(8):
            row = jnp.where(in_panel, jnp.where(lane == first + i, 1.0, 0.0), over_rows(now, i))
            for e in range(i):
                row = row - low[i][e] * upper[e]
            upper.append(row)
        tile, scale = upper[0], inv[0]
        for i in range(1, 8):
            tile = jnp.where(sub == i, upper[i], tile)
            scale = jnp.where(sub == i, inv[i], scale)
        done.append(jnp.where(lane <= sub + first, tile, 0.0) * jnp.sqrt(scale))
        scaled = [upper[e] * inv[e] for e in range(8)]
        for q in range(p + 1, 16):
            total = jnp.where(in_panel, 0.0, tiles[q])
            lower = []
            for e in range(8):
                col = over_lanes(tiles[q], first + e)
                for f in range(e):
                    col = col - lower[f] * low[e][f]
                lower.append(col)
                total = total - col * scaled[e]
            tiles[q] = total
    return jnp.concatenate(done, axis=0)


def apply_factor(gram, block):
    return dot(block, inverse_factor([gram[8 * i : 8 * i + 8, :] for i in range(16)]), 1, 1, HI)


def kernel(
    snap_hbm, fi_hbm, fo_hbm, x0_hbm, cov_ref, basis_ref,
    snap, fi, fo, x0, proj, full, slab, acc, sibc, piece, img, part, sibp, scat, zall, xr, img2, image2, last,
    gx, gsib, gown, gscat, gpart2, gram2, in_sem,
    p_s, p_r, g_s, g_r, a_s, a_r, x_s, x_r, c_s, c_r, v_s, v_r, i_s, i_r, q_s, q_r, r_s, r_r, z_s, z_r,
    y_s, y_r, j_s, j_r, o_s, o_r, gs_s, gs_r, ga_s, ga_r, gb_s, gb_r, h_s, h_r, l_sem,
):
    b = lax.axis_index("bin")
    x = lax.axis_index("row")
    c = lax.axis_index("col")
    k = lax.rem(c, 2)
    zl = c // 2
    y = lax.rem(b, 4)
    zh = b // 4
    z = zh * 2 + zl

    def at(x_, y_, z_, k_):
        return {"bin": (z_ // 2) * 4 + y_, "row": x_, "col": lax.rem(z_, 2) * 2 + k_}

    xs, ys, zs = ([v] + [mod4(v + i) for i in (1, 2, 3)] for v in (x, y, z))
    zhs = [zh] + [v // 2 for v in zs[1:]]
    zls = [zl] + [v - 2 * h for v, h in zip(zs[1:], zhs[1:])]
    zh2, zl2, ks = (zh, 1 - zh), (zl, 1 - zl), (k, 1 - k)

    def plane_peer(i, dk=0):
        return {"bin": zhs[i // 4] * 4 + ys[i % 4], "row": x, "col": zls[i // 4] * 2 + ks[dk]}

    def plane_from(i):
        return zs[-(i // 4)] * 4 + ys[-(i % 4)]

    def mesh_peer(i):
        return {"bin": b, "row": xs[i // 4], "col": zl2[i // 2 % 2] * 2 + ks[i % 2]}

    def mesh_from(i):
        return xs[-(i // 4)] * 4 + zl2[i // 2 % 2] * 2 + ks[i % 2]

    def bin_peer(i):
        return zh2[i // 4] * 4 + ys[i % 4]

    def bin_from(i):
        return zh2[i // 4] * 4 + ys[-(i % 4)]

    sibling = {"bin": b, "row": x, "col": zl * 2 + (1 - k)}
    pending, late = [], []

    def rdma(src, dst, s, r, device):
        return pltpu.make_async_remote_copy(
            src_ref=src, dst_ref=dst, send_sem=s, recv_sem=r, device_id=device, device_id_type=MESH
        )

    loads = [
        pltpu.make_async_copy(snap_hbm, snap, in_sem.at[0]),
        pltpu.make_async_copy(fi_hbm, fi, in_sem.at[1]),
        pltpu.make_async_copy(fo_hbm, fo, in_sem.at[2]),
        pltpu.make_async_copy(x0_hbm.at[pl.ds(pl.multiple_of(x * 1024, 1024), 1024)], x0, in_sem.at[3]),
    ]
    for load in loads:
        load.start()

    barrier = pltpu.get_barrier_semaphore()
    for i in range(1, 32):
        pl.semaphore_signal(barrier, inc=1, device_id=plane_peer(i // 2, i % 2), device_id_type=MESH)
    for i in range(4, 16):
        pl.semaphore_signal(barrier, inc=1, device_id=mesh_peer(i), device_id_type=MESH)

    loads[0].wait()
    loads[1].wait()
    for bb in range(8):
        proj[x, 16 * bb : 16 * bb + 16, :] = dot(snap[16 * bb : 16 * bb + 16, :], fi[bb], 1, 0)
    pl.semaphore_wait(barrier, 43)

    def row_exchange(buf, s, r):
        for i in (2, 1, 3):
            cp = rdma(buf.at[x], buf.at[x], s.at[i], r.at[i], {"bin": b, "row": xs[i], "col": c})
            cp.start()
            pending.append(cp)

    def row_collect(buf, s, r):
        for i in (1, 3, 2):
            frm = xs[-i]
            rdma(buf.at[frm], buf.at[frm], s.at[i], r.at[i], sibling).wait_recv()
        return (buf[0] + buf[1]) + (buf[2] + buf[3])

    row_exchange(proj, p_s, p_r)
    def start_all(send, n):
        for i in range(1, n):
            cp = send(i)
            cp.start()
            pending.append(cp)

    loads[2].wait()
    projected = row_collect(proj, p_s, p_r).astype(BF16)
    here = z * 4 + y
    for bb in range(8):
        lifted = dot(projected[16 * bb : 16 * bb + 16, :], fo[bb], 1, 1)
        full[here, 16 * bb : 16 * bb + 16, :] = (
            snap[16 * bb : 16 * bb + 16, :].astype(F32) + lifted
        ).astype(BF16)

    is_source = zl == x // 2
    own_ci = lax.rem(x, 2)

    def slab_send(i):
        to = bin_peer(i)
        return rdma(
            full.at[here, :, pl.ds(pl.multiple_of(to * 128, 128), 128)], slab.at[own_ci, here], a_s.at[i],
            a_r.at[here], {"bin": to, "row": x, "col": (x // 2) * 2 + k},
        )

    start_all(slab_send, 8)
    slab_local = pltpu.make_async_copy(
        full.at[here, :, pl.ds(pl.multiple_of(b * 128, 128), 128)], slab.at[own_ci, here], l_sem.at[0]
    )

    @pl.when(is_source)
    def _():
        slab_local.start()

    @pl.when(jnp.logical_not(is_source))
    def _():
        slab_send(0).start()

    def finish_slab():
        @pl.when(jnp.logical_not(is_source))
        def _():
            slab_send(0).wait_send()

    late.append(finish_slab)

    def block_of(half, u, v):
        return (v * 4 + u) if half == 0 else (u * 4 + v)

    def dev_of(half, u, v):
        return at(x, u, v, k) if half == 0 else at(x, v, u, k)

    def ring(half):
        return (y, z) if half == 0 else (z, y)

    def gcopy(half, event, u, v, lo, rows, tu, tv):
        blk = full.at[block_of(half, u, v), pl.ds(64 * half + lo, rows)]
        e = 20 * half + event
        return rdma(blk, blk, g_s.at[e], g_r.at[e], dev_of(half, tu, tv))

    def gsend(*args):
        cp = gcopy(*args)
        cp.start()
        pending.append(cp)

    def gwait(half, event, u, v, lo, rows):
        gcopy(half, event, u, v, lo, rows, mod4(ring(half)[0] + 1), v).wait_recv()

    def second_send(half, t):
        u, v = ring(half)
        w = mod4(u + (0, -1, 1, 2)[t])
        gsend(half, 4 + 4 * t, w, v, 0, 64, u, mod4(v + 1))
        gsend(half, 5 + 4 * t, w, v, 0, 64, u, mod4(v - 1))

    def second_forward(half, t):
        u, v = ring(half)
        w = mod4(u + (0, -1, 1, 2)[t])
        gwait(half, 4 + 4 * t, w, mod4(v - 1), 0, 64)
        gsend(half, 6 + 4 * t, w, mod4(v - 1), 0, 32, u, mod4(v + 1))
        gwait(half, 5 + 4 * t, w, mod4(v + 1), 0, 64)
        gsend(half, 7 + 4 * t, w, mod4(v + 1), 32, 32, u, mod4(v - 1))

    def second_last(half, t):
        u, v = ring(half)
        w = mod4(u + (0, -1, 1, 2)[t])
        gwait(half, 6 + 4 * t, w, mod4(v + 2), 0, 32)
        gwait(half, 7 + 4 * t, w, mod4(v + 2), 32, 32)

    for half in (0, 1):
        u, v = ring(half)
        gsend(half, 0, u, v, 0, 64, mod4(u + 1), v)
        gsend(half, 1, u, v, 0, 64, mod4(u - 1), v)
    for half in (0, 1):
        second_send(half, 0)

    loads[3].wait()
    img[x] = dot_split(full[here], x0[...], 1, 0)
    row_exchange(img, i_s, i_r)

    def spread(ci, g, n, device):
        blk = slab.at[ci, pl.ds(4 * g, 4)]
        return rdma(blk, blk, x_s.at[ci, g, n], x_r.at[ci, g], device)

    right, left = at(mod4(x + 1), y, z, k), at(mod4(x - 1), y, z, k)

    @pl.when(is_source)
    def _():
        slab_local.wait()

        for dz in range(4):
            for i in range(4 * dz, 4 * dz + 4):
                if i:
                    frm = plane_from(i)
                    rdma(slab.at[own_ci, frm], slab.at[own_ci, frm], a_s.at[0], a_r.at[frm], sibling).wait_recv()
            spread(own_ci, zs[-dz], 0, right).start()
            spread(own_ci, zs[-dz], 1, left).start()


    for half in (0, 1):
        u, v = ring(half)
        gwait(half, 0, mod4(u - 1), v, 0, 64)
        gsend(half, 2, mod4(u - 1), v, 0, 32, mod4(u + 1), v)
        gwait(half, 1, mod4(u + 1), v, 0, 64)
        gsend(half, 3, mod4(u + 1), v, 32, 32, mod4(u - 1), v)
        second_send(half, 1)
        second_send(half, 2)

    weights = row_collect(img, i_s, i_r)
    part[...] = (dot_split(full[here].T, weights, 1, 0) * (1.0 / 4096)).reshape(2, 2, 256, 128)
    sibp_sends = []
    for h in (0, 1):
        cp = rdma(part.at[h, 1 - k], sibp.at[h], q_s.at[h], q_r.at[h], sibling)
        cp.start()
        sibp_sends.append(cp)
        pending.append(cp)

    def spread_roles(forward):
        for ci in (0, 1):
            d = mod4(x - (2 * zl + ci))
            passes_on = d == (3 if ci == 0 else 1)
            yield ci, (passes_on if forward else (d != 0) & jnp.logical_not(passes_on))

    def spread_step(g):
        for ci, passes_on in spread_roles(True):

            @pl.when(passes_on)
            def _():
                spread(ci, zs[-g], 0, right).wait_recv()
                spread(ci, zs[-g], 0, left if ci == 0 else right).start()

    def spread_last():
        for ci, receives in spread_roles(False):

            @pl.when(receives)
            def _():
                for g in range(4):
                    spread(ci, g, 0, right).wait_recv()

    def finish_spread():
        @pl.when(is_source)
        def _():
            for g in range(4):
                spread(own_ci, g, 0, right).wait_send()
                spread(own_ci, g, 1, left).wait_send()

        for ci, passes_on in spread_roles(True):

            @pl.when(passes_on)
            def _():
                for g in range(4):
                    spread(ci, g, 0, left if ci == 0 else right).wait_send()

    late.append(finish_spread)

    for half in (0, 1):
        second_forward(half, 0)

    def add_slots(ref, n):
        total = ref[0]
        for i in range(1, n):
            total = total + ref[i]
        return total

    for h in (0, 1):
        sibp_sends[h].wait_recv()
        sibp[h] = sibp[h] + part[h, k]

    def scat_send(i):
        ob = zhs[i // 4] * 4 + ys[i % 4]
        return rdma(
            sibp.at[zls[i // 4], pl.ds(pl.multiple_of(32 * ob, 32), 32)], scat.at[here], r_s.at[i], r_r.at[i],
            plane_peer(i),
        )

    start_all(scat_send, 16)
    scat[here] = sibp[zl, pl.ds(pl.multiple_of(32 * b, 32), 32)]

    for half in (0, 1):
        u, v = ring(half)
        gwait(half, 2, mod4(u + 2), v, 0, 32)
        gwait(half, 3, mod4(u + 2), v, 32, 32)
        second_send(half, 3)
    spread_step(0)
    for half in (0, 1):
        second_forward(half, 1)
    spread_step(1)

    for i in range(1, 16):
        frm = plane_from(i)
        rdma(scat.at[frm], scat.at[frm], r_s.at[i], r_r.at[i], sibling).wait_recv()
    zall[pl.ds(pl.multiple_of(32 * b, 32), 32), :] = add_slots(scat, 16)

    def bin_share(i):
        blk = zall.at[pl.ds(pl.multiple_of(32 * b, 32), 32)]
        return rdma(blk, blk, z_s.at[i], z_r.at[i], {"bin": bin_peer(i), "row": x, "col": c})

    start_all(bin_share, 8)

    for half in (0, 1):
        second_forward(half, 2)
    spread_step(2)
    spread_step(3)

    for half in (0, 1):
        second_forward(half, 3)

    for i in range(1, 8):
        frm = bin_from(i)
        blk = zall.at[pl.ds(pl.multiple_of(32 * frm, 32), 32)]
        rdma(blk, blk, z_s.at[i], z_r.at[i], sibling).wait_recv()

    def col_share(i):
        return rdma(zall, xr.at[c], y_s.at[i], y_r.at[i], {"bin": b, "row": x, "col": mod4(c + i)})

    for i in (2, 1, 3):
        col_share(i).start()
        pending.append(col_share(i))
    xr[c] = zall[...]

    def gram_share(i):
        blk = gram2.at[pl.ds(pl.multiple_of(16 * (x * 2 + k), 16), 16)]
        return rdma(blk, blk, gb_s.at[i], gb_r.at[i], {"bin": b, "row": xs[i // 2], "col": zl * 2 + ks[i % 2]})

    def share_wait():
        for i in range(1, 8):
            frm = xs[-(i // 2)] * 2 + ks[i % 2]
            blk = gram2.at[pl.ds(pl.multiple_of(16 * frm, 16), 16)]
            rdma(blk, blk, gb_s.at[i], gb_r.at[i], sibling).wait_recv()

    spread_last()

    def stack(places):
        lhs = [
            jnp.concatenate([slab[ci, j, 64 * half : 64 * half + 64, :] for half, j in places], axis=0).T
            for ci in (0, 1)
        ]
        return jnp.concatenate(lhs, axis=0)

    def multiply(places, lhs, n):
        rhs = jnp.concatenate(
            [full[j, 64 * half : 64 * half + 64, 256 * n : 256 * n + 256] for half, j in places], axis=0
        )
        return dot(lhs, rhs, 1, 0)

    early, late_blocks = [], []
    for half in (0, 1):
        u, v = ring(half)
        for i in (0, 1, 3, 2):
            for w in range(4):
                (late_blocks if i == 2 else early).append((half, block_of(half, w, mod4(v + i))))
    lhs = stack(early)
    for n in range(4):
        acc[n] = multiply(early, lhs, n)

    for i in (1, 2, 3):
        frm = mod4(c - i)
        rdma(zall, xr.at[frm], y_s.at[i], y_r.at[i], sibling).wait_recv()
    rows_image = xr[...].reshape(1024, 128)
    gx[x] = dot(rows_image.T, rows_image, 1, 0, HI)
    row_exchange(gx, h_s, h_r)

    for half in (0, 1):
        for t in range(4):
            second_last(half, t)
    sib_sends = []
    lhs = stack(late_blocks)
    for n in range(4):
        acc[n] = acc[n] + multiply(late_blocks, lhs, n)
        cp = rdma(
            acc.at[n, pl.ds(pl.multiple_of((1 - k) * 128, 128), 128)], sibc.at[n], c_s.at[n], c_r.at[n], sibling
        )
        cp.start()
        sib_sends.append(cp)
        pending.append(cp)
    scaling = 1.0 / 4096
    mine = pl.ds(pl.multiple_of(k * 128, 128), 128)
    for n in range(4):
        sib_sends[n].wait_recv()
        total = (acc[n, mine] + sibc[n]) * scaling
        piece[:, 256 * n : 256 * n + 256] = total
        cov_ref[b, :, 256 * n : 256 * n + 256] = total.astype(BF16)

    img2[x] = dot(piece[...], xr[...].reshape(1024, 128), 1, 0, HI)
    row_exchange(img2, j_s, j_r)

    def csend(event, blk_b, lo, rows, device):
        blk = cov_ref.at[blk_b, pl.ds(lo, rows)]
        cp = rdma(blk, blk, v_s.at[event], v_r.at[event], device)
        cp.start()
        pending.append(cp)

    def cwait(event, blk_b, lo, rows):
        blk = cov_ref.at[blk_b, pl.ds(lo, rows)]
        rdma(blk, blk, v_s.at[event], v_r.at[event], sibling).wait_recv()

    yup, ydn = at(x, mod4(y + 1), z, k), at(x, mod4(y - 1), z, k)
    zfar = at(x, y, mod4(z + 2), k)
    yu, yd, yo = mod4(y + 1), mod4(y - 1), mod4(y + 2)
    far = 4 * (1 - zh)
    near = 4 * zh
    for event, lo, device in ((0, 0, yup), (1, 0, ydn), (8, 64, zfar), (2, 0, zfar), (9, 64, yup), (10, 64, ydn)):
        csend(event, b, lo, 64, device)

    gram = row_collect(gx, h_s, h_r)
    inverse = inverse_factor([gram[8 * i : 8 * i + 8, :] for i in range(16)])
    second = dot(row_collect(img2, j_s, j_r), inverse, 1, 1, HI)

    cwait(0, near + yd, 0, 64)
    csend(3, near + yd, 0, 32, yup)
    csend(5, near + yd, 0, 64, zfar)
    cwait(1, near + yu, 0, 64)
    csend(4, near + yu, 32, 32, ydn)
    csend(6, near + yu, 0, 64, zfar)
    cwait(8, far + y, 64, 64)
    csend(11, far + y, 64, 64, yup)
    csend(12, far + y, 64, 64, ydn)
    cwait(9, near + yd, 64, 64)
    csend(13, near + yd, 64, 32, yup)
    cwait(10, near + yu, 64, 64)
    csend(14, near + yu, 96, 32, ydn)

    gpart2[...] = dot(second.T, second, 1, 0, HI)
    gsib_send = rdma(
        gpart2.at[pl.ds(pl.multiple_of(32 * x + 16 * (1 - k), 16), 16)], gsib, gs_s.at[0], gs_r.at[0], sibling
    )
    gsib_send.start()
    pending.append(gsib_send)

    gsib_send.wait_recv()
    gown[...] = gpart2[pl.ds(pl.multiple_of(32 * x + 16 * k, 16), 16), :] + gsib[...]
    gscat[here] = gown[...]

    def gram2_send(i):
        return rdma(gown, gscat.at[here], ga_s.at[i], ga_r.at[i], plane_peer(i))

    start_all(gram2_send, 16)

    image2[...] = second
    holder = c == x
    half_bin = b // 2
    odd = b - 2 * half_bin

    def out_send(i):
        return rdma(
            image2, last.at[odd], o_s.at[i], o_r.at[odd],
            {"bin": bin_peer(i), "row": x, "col": half_bin},
        )

    @pl.when(holder)
    def _():
        for i in range(1, 8):
            out_send(i).start()

        @pl.when(half_bin == c)
        def _():
            last[odd] = second

        @pl.when(half_bin != c)
        def _():
            out_send(0).start()

    def finish_out():
        @pl.when(holder)
        def _():
            for i in range(1, 8):
                out_send(i).wait_send()

            @pl.when(half_bin != c)
            def _():
                out_send(0).wait_send()

    late.append(finish_out)

    for i in range(1, 16):
        frm = plane_from(i)
        rdma(gown, gscat.at[frm], ga_s.at[i], ga_r.at[i], sibling).wait_recv()
    gram2[pl.ds(pl.multiple_of(32 * x + 16 * k, 16), 16), :] = add_slots(gscat, 16)
    start_all(gram_share, 8)

    cwait(3, near + yo, 0, 32)
    cwait(4, near + yo, 32, 32)
    csend(7, near + yo, 0, 64, zfar)
    cwait(11, far + yd, 64, 64)
    csend(15, far + yd, 64, 32, yup)
    cwait(12, far + yu, 64, 64)
    csend(16, far + yu, 96, 32, ydn)

    share_wait()
    inverse = inverse_factor([gram2[8 * i : 8 * i + 8, :] for i in range(16)])

    for h in (0, 1):
        @pl.when(jnp.logical_not((c == x) & (b == 2 * c + h)))
        def _():
            rdma(image2, last.at[h], o_s.at[0], o_r.at[h], sibling).wait_recv()

    basis_ref[...] = dot(last[...].reshape(256, 128), inverse, 1, 1, HI) * 64.0

    cwait(2, far + y, 0, 64)
    cwait(5, far + yd, 0, 64)
    cwait(6, far + yu, 0, 64)
    cwait(7, far + yo, 0, 64)
    cwait(13, near + yo, 64, 32)
    cwait(14, near + yo, 96, 32)
    cwait(15, far + yo, 64, 32)
    cwait(16, far + yo, 96, 32)

    for cp in pending:
        cp.wait_send()
    for finish in late:
        finish()


def shards(snapshots, focus_in, focus_out, start_basis):
    snaps = snapshots.transpose(1, 2, 0).reshape(128, 1024)
    dma = pltpu.SemaphoreType.DMA
    anywhere = pl.BlockSpec(memory_space=pl.ANY)
    in_vmem = pl.BlockSpec(memory_space=pltpu.VMEM)
    pieces, basis_out = pl.pallas_call(
        kernel,
        out_shape=(
            jax.ShapeDtypeStruct((8, 128, 1024), BF16),
            jax.ShapeDtypeStruct((256, 128), F32),
        ),
        in_specs=[pl.BlockSpec(memory_space=pltpu.HBM)] * 4,
        out_specs=(in_vmem, in_vmem),
        scratch_shapes=[
            pltpu.VMEM((128, 1024), BF16),
            pltpu.VMEM((8, 1024, 128), BF16),
            pltpu.VMEM((8, 1024, 128), BF16),
            pltpu.VMEM((1024, 128), F32),
            pltpu.VMEM((4, 128, 128), F32),
            pltpu.VMEM((16, 128, 1024), BF16),
            pltpu.VMEM((2, 16, 128, 128), BF16),
            pltpu.VMEM((4, 256, 256), F32),
            pltpu.VMEM((4, 128, 256), F32),
            pltpu.VMEM((128, 1024), F32),
            pltpu.VMEM((4, 128, 128), F32),
            pltpu.VMEM((2, 2, 256, 128), F32),
            pltpu.VMEM((2, 256, 128), F32),
            pltpu.VMEM((16, 32, 128), F32),
            pltpu.VMEM((256, 128), F32),
            pltpu.VMEM((4, 256, 128), F32),
            pltpu.VMEM((4, 128, 128), F32),
            pltpu.VMEM((128, 128), F32),
            pltpu.VMEM((2, 128, 128), F32),
            pltpu.VMEM((4, 128, 128), F32),
            pltpu.VMEM((16, 128), F32),
            pltpu.VMEM((16, 128), F32),
            pltpu.VMEM((16, 16, 128), F32),
            pltpu.VMEM((128, 128), F32),
            pltpu.VMEM((128, 128), F32),
            dma((4,)),
            dma((4,)), dma((4,)),
            dma((40,)), dma((40,)),
            dma((8,)), dma((16,)),
            dma((2, 4, 2)), dma((2, 4)),
            dma((4,)), dma((4,)),
            dma((17,)), dma((17,)),
            dma((4,)), dma((4,)),
            dma((2,)), dma((2,)),
            dma((16,)), dma((16,)),
            dma((8,)), dma((8,)),
            dma((4,)), dma((4,)),
            dma((4,)), dma((4,)),
            dma((8,)), dma((2,)),
            dma((1,)), dma((1,)),
            dma((16,)), dma((16,)),
            dma((8,)), dma((8,)),
            dma((4,)), dma((4,)),
            dma((1,)),
        ],
        compiler_params=pltpu.CompilerParams(
            collective_id=0, has_side_effects=True, vmem_limit_bytes=60 * 2**20
        ),
    )(snaps, focus_in, focus_out, start_basis)
    return pieces.reshape(1024, 1024).astype(F32), basis_out


def solution(mesh):
    in_specs = (P("row", "bin", "col"), P("bin", "row", None), P("bin", "row", None), P())
    out_specs = (P("col", "row"), P(("row", "col"), None))
    return jax.shard_map(shards, mesh=mesh, in_specs=in_specs, out_specs=out_specs, check_vma=False)
```
